32 devices in a mesh: seq: 2 (over x), shard: 4 (over y, core), rep: 4 (over z).
Axes of the slice: x: 2, y: 2, z: 4, core: 2. Of those that a mesh axis runs over, the one named last changes fastest.
Arguments:
- tokens: bfloat16 [16, 512, 2048], P(('shard', 'rep'), 'seq'), may hold values from -6 to 6
- lengths: int32 [16], P(('shard', 'rep')), may hold values from 128 to 512, as said below
- w_query: bfloat16 [2048, 2048], P(('shard', 'rep')), may hold values from -0.125 to 0.125
- w_forget: bfloat16 [2048, 2048], P(('shard', 'rep')), may hold values from -0.125 to 0.125
- w_input: bfloat16 [2048, 2048], P(('shard', 'rep')), may hold values from -0.125 to 0.125
- w_gate_out: bfloat16 [2048, 2048], P(('shard', 'rep')), may hold values from -0.125 to 0.125
- w_output: bfloat16 [2048, 2048], P(('shard', 'rep')), may hold values from -0.125 to 0.125
- w_ffn_gate: bfloat16 [2048, 5632], P(('shard', 'rep')), may hold values from -0.125 to 0.125
- w_ffn_up: bfloat16 [2048, 5632], P(('shard', 'rep')), may hold values from -0.125 to 0.125
- w_ffn_down: bfloat16 [5632, 2048], P(('shard', 'rep')), may hold values from -0.078125 to 0.078125
- norm_in: bfloat16 [2048], P(('shard', 'rep')), may hold values from 0.5 to 1.5
- norm_mid: bfloat16 [2048], P(('shard', 'rep')), may hold values from 0.5 to 1.5
- head_gain: bfloat16 [128], P(('shard', 'rep')), may hold values from 0.5 to 1.5
- gate_gap: bfloat16 [2048], P(('shard', 'rep')), may hold values from 1e-05 to 0.08, as said below
- cotangent: bfloat16 [16, 512, 2048], P(('shard', 'rep'), 'seq'), may hold values from -6 to 6
Outputs:
- layer_out: bfloat16 [16, 512, 2048], P(('shard', 'rep'), 'seq')
- input_grad: bfloat16 [16, 512, 2048], P(('shard', 'rep'), 'seq')
- grad_query: float32 [2048, 2048], P(('shard', 'rep'))
- grad_forget: float32 [2048, 2048], P(('shard', 'rep'))
- grad_input: float32 [2048, 2048], P(('shard', 'rep'))
- grad_gate_out: float32 [2048, 2048], P(('shard', 'rep'))
- grad_output: float32 [2048, 2048], P(('shard', 'rep'))
- grad_ffn_gate: float32 [2048, 5632], P(('shard', 'rep'))
- grad_ffn_up: float32 [2048, 5632], P(('shard', 'rep'))
- grad_ffn_down: float32 [5632, 2048], P(('shard', 'rep'))
- grad_norm_in: float32 [2048], P(('shard', 'rep'))
- grad_norm_mid: float32 [2048], P(('shard', 'rep'))
- grad_head_gain: float32 [128], P(('shard', 'rep'))
- grad_gate_gap: float32 [2048], P(('shard', 'rep'))
The draws below stay inside these ranges and needn't reach their ends.
Inputs may be any that keep to these rules, and one draw needn't show every extreme that they name: `lengths`: valid tokens of each sequence, counted from its start; in every draw one sequence has 512 and one 512 // 4. `gate_gap`: positive.
All inputs are finite; a program needn't handle non-finite values.
Results may differ from the reference program's by a relative error of at most 0.023.
Values may be sent and summed in bfloat16 or wider, within the bound.
A program may use at most 512 MiB of HBM per device.

```python
import math
import jax
import jax.numpy as jnp
from jax import lax

D = 2048
H = 16
HD = 128
FF = 5632
BLK = 128
LEN = 512
SEQS = 16


def draw_lengths(key, part):
    key = jax.random.fold_in(key, 11)
    first_key, second_key = jax.random.split(key)
    drawn = jax.random.randint(first_key, (SEQS,), LEN // 4, LEN + 1)
    order = jax.random.permutation(second_key, SEQS)
    drawn = jnp.where(order == 0, LEN, drawn)
    drawn = jnp.where(order == 1, LEN // 4, drawn)
    return drawn.astype(jnp.int32)


def draw_gate_gap(key, part):
    key = jax.random.fold_in(key, 23)
    uniform_draw = jax.random.uniform(key, (D,), jnp.float32)
    low_end = 0.0001
    high_end = 0.08
    spread_log = math.log(high_end) - math.log(low_end)
    return jnp.exp(math.log(low_end) + uniform_draw * spread_log).astype(jnp.bfloat16)


def steps_of(own_key, dims, cuts, least, largest):
    factor_of, own = 1.0, jax.random.fold_in(own_key, 6)
    for position, parts in cuts:
        draws = jnp.exp(jax.random.uniform(jax.random.fold_in(own, position), (parts,), jnp.float32, least / len(cuts), largest / len(cuts)))
        factor_of = factor_of * jnp.repeat(draws, dims[position] // parts).reshape([-1 if axis == position else 1 for axis in range(len(dims))])
    return factor_of


def noise(own_key, extent, spread, most, cuts=(), kind=jnp.bfloat16):
    values = jax.random.normal(own_key, extent, jnp.float32) * spread
    if len(cuts) > 0:
        values = steps_of(own_key, extent, cuts, -0.22, 0.18) * values
    return jnp.clip(values, min=-most, max=most).astype(kind)


def setup_inputs(seed: int = 0) -> dict:
    streams_of = jax.random.split(jax.random.key(seed), 16)
    tokens = noise(streams_of[0], (SEQS, LEN, D), 1.0, 6.0, ((0, 16), (1, 2)))
    lengths = draw_lengths(jax.random.fold_in(streams_of[15], 71), 0)
    w_query = noise(streams_of[2], (D, D), D ** -0.5, 0.125, ((0, 16),))
    w_forget = noise(streams_of[3], (D, D), D ** -0.5, 0.125, ((0, 16),))
    w_input = noise(streams_of[4], (D, D), D ** -0.5, 0.125, ((0, 16),))
    w_gate_out = noise(streams_of[5], (D, D), D ** -0.5, 0.125, ((0, 16),))
    w_output = noise(streams_of[6], (D, D), D ** -0.5, 0.125, ((0, 16),))
    w_ffn_gate = noise(streams_of[7], (D, FF), D ** -0.5, 0.125, ((0, 16),))
    w_ffn_up = noise(streams_of[8], (D, FF), D ** -0.5, 0.125, ((0, 16),))
    w_ffn_down = noise(streams_of[9], (FF, D), FF ** -0.5, 0.078125, ((0, 16),))
    norm_in = jnp.clip(1.0 + 0.1 * jax.random.normal(streams_of[10], (D,), jnp.float32), 0.5, 1.5).astype(jnp.bfloat16)
    norm_mid = jnp.clip(1.0 + 0.1 * jax.random.normal(streams_of[11], (D,), jnp.float32), 0.5, 1.5).astype(jnp.bfloat16)
    head_gain = jnp.clip(1.0 + 0.1 * jax.random.normal(streams_of[12], (HD,), jnp.float32), 0.5, 1.5).astype(jnp.bfloat16)
    gate_gap = draw_gate_gap(jax.random.fold_in(streams_of[15], 71), 0)
    cotangent = noise(streams_of[14], (SEQS, LEN, D), 1.0, 6.0, ((0, 16), (1, 2)))
    return dict(tokens=tokens, lengths=lengths, w_query=w_query, w_forget=w_forget, w_input=w_input, w_gate_out=w_gate_out, w_output=w_output, w_ffn_gate=w_ffn_gate, w_ffn_up=w_ffn_up, w_ffn_down=w_ffn_down, norm_in=norm_in, norm_mid=norm_mid, head_gain=head_gain, gate_gap=gate_gap, cotangent=cotangent)


norm_eps = 1e-05
head_eps = 1e-06

@jax.custom_vjp
def low(v):
    return lax.optimization_barrier(v.astype(jnp.bfloat16)).astype(jnp.float32)

@jax.custom_vjp
def low_back(v):
    return v

def low_keep(v):
    return (low(v), None)

def low_pass(kept, grad):
    return (grad,)

def back_keep(v):
    return (v, None)

def back_low(kept, grad):
    return (low(grad),)
low.defvjp(low_keep, low_pass)
low_back.defvjp(back_keep, back_low)

def rms_scale(values_in, gain_vec, eps_value):
    return values_in * lax.rsqrt(lax.optimization_barrier(jnp.mean(values_in * values_in, axis=-1, keepdims=True)) + eps_value) * gain_vec

def product(left, right):
    return jnp.dot(left, right, precision=lax.Precision.HIGHEST)

def block_scan(queries, key_rows, value_rows, log_decay, state_init):
    block_count = queries.shape[0] // BLK
    head_count = queries.shape[1]
    shaped = tuple((item.reshape(block_count, BLK, head_count, -1) for item in (queries, key_rows, value_rows, log_decay)))
    causal_mask = jnp.arange(BLK)[:, None] >= jnp.arange(BLK)[None, :]
    highest = lax.Precision.HIGHEST

    def one_block(carried, block_items):
        query_blk, key_blk, value_blk, decay_blk = block_items
        cumul = jnp.cumsum(decay_blk, axis=0)
        query_dec = query_blk * jnp.exp(cumul)
        key_dec = key_blk * jnp.exp(-cumul)
        scores = jnp.einsum('thd,shd->hts', query_dec, key_dec, precision=highest)
        scores = jnp.where(causal_mask[None], scores, jnp.zeros_like(scores))
        outputs = jnp.einsum('hts,shv->thv', scores, value_blk, precision=highest)
        outputs = outputs + jnp.einsum('thd,hdv->thv', query_dec, carried, precision=highest)
        last_cum = cumul[-1]
        key_tail = key_blk * jnp.exp(last_cum[None] - cumul)
        new_state = jnp.exp(last_cum)[:, :, None] * carried + jnp.einsum('thd,thv->hdv', key_tail, value_blk, precision=highest)
        return (new_state, outputs)
    final_state, outputs = lax.scan(jax.checkpoint(one_block), state_init, shaped)
    return (outputs.reshape(queries.shape), final_state)

def layer(params, inputs, valid_rows):
    w_query, w_forget, w_input, w_gate_out, w_output, w_ffn_gate, w_ffn_up, w_ffn_down, norm_in, norm_mid, head_gain, gate_gap = params
    seq_len = inputs.shape[0]
    valid_col = valid_rows[:, None]
    normed = low(rms_scale(inputs, norm_in, norm_eps))
    proj_query = low_back(product(normed, w_query))
    proj_forget = low_back(product(normed, w_forget))
    proj_input = low_back(product(normed, w_input))
    proj_gate = low_back(product(normed, w_gate_out))
    queries = low(jax.nn.silu(proj_query))
    key_full = gate_gap * jax.nn.sigmoid(-proj_forget)
    key_rows = low(key_full)
    log_decay = jnp.log1p(-key_full)
    value_rows = low(proj_input)
    mixed, _ = block_scan(queries.reshape(seq_len, H, HD), key_rows.reshape(seq_len, H, HD), value_rows.reshape(seq_len, H, HD), log_decay.reshape(seq_len, H, HD), jnp.zeros((H, HD, HD), dtype=inputs.dtype))
    head_normed = rms_scale(mixed, head_gain, head_eps).reshape(seq_len, D)
    branch_in = low(head_normed * jax.nn.silu(proj_gate))
    branch_out = low_back(product(branch_in, w_output))
    hidden = inputs + valid_col * branch_out
    normed_mid = low(rms_scale(hidden, norm_mid, norm_eps))
    gate_vals = low_back(product(normed_mid, w_ffn_gate))
    up_vals = low_back(product(normed_mid, w_ffn_up))
    inner = low(jax.nn.silu(gate_vals) * up_vals)
    ffn_out = low_back(product(inner, w_ffn_down))
    return hidden + valid_col * ffn_out

def reference(tokens, lengths, w_query, w_forget, w_input, w_gate_out, w_output, w_ffn_gate, w_ffn_up, w_ffn_down, norm_in, norm_mid, head_gain, gate_gap, cotangent):
    params = tuple((item.astype(jnp.float32) for item in (w_query, w_forget, w_input, w_gate_out, w_output, w_ffn_gate, w_ffn_up, w_ffn_down, norm_in, norm_mid, head_gain, gate_gap)))
    positions = jnp.arange(LEN).astype(jnp.int32)

    def one_sequence(totals, seq_items):
        seq_tokens, seq_length, seq_cot = seq_items
        valid_rows = (positions < seq_length).astype(jnp.float32)
        outputs, backward = jax.vjp(lambda weights, inputs: layer(weights, inputs, valid_rows), params, seq_tokens.astype(jnp.float32))
        weight_grads, token_grad = backward(seq_cot.astype(jnp.float32))
        totals = jax.tree.map(lambda total, extra: total + extra, totals, weight_grads)
        return (totals, (outputs.astype(jnp.bfloat16), token_grad.astype(jnp.bfloat16)))
    zero_grads = jax.tree.map(jnp.zeros_like, params)
    grads, (outputs, token_grads) = lax.scan(one_sequence, zero_grads, (tokens, lengths, cotangent))
    return (outputs, token_grads, grads[0], grads[1], grads[2], grads[3], grads[4], grads[5], grads[6], grads[7], grads[8], grads[9], grads[10], grads[11])
```

```python
import functools

import jax
import jax.numpy as jnp
from jax import lax
from jax.experimental import pallas as pl
from jax.experimental.pallas import tpu as pltpu
from jax.sharding import PartitionSpec as P

H = 16
HD = 128
BLK = 128
SR = ("shard", "rep")

norm_eps = 1e-05
head_eps = 1e-06

f32 = jnp.float32
bf16 = jnp.bfloat16


def dsilu(values_in):
    sig_vals = jax.nn.sigmoid(values_in)
    return sig_vals * (1.0 + values_in * (1.0 - sig_vals))


def matmul(left, right):
    return jnp.dot(left, right, preferred_element_type=f32)


def matmul_nt(left, right):
    return lax.dot_general(left, right, (((1,), (1,)), ((), ())), preferred_element_type=f32)


def matmul_tn(left, right):
    return lax.dot_general(left, right, (((0,), (0,)), ((), ())), preferred_element_type=f32)


def block_sums(lower, values):
    high = values.astype(bf16)
    low = (values - high.astype(f32)).astype(bf16)
    return matmul(lower, high) + matmul(lower, low)


def head_forward(proj, gap, group_width):
    proj_query = proj[:, :group_width]
    proj_forget = proj[:, group_width : 2 * group_width]
    proj_input = proj[:, 2 * group_width : 3 * group_width]
    proj_gate = proj[:, 3 * group_width :]
    sig_query = jax.nn.sigmoid(proj_query)
    queries = (proj_query * sig_query).astype(bf16).astype(f32)
    forget_sig = jax.nn.sigmoid(-proj_forget)
    key_full = gap * forget_sig
    keys = key_full.astype(bf16).astype(f32)
    log_decay = jnp.log1p(-key_full)
    values = proj_input.astype(bf16)
    return proj_query, proj_gate, sig_query, queries, forget_sig, key_full, keys, log_decay, values


def triangle(kind, dtype):
    rows = lax.broadcasted_iota(jnp.int32, (BLK, BLK), 0)
    cols = lax.broadcasted_iota(jnp.int32, (BLK, BLK), 1)
    return (rows >= cols if kind == "lower" else rows <= cols).astype(dtype)


def forward_kernel(heads, proj_ref, gap_ref, gain_ref, branch_ref, states_ref, state):
    width = heads * HD

    @pl.when(pl.program_id(1) == 0)
    def _():
        state[...] = jnp.zeros_like(state)

    proj = proj_ref[...]
    _, proj_gate, _, queries, _, _, keys, log_decay, values = head_forward(proj, gap_ref[...], width)
    lower = triangle("lower", f32)
    cumul = block_sums(lower.astype(bf16), log_decay)
    grown = jnp.exp(cumul)
    query_dec = (queries * grown).astype(bf16)
    key_dec = (keys * jnp.exp(-cumul)).astype(bf16)
    last = cumul[BLK - 1 : BLK, :]
    key_tail = (keys * jnp.exp(last - cumul)).astype(bf16)
    last_decay = jnp.exp(last)
    gate_act = proj_gate * jax.nn.sigmoid(proj_gate)
    gain = gain_ref[...]
    for head in range(heads):
        span = slice(head * HD, (head + 1) * HD)
        before = state[head]
        states_ref[0, head] = before
        scores = matmul_nt(query_dec[:, span], key_dec[:, span]) * lower
        mixed = matmul(scores.astype(bf16), values[:, span])
        mixed = mixed + matmul(query_dec[:, span], before.astype(bf16))
        decay_col = jnp.transpose(jnp.broadcast_to(last_decay[:, span], (HD, HD)))
        state[head] = decay_col * before + matmul_tn(key_tail[:, span], values[:, span])
        scale = lax.rsqrt(jnp.mean(mixed * mixed, axis=-1, keepdims=True) + head_eps)
        branch_ref[:, span] = (mixed * scale * gain * gate_act[:, span]).astype(bf16)


def backward_kernel(
    heads, proj_ref, gap_ref, gain_ref, states_ref, grad_ref, out_ref, gap_out, gain_out, dstate, after
):
    width = heads * HD

    @pl.when(pl.program_id(1) == 0)
    def _():
        dstate[...] = jnp.zeros_like(dstate)
        after[...] = jnp.zeros_like(after)
        gap_out[...] = jnp.zeros_like(gap_out)
        gain_out[...] = jnp.zeros_like(gain_out)

    proj = proj_ref[...]
    gap = gap_ref[...]
    proj_query, proj_gate, sig_query, queries, forget_sig, key_full, keys, log_decay, values = head_forward(
        proj, gap, width
    )
    lower = triangle("lower", f32)
    upper = triangle("upper", bf16)
    cumul = block_sums(lower.astype(bf16), log_decay)
    grown = jnp.exp(cumul)
    shrunk = jnp.exp(-cumul)
    last = cumul[BLK - 1 : BLK, :]
    tail = jnp.exp(last - cumul)
    last_decay = jnp.exp(last)
    query_dec = (queries * grown).astype(bf16)
    key_dec = (keys * shrunk).astype(bf16)
    key_tail = (keys * tail).astype(bf16)
    sig_gate = jax.nn.sigmoid(proj_gate)
    gate_act = proj_gate * sig_gate
    gate_slope = sig_gate * (1.0 + proj_gate * (1.0 - sig_gate))
    grad_in = grad_ref[...].astype(f32)
    gain = gain_ref[...]
    gain_sum = jnp.zeros((1, HD), f32)
    query_grads, key_grads, value_grads, gate_grads, ends = [], [], [], [], []
    for head in range(heads):
        span = slice(head * HD, (head + 1) * HD)
        before = states_ref[0, head]
        before_low = before.astype(bf16)
        q_dec, k_dec, vals = query_dec[:, span], key_dec[:, span], values[:, span]
        scores = (matmul_nt(q_dec, k_dec) * lower).astype(bf16)
        mixed = matmul(scores, vals) + matmul(q_dec, before_low)
        scale = lax.rsqrt(jnp.mean(mixed * mixed, axis=-1, keepdims=True) + head_eps)
        unit = mixed * scale
        grad_b = grad_in[:, span]
        gate_grads.append(grad_b * unit * gain * gate_slope[:, span])
        grad_normed = grad_b * gate_act[:, span]
        gain_sum = gain_sum + jnp.sum(grad_normed * unit, axis=0, keepdims=True)
        grad_unit = grad_normed * gain
        grad_mixed = scale * (grad_unit - unit * jnp.mean(grad_unit * unit, axis=-1, keepdims=True))
        grad_low = grad_mixed.astype(bf16)
        down = dstate[head]
        down_low = down.astype(bf16)
        grad_scores = (matmul_nt(grad_low, vals) * lower).astype(bf16)
        value_grads.append(matmul_tn(scores, grad_low) + matmul(key_tail[:, span], down_low))
        grad_q = matmul(grad_scores, k_dec) + matmul_nt(grad_low, before_low)
        grad_k = matmul_tn(grad_scores, q_dec)
        grad_t = matmul_nt(vals, down_low)
        query_grads.append(grad_q * grown[:, span])
        key_grads.append(grad_k * shrunk[:, span] + grad_t * tail[:, span])
        ends.append(jnp.transpose(jnp.sum(down * after[head], axis=1, keepdims=True)))
        after[head] = before
        decay_col = jnp.transpose(jnp.broadcast_to(last_decay[:, span], (HD, HD)))
        dstate[head] = decay_col * down + matmul_tn(q_dec, grad_low)
    grad_queries = jnp.concatenate(query_grads, axis=1)
    grad_keys = jnp.concatenate(key_grads, axis=1)
    grad_values = jnp.concatenate(value_grads, axis=1)
    end = jnp.concatenate(ends, axis=1)
    grad_decay = block_sums(upper, queries * grad_queries - keys * grad_keys) + end
    grad_key_full = grad_keys - grad_decay / (1.0 - key_full)
    gap_out[...] += jnp.sum(grad_key_full * forget_sig, axis=0, keepdims=True)
    gain_out[...] += gain_sum
    query_slope = sig_query * (1.0 + proj_query * (1.0 - sig_query))
    out_ref[:, :width] = (grad_queries * query_slope).astype(bf16)
    out_ref[:, width : 2 * width] = (-grad_key_full * gap * forget_sig * (1.0 - forget_sig)).astype(bf16)
    out_ref[:, 2 * width : 3 * width] = grad_values.astype(bf16)
    out_ref[:, 3 * width :] = jnp.concatenate(gate_grads, axis=1).astype(bf16)


def mixer_forward(proj, gap, gain, heads):
    tokens, total = proj.shape
    groups, blocks = total // (4 * heads * HD), tokens // BLK
    width = heads * HD
    return pl.pallas_call(
        functools.partial(forward_kernel, heads),
        grid=(groups, blocks),
        in_specs=[
            pl.BlockSpec((BLK, 4 * width), lambda g, b: (b, g)),
            pl.BlockSpec((1, width), lambda g, b: (0, g)),
            pl.BlockSpec((1, HD), lambda g, b: (0, 0)),
        ],
        out_specs=[
            pl.BlockSpec((BLK, width), lambda g, b: (b, g)),
            pl.BlockSpec((1, heads, HD, HD), lambda g, b: (b, g, 0, 0)),
        ],
        out_shape=[
            jax.ShapeDtypeStruct((tokens, groups * width), bf16),
            jax.ShapeDtypeStruct((blocks, groups * heads, HD, HD), f32),
        ],
        scratch_shapes=[pltpu.VMEM((heads, HD, HD), f32)],
        compiler_params=pltpu.CompilerParams(vmem_limit_bytes=48 << 20),
        name="mixer_forward",
    )(proj, gap, gain)


def mixer_backward(proj, gap, gain, states, grad, heads):
    tokens, total = proj.shape
    groups, blocks = total // (4 * heads * HD), tokens // BLK
    width = heads * HD
    return pl.pallas_call(
        functools.partial(backward_kernel, heads),
        grid=(groups, blocks),
        in_specs=[
            pl.BlockSpec((BLK, 4 * width), lambda g, b: (blocks - 1 - b, g)),
            pl.BlockSpec((1, width), lambda g, b: (0, g)),
            pl.BlockSpec((1, HD), lambda g, b: (0, 0)),
            pl.BlockSpec((1, heads, HD, HD), lambda g, b: (blocks - 1 - b, g, 0, 0)),
            pl.BlockSpec((BLK, width), lambda g, b: (blocks - 1 - b, g)),
        ],
        out_specs=[
            pl.BlockSpec((BLK, 4 * width), lambda g, b: (blocks - 1 - b, g)),
            pl.BlockSpec((1, width), lambda g, b: (0, g)),
            pl.BlockSpec((1, 1, HD), lambda g, b: (g, 0, 0)),
        ],
        out_shape=[
            jax.ShapeDtypeStruct((tokens, total), bf16),
            jax.ShapeDtypeStruct((1, groups * width), f32),
            jax.ShapeDtypeStruct((groups, 1, HD), f32),
        ],
        scratch_shapes=[pltpu.VMEM((heads, HD, HD), f32), pltpu.VMEM((heads, HD, HD), f32)],
        compiler_params=pltpu.CompilerParams(vmem_limit_bytes=48 << 20),
        name="mixer_backward",
    )(proj, gap, gain, states, grad)


def swap(value):
    return lax.ppermute(value, "seq", [(0, 1), (1, 0)])


def in_order(own, other, axis):
    first = lax.axis_index("seq") == 0
    return jnp.concatenate([jnp.where(first, own, other), jnp.where(first, other, own)], axis=axis)


def gather_tokens(value):
    if lax.axis_size("seq") != 2:
        return lax.all_gather(value, "seq", axis=0, tiled=True)
    return in_order(value, swap(value), 0)


def scatter_tokens(partial):
    if lax.axis_size("seq") != 2:
        return lax.psum_scatter(partial.astype(bf16), "seq", scatter_dimension=0, tiled=True).astype(f32)
    rows = partial.shape[0] // 2
    me = lax.axis_index("seq")
    theirs = lax.dynamic_slice_in_dim(partial, (1 - me) * rows, rows, 0).astype(bf16)
    return lax.dynamic_slice_in_dim(partial, me * rows, rows, 0) + swap(theirs).astype(f32)


def columns_to_tokens(value):
    if lax.axis_size("seq") != 2:
        return lax.all_to_all(value, "seq", 0, 1, tiled=True)
    rows = value.shape[0] // 2
    me = lax.axis_index("seq")
    theirs = swap(lax.dynamic_slice_in_dim(value, (1 - me) * rows, rows, 0))
    return in_order(lax.dynamic_slice_in_dim(value, me * rows, rows, 0), theirs, 1)


def tokens_to_columns(value):
    if lax.axis_size("seq") != 2:
        return lax.all_to_all(value, "seq", 1, 0, tiled=True)
    cols = value.shape[1] // 2
    me = lax.axis_index("seq")
    theirs = swap(lax.dynamic_slice_in_dim(value, (1 - me) * cols, cols, 1))
    return in_order(lax.dynamic_slice_in_dim(value, me * cols, cols, 1), theirs, 0)


def body(
    tokens,
    lengths,
    w_query,
    w_forget,
    w_input,
    w_gate_out,
    w_output,
    w_ffn_gate,
    w_ffn_up,
    w_ffn_down,
    norm_in,
    norm_mid,
    head_gain,
    gate_gap,
    cotangent,
):
    row_count, width = tokens.shape[1:]
    seqs = lax.axis_size("seq")
    owners = lax.axis_size(SR)
    seq_index = lax.axis_index("seq")
    owner_index = lax.axis_index(SR)
    share = w_query.shape[0]
    local_width = width // seqs
    local_heads = H // seqs
    group = min(4, local_heads)
    groups = local_heads // group
    down_rows = w_ffn_down.shape[0]
    part = down_rows // seqs
    local_ff = owners * part

    inputs = tokens[0].astype(f32)
    positions = seq_index * row_count + jnp.arange(row_count)
    valid_col = (positions < lengths[0]).astype(f32)[:, None]

    def gathered(value):
        return lax.all_gather(value, SR, axis=0, tiled=True)

    def my_columns(weight):
        return lax.dynamic_slice_in_dim(weight, seq_index * local_width, local_width, 1)

    def my_units(weight):
        shaped = weight.reshape(share, owners, seqs, part)
        return lax.dynamic_index_in_dim(shaped, seq_index, 2, keepdims=False).reshape(share, local_ff)

    gains = jnp.concatenate([norm_in, norm_mid, gate_gap, head_gain])
    gains = lax.all_gather(gains, SR, axis=0, tiled=False).astype(f32)
    gain_in = gains[:, :share].reshape(1, width)
    gain_mid = gains[:, share : 2 * share].reshape(1, width)
    gap_full = gains[:, 2 * share : 3 * share].reshape(1, width)
    gain_head = gains[:, 3 * share :].reshape(1, HD)
    gap = lax.dynamic_slice_in_dim(gap_full, seq_index * local_width, local_width, 1)

    mix_share = jnp.stack([my_columns(w) for w in (w_query, w_forget, w_input, w_gate_out)], axis=1)
    mix_share = mix_share.reshape(share, 4, groups, group * HD).transpose(0, 2, 1, 3).reshape(share, 4 * local_width)
    w_mix = gathered(mix_share)
    w_out = gathered(w_output)
    w_gate_up = gathered(jnp.concatenate([my_units(w_ffn_gate), my_units(w_ffn_up)], axis=1))
    w_down = gathered(lax.dynamic_slice_in_dim(w_ffn_down, seq_index * part, part, 0))

    scale_in = lax.rsqrt(jnp.mean(inputs * inputs, axis=-1, keepdims=True) + norm_eps)
    unit_in = inputs * scale_in
    normed = gather_tokens((unit_in * gain_in).astype(bf16))
    grad_out = cotangent[0].astype(f32)
    grad_ffn = gather_tokens((valid_col * grad_out).astype(bf16))
    proj = matmul(normed, w_mix)
    branch_heads, states = mixer_forward(proj, gap, gain_head, group)
    branch_in = columns_to_tokens(branch_heads)
    hidden = inputs + valid_col * matmul(branch_in, w_out)

    scale_mid = lax.rsqrt(jnp.mean(hidden * hidden, axis=-1, keepdims=True) + norm_eps)
    unit_mid = hidden * scale_mid
    normed_mid = gather_tokens((unit_mid * gain_mid).astype(bf16))
    gate_up = matmul(normed_mid, w_gate_up)
    gate_vals = gate_up[:, :local_ff]
    up_vals = gate_up[:, local_ff:]
    gate_act = jax.nn.silu(gate_vals)
    inner = (gate_act * up_vals).astype(bf16)
    ffn_out = scatter_tokens(matmul(inner, w_down))
    layer_out = (hidden + valid_col * ffn_out).astype(bf16)[None]

    grad_inner = matmul_nt(grad_ffn, w_down)
    grad_down_w = matmul_tn(inner, grad_ffn).astype(bf16)
    grad_gate_vals = (grad_inner * up_vals * dsilu(gate_vals)).astype(bf16)
    grad_up_vals = (grad_inner * gate_act).astype(bf16)
    grad_gate_up = jnp.concatenate([grad_gate_vals, grad_up_vals], axis=1)
    grad_normed_mid = scatter_tokens(matmul_nt(grad_gate_up, w_gate_up))
    grad_gate_up_w = matmul_tn(normed_mid, grad_gate_up).astype(bf16)
    grad_gain_mid = jnp.sum(grad_normed_mid * unit_mid, axis=0)
    grad_unit_mid = grad_normed_mid * gain_mid
    grad_hidden = grad_out + scale_mid * (
        grad_unit_mid - unit_mid * jnp.mean(grad_unit_mid * unit_mid, axis=-1, keepdims=True)
    )

    grad_branch = (valid_col * grad_hidden).astype(bf16)
    grad_branch_in = tokens_to_columns(matmul_nt(grad_branch, w_out).astype(bf16))
    grad_output_w = matmul_tn(branch_in, grad_branch).astype(bf16)
    grad_proj, grad_gap, grad_gain_head = mixer_backward(proj, gap, gain_head, states, grad_branch_in, group)
    grad_normed = scatter_tokens(matmul_nt(grad_proj, w_mix))
    grad_mix_w = matmul_tn(normed, grad_proj).astype(bf16)
    grad_gain_in = jnp.sum(grad_normed * unit_in, axis=0)
    grad_unit_in = grad_normed * gain_in
    grad_inputs = grad_hidden + scale_in * (
        grad_unit_in - unit_in * jnp.mean(grad_unit_in * unit_in, axis=-1, keepdims=True)
    )
    input_grad = grad_inputs.astype(bf16)[None]

    def owned(value):
        return lax.psum_scatter(value, SR, scatter_dimension=0, tiled=True)

    down_share = owned(grad_down_w)
    gate_up_share = owned(grad_gate_up_w)
    out_share = owned(grad_output_w)
    mix_share = owned(grad_mix_w)

    grad_down = lax.all_gather(down_share, "seq", axis=0, tiled=True).astype(f32)
    gate_up_all = lax.all_gather(gate_up_share, "seq", axis=0).astype(f32)
    gate_up_all = gate_up_all.reshape(seqs, share, 2, owners, part).transpose(2, 1, 3, 0, 4)
    gate_up_all = gate_up_all.reshape(2, share, owners * down_rows)
    grad_output = lax.psum(out_share, "seq").astype(f32)
    mix_all = lax.all_gather(mix_share, "seq", axis=0).astype(f32)
    mix_all = mix_all.reshape(seqs, share, groups, 4, group * HD).transpose(3, 1, 0, 2, 4).reshape(4, share, width)

    gap_placed = lax.dynamic_update_slice_in_dim(
        jnp.zeros((width,), f32), grad_gap.reshape(local_width), seq_index * local_width, 0
    )
    head_total = jnp.sum(grad_gain_head, axis=(0, 1))
    small = jnp.concatenate([grad_gain_in, grad_gain_mid, gap_placed, head_total])
    small = lax.psum(small, ("seq",) + SR)

    def my_share(start, size):
        return lax.dynamic_slice_in_dim(small, start + owner_index * size, size, 0)

    return (
        layer_out,
        input_grad,
        mix_all[0],
        mix_all[1],
        mix_all[2],
        mix_all[3],
        grad_output,
        gate_up_all[0],
        gate_up_all[1],
        grad_down,
        my_share(0, share),
        my_share(width, share),
        my_share(3 * width, HD // owners),
        my_share(2 * width, share),
    )


def solution(mesh):
    rows = P(SR, None)
    vector = P(SR)
    by_token = P(SR, "seq", None)
    placed = (by_token, vector) + (rows,) * 8 + (vector,) * 4 + (by_token,)
    return jax.shard_map(
        body,
        mesh=mesh,
        in_specs=placed,
        out_specs=(by_token, by_token) + (rows,) * 8 + (vector,) * 4,
        check_vma=False,
    )
```

```python
import functools

import jax
import jax.numpy as jnp
from jax import lax
from jax.experimental import pallas as pl
from jax.experimental.pallas import tpu as pltpu
from jax.sharding import PartitionSpec as P

H = 16
HD = 128
BLK = 128
SR = ("shard", "rep")
MESH = pl.DeviceIdType.MESH

norm_eps = 1e-05
head_eps = 1e-06

f32 = jnp.float32
bf16 = jnp.bfloat16


def dsilu(values_in):
    sig_vals = jax.nn.sigmoid(values_in)
    return sig_vals * (1.0 + values_in * (1.0 - sig_vals))


def matmul(left, right):
    return jnp.dot(left, right, preferred_element_type=f32)


def matmul_nt(left, right):
    return lax.dot_general(left, right, (((1,), (1,)), ((), ())), preferred_element_type=f32)


def matmul_tn(left, right):
    return lax.dot_general(left, right, (((0,), (0,)), ((), ())), preferred_element_type=f32)


def block_sums(lower, values):
    high = values.astype(bf16)
    low = (values - high.astype(f32)).astype(bf16)
    return matmul(lower, high) + matmul(lower, low)


def head_forward(proj, gap, group_width):
    proj_query = proj[:, :group_width]
    proj_forget = proj[:, group_width : 2 * group_width]
    proj_input = proj[:, 2 * group_width : 3 * group_width]
    proj_gate = proj[:, 3 * group_width :]
    sig_query = jax.nn.sigmoid(proj_query)
    queries = (proj_query * sig_query).astype(bf16).astype(f32)
    forget_sig = jax.nn.sigmoid(-proj_forget)
    key_full = gap * forget_sig
    keys = key_full.astype(bf16).astype(f32)
    log_decay = jnp.log1p(-key_full)
    values = proj_input.astype(bf16)
    return proj_query, proj_gate, sig_query, queries, forget_sig, key_full, keys, log_decay, values


def triangle(kind, dtype):
    rows = lax.broadcasted_iota(jnp.int32, (BLK, BLK), 0)
    cols = lax.broadcasted_iota(jnp.int32, (BLK, BLK), 1)
    return (rows >= cols if kind == "lower" else rows <= cols).astype(dtype)


def forward_kernel(heads, proj_ref, gap_ref, gain_ref, branch_ref, states_ref, state):
    width = heads * HD

    @pl.when(pl.program_id(1) == 0)
    def _():
        state[...] = jnp.zeros_like(state)

    proj = proj_ref[...]
    _, proj_gate, _, queries, _, _, keys, log_decay, values = head_forward(proj, gap_ref[...], width)
    lower = triangle("lower", f32)
    cumul = block_sums(lower.astype(bf16), log_decay)
    grown = jnp.exp(cumul)
    query_dec = (queries * grown).astype(bf16)
    key_dec = (keys * jnp.exp(-cumul)).astype(bf16)
    last = cumul[BLK - 1 : BLK, :]
    key_tail = (keys * jnp.exp(last - cumul)).astype(bf16)
    last_decay = jnp.exp(last)
    gate_act = proj_gate * jax.nn.sigmoid(proj_gate)
    gain = gain_ref[...]
    for head in range(heads):
        span = slice(head * HD, (head + 1) * HD)
        before = state[head]
        states_ref[0, head] = before
        scores = matmul_nt(query_dec[:, span], key_dec[:, span]) * lower
        mixed = matmul(scores.astype(bf16), values[:, span])
        mixed = mixed + matmul(query_dec[:, span], before.astype(bf16))
        decay_col = jnp.transpose(jnp.broadcast_to(last_decay[:, span], (HD, HD)))
        state[head] = decay_col * before + matmul_tn(key_tail[:, span], values[:, span])
        scale = lax.rsqrt(jnp.mean(mixed * mixed, axis=-1, keepdims=True) + head_eps)
        branch_ref[:, span] = (mixed * scale * gain * gate_act[:, span]).astype(bf16)


def backward_kernel(
    heads, proj_ref, gap_ref, gain_ref, states_ref, grad_ref, out_ref, gap_out, gain_out, dstate, after
):
    width = heads * HD

    @pl.when(pl.program_id(1) == 0)
    def _():
        dstate[...] = jnp.zeros_like(dstate)
        after[...] = jnp.zeros_like(after)
        gap_out[...] = jnp.zeros_like(gap_out)
        gain_out[...] = jnp.zeros_like(gain_out)

    proj = proj_ref[...]
    gap = gap_ref[...]
    proj_query, proj_gate, sig_query, queries, forget_sig, key_full, keys, log_decay, values = head_forward(
        proj, gap, width
    )
    lower = triangle("lower", f32)
    upper = triangle("upper", bf16)
    cumul = block_sums(lower.astype(bf16), log_decay)
    grown = jnp.exp(cumul)
    shrunk = jnp.exp(-cumul)
    last = cumul[BLK - 1 : BLK, :]
    tail = jnp.exp(last - cumul)
    last_decay = jnp.exp(last)
    query_dec = (queries * grown).astype(bf16)
    key_dec = (keys * shrunk).astype(bf16)
    key_tail = (keys * tail).astype(bf16)
    sig_gate = jax.nn.sigmoid(proj_gate)
    gate_act = proj_gate * sig_gate
    gate_slope = sig_gate * (1.0 + proj_gate * (1.0 - sig_gate))
    grad_in = grad_ref[...].astype(f32)
    gain = gain_ref[...]
    gain_sum = jnp.zeros((1, HD), f32)
    query_grads, key_grads, value_grads, gate_grads, ends = [], [], [], [], []
    for head in range(heads):
        span = slice(head * HD, (head + 1) * HD)
        before = states_ref[0, head]
        before_low = before.astype(bf16)
        q_dec, k_dec, vals = query_dec[:, span], key_dec[:, span], values[:, span]
        scores = (matmul_nt(q_dec, k_dec) * lower).astype(bf16)
        mixed = matmul(scores, vals) + matmul(q_dec, before_low)
        scale = lax.rsqrt(jnp.mean(mixed * mixed, axis=-1, keepdims=True) + head_eps)
        unit = mixed * scale
        grad_b = grad_in[:, span]
        gate_grads.append(grad_b * unit * gain * gate_slope[:, span])
        grad_normed = grad_b * gate_act[:, span]
        gain_sum = gain_sum + jnp.sum(grad_normed * unit, axis=0, keepdims=True)
        grad_unit = grad_normed * gain
        grad_mixed = scale * (grad_unit - unit * jnp.mean(grad_unit * unit, axis=-1, keepdims=True))
        grad_low = grad_mixed.astype(bf16)
        down = dstate[head]
        down_low = down.astype(bf16)
        grad_scores = (matmul_nt(grad_low, vals) * lower).astype(bf16)
        value_grads.append(matmul_tn(scores, grad_low) + matmul(key_tail[:, span], down_low))
        grad_q = matmul(grad_scores, k_dec) + matmul_nt(grad_low, before_low)
        grad_k = matmul_tn(grad_scores, q_dec)
        grad_t = matmul_nt(vals, down_low)
        query_grads.append(grad_q * grown[:, span])
        key_grads.append(grad_k * shrunk[:, span] + grad_t * tail[:, span])
        ends.append(jnp.transpose(jnp.sum(down * after[head], axis=1, keepdims=True)))
        after[head] = before
        decay_col = jnp.transpose(jnp.broadcast_to(last_decay[:, span], (HD, HD)))
        dstate[head] = decay_col * down + matmul_tn(q_dec, grad_low)
    grad_queries = jnp.concatenate(query_grads, axis=1)
    grad_keys = jnp.concatenate(key_grads, axis=1)
    grad_values = jnp.concatenate(value_grads, axis=1)
    end = jnp.concatenate(ends, axis=1)
    grad_decay = block_sums(upper, queries * grad_queries - keys * grad_keys) + end
    grad_key_full = grad_keys - grad_decay / (1.0 - key_full)
    gap_out[...] += jnp.sum(grad_key_full * forget_sig, axis=0, keepdims=True)
    gain_out[...] += gain_sum
    query_slope = sig_query * (1.0 + proj_query * (1.0 - sig_query))
    out_ref[:, :width] = (grad_queries * query_slope).astype(bf16)
    out_ref[:, width : 2 * width] = (-grad_key_full * gap * forget_sig * (1.0 - forget_sig)).astype(bf16)
    out_ref[:, 2 * width : 3 * width] = grad_values.astype(bf16)
    out_ref[:, 3 * width :] = jnp.concatenate(gate_grads, axis=1).astype(bf16)


def mixer_forward(proj, gap, gain, heads):
    tokens, total = proj.shape
    groups, blocks = total // (4 * heads * HD), tokens // BLK
    width = heads * HD
    return pl.pallas_call(
        functools.partial(forward_kernel, heads),
        grid=(groups, blocks),
        in_specs=[
            pl.BlockSpec((BLK, 4 * width), lambda g, b: (b, g)),
            pl.BlockSpec((1, width), lambda g, b: (0, g)),
            pl.BlockSpec((1, HD), lambda g, b: (0, 0)),
        ],
        out_specs=[
            pl.BlockSpec((BLK, width), lambda g, b: (b, g)),
            pl.BlockSpec((1, heads, HD, HD), lambda g, b: (b, g, 0, 0)),
        ],
        out_shape=[
            jax.ShapeDtypeStruct((tokens, groups * width), bf16),
            jax.ShapeDtypeStruct((blocks, groups * heads, HD, HD), f32),
        ],
        scratch_shapes=[pltpu.VMEM((heads, HD, HD), f32)],
        compiler_params=pltpu.CompilerParams(vmem_limit_bytes=48 << 20),
        name="mixer_forward",
    )(proj, gap, gain)


def mixer_backward(proj, gap, gain, states, grad, heads):
    tokens, total = proj.shape
    groups, blocks = total // (4 * heads * HD), tokens // BLK
    width = heads * HD
    return pl.pallas_call(
        functools.partial(backward_kernel, heads),
        grid=(groups, blocks),
        in_specs=[
            pl.BlockSpec((BLK, 4 * width), lambda g, b: (blocks - 1 - b, g)),
            pl.BlockSpec((1, width), lambda g, b: (0, g)),
            pl.BlockSpec((1, HD), lambda g, b: (0, 0)),
            pl.BlockSpec((1, heads, HD, HD), lambda g, b: (blocks - 1 - b, g, 0, 0)),
            pl.BlockSpec((BLK, width), lambda g, b: (blocks - 1 - b, g)),
        ],
        out_specs=[
            pl.BlockSpec((BLK, 4 * width), lambda g, b: (blocks - 1 - b, g)),
            pl.BlockSpec((1, width), lambda g, b: (0, g)),
            pl.BlockSpec((1, 1, HD), lambda g, b: (g, 0, 0)),
        ],
        out_shape=[
            jax.ShapeDtypeStruct((tokens, total), bf16),
            jax.ShapeDtypeStruct((1, groups * width), f32),
            jax.ShapeDtypeStruct((groups, 1, HD), f32),
        ],
        scratch_shapes=[pltpu.VMEM((heads, HD, HD), f32), pltpu.VMEM((heads, HD, HD), f32)],
        compiler_params=pltpu.CompilerParams(vmem_limit_bytes=48 << 20),
        name="mixer_backward",
    )(proj, gap, gain, states, grad)


def swap(value):
    return lax.ppermute(value, "seq", [(0, 1), (1, 0)])


def in_order(own, other, axis):
    first = lax.axis_index("seq") == 0
    return jnp.concatenate([jnp.where(first, own, other), jnp.where(first, other, own)], axis=axis)


def gather_tokens(value):
    if lax.axis_size("seq") != 2:
        return lax.all_gather(value, "seq", axis=0, tiled=True)
    return in_order(value, swap(value), 0)


def scatter_tokens(partial):
    if lax.axis_size("seq") != 2:
        return lax.psum_scatter(partial.astype(bf16), "seq", scatter_dimension=0, tiled=True).astype(f32)
    rows = partial.shape[0] // 2
    me = lax.axis_index("seq")
    theirs = lax.dynamic_slice_in_dim(partial, (1 - me) * rows, rows, 0).astype(bf16)
    return lax.dynamic_slice_in_dim(partial, me * rows, rows, 0) + swap(theirs).astype(f32)


def columns_to_tokens(value):
    if lax.axis_size("seq") != 2:
        return lax.all_to_all(value, "seq", 0, 1, tiled=True)
    rows = value.shape[0] // 2
    me = lax.axis_index("seq")
    theirs = swap(lax.dynamic_slice_in_dim(value, (1 - me) * rows, rows, 0))
    return in_order(lax.dynamic_slice_in_dim(value, me * rows, rows, 0), theirs, 1)


def tokens_to_columns(value):
    if lax.axis_size("seq") != 2:
        return lax.all_to_all(value, "seq", 1, 0, tiled=True)
    cols = value.shape[1] // 2
    me = lax.axis_index("seq")
    theirs = swap(lax.dynamic_slice_in_dim(value, (1 - me) * cols, cols, 1))
    return in_order(lax.dynamic_slice_in_dim(value, me * cols, cols, 1), theirs, 0)


RING = 8
CHUNK = 256


def reduce_kernel(counts, *refs):
    kinds = len(counts)
    lefts, rights = refs[:kinds], refs[kinds : 2 * kinds]
    (
        out_ref,
        core_out,
        core_in,
        pair_out,
        pair_in,
        sums,
        line_in,
        done,
        core_sems,
        pair_sems,
        line_send,
        line_recv,
        done_sems,
    ) = refs[2 * kinds :]
    total = sum(counts)
    planes, rows = sums.shape[1:3]
    seq = lax.axis_index("seq")
    shard = lax.axis_index("shard")
    plane = lax.axis_index("rep")
    core, pair = shard % 2, shard // 2
    other_core = {"shard": shard + 1 - 2 * core}
    other_pair = {"shard": (shard + 2) % 4}
    other_seq = {"seq": 1 - seq}
    below, above = {"rep": plane - 1}, {"rep": plane + 1}
    has_below, has_above = plane > 0, plane < planes - 1

    barrier = pltpu.get_barrier_semaphore()
    for device in (other_core, other_pair, other_seq):
        pl.semaphore_signal(barrier, inc=1, device_id=device, device_id_type=MESH)
    for there, device in ((has_below, below), (has_above, above)):

        @pl.when(there)
        def _(device=device):
            pl.semaphore_signal(barrier, inc=1, device_id=device, device_id_type=MESH)

    pl.semaphore_wait(barrier, 3 + has_below.astype(jnp.int32) + has_above.astype(jnp.int32))

    def remote(source, target, send, recv, device):
        return pltpu.make_async_remote_copy(
            src_ref=source, dst_ref=target, send_sem=send, recv_sem=recv, device_id=device, device_id_type=MESH
        )

    def core_copy(slot):
        return remote(
            core_out.at[slot], core_in.at[slot], core_sems.at[0, slot], core_sems.at[1, slot], other_core
        )

    def pair_copy(slot):
        return remote(
            pair_out.at[slot], pair_in.at[slot], pair_sems.at[0, slot], pair_sems.at[1, slot], other_pair
        )

    def line_copy(way, step, slot, target):
        return remote(
            sums.at[slot, target],
            line_in.at[way, step - 1, slot],
            line_send.at[way, step - 1, slot],
            line_recv.at[way, step - 1, slot],
            above if way else below,
        )

    def done_copies(chunk):
        slot = chunk % RING
        place = out_ref.at[seq, :, pl.ds(pl.multiple_of(chunk * CHUNK, CHUNK), CHUNK)]
        kept = pltpu.make_async_copy(done.at[slot], place, done_sems.at[2, slot])
        sent = remote(done.at[slot], place, done_sems.at[0, slot], done_sems.at[1, slot], other_seq)
        return kept, sent

    def product(kind, chunk, half, which):
        first = (half * 2 + which) * planes * rows
        left = lefts[kind][pl.ds(pl.multiple_of(first, planes * rows), planes * rows), :]
        start = (chunk - sum(counts[:kind])) * CHUNK
        return matmul(left, rights[kind][:, pl.ds(pl.multiple_of(start, CHUNK), CHUNK)])

    def line_target(way, step):
        return plane + planes - step if way else plane - planes + step

    def sends(way, step):
        return plane < step if way else plane >= planes - step

    def receives(way, step):
        return jnp.logical_and(plane > 0, plane <= step) if way else jnp.logical_and(plane < planes - 1, plane >= planes - step - 1)

    def front(kind, chunk):
        slot = chunk % RING

        @pl.when(chunk >= RING)
        def _():
            core_copy(slot).wait_send()

        for half in range(2):
            core_out[slot, half] = product(kind, chunk, half, 1 - core).astype(bf16)
        core_copy(slot).start()

    def middle(kind, chunk):
        slot = chunk % RING

        @pl.when(chunk >= RING)
        def _():
            pair_copy(slot).wait_send()

        theirs = product(kind, chunk, 1 - pair, core)
        mine = product(kind, chunk, pair, core)
        core_copy(slot).wait_recv()
        pair_out[slot] = (theirs + core_in[slot, 1 - pair].astype(f32)).astype(bf16)
        pair_copy(slot).start()
        mine = mine + core_in[slot, pair].astype(f32)
        sums[slot] = mine.astype(bf16).reshape(planes, rows, CHUNK)

    def line_start(chunk, step):
        slot = chunk % RING
        for way in range(2):

            @pl.when(sends(way, step))
            def _(way=way):
                target = line_target(way, step)
                if step > 1:

                    @pl.when(receives(way, step - 1))
                    def _():
                        line_copy(way, step - 1, slot, 0).wait_recv()
                        got = line_in[way, step - 2, slot].astype(f32)
                        sums[slot, target] = (sums[slot, target].astype(f32) + got).astype(bf16)

                line_copy(way, step, slot, target).start()

    def pair_done(chunk):
        slot = chunk % RING
        pair_copy(slot).wait_recv()
        got = pair_in[slot].reshape(planes, rows, CHUNK).astype(f32)
        sums[slot] = (sums[slot].astype(f32) + got).astype(bf16)
        line_start(chunk, 1)

    def finish(chunk):
        slot = chunk % RING
        kept, sent = done_copies(chunk)

        @pl.when(chunk >= RING)
        def _():
            kept.wait()
            sent.wait_send()

        last = planes - 1
        for way in range(2):

            @pl.when(receives(way, last))
            def _(way=way):
                line_copy(way, last, slot, 0).wait_recv()
                got = line_in[way, last - 1, slot].astype(f32)
                sums[slot, plane] = (sums[slot, plane].astype(f32) + got).astype(bf16)

        done[slot] = sums[slot, plane]
        kept.start()
        sent.start()
        for way in range(2):
            for step in range(1, planes):

                @pl.when(sends(way, step))
                def _(way=way, step=step):
                    line_copy(way, step, slot, 0).wait_send()

    def received(chunk):
        done_copies(chunk)[1].wait_recv()

    later = [(pair_done, 3)] + [
        (functools.partial(line_start, step=step), 2 + step) for step in range(2, planes)
    ] + [(finish, 2 + planes), (received, 4 + planes)]
    first = 0
    for kind, count in enumerate(counts):

        def step(turn, _, kind=kind, first=first):
            front(kind, turn)
            if kind == 0:
                pl.when(turn >= 1)(lambda: middle(0, turn - 1))
            else:
                pl.when(turn == first)(lambda: middle(kind - 1, turn - 1))
                pl.when(turn > first)(lambda: middle(kind, turn - 1))
            for act, lag in later:
                pl.when(turn >= lag)(lambda act=act, lag=lag: act(turn - lag))
            return 0

        lax.fori_loop(first, first + count, step, 0)
        first += count

    def drain(turn, _):
        pl.when(turn == total)(lambda: middle(kinds - 1, turn - 1))
        for act, lag in later:
            pl.when(turn - lag < total)(lambda act=act, lag=lag: act(turn - lag))
        return 0

    lax.fori_loop(total, total + later[-1][1], drain, 0)
    for chunk in range(total - RING, total):
        slot = chunk % RING
        core_copy(slot).wait_send()
        pair_copy(slot).wait_send()
        kept, sent = done_copies(chunk)
        kept.wait()
        sent.wait_send()


def reduced_gradients(lefts, rights):
    counts = [right.shape[1] // CHUNK for right in rights]
    planes = lax.axis_size("rep")
    rows = lefts[0].shape[0] // lax.axis_size(SR)
    block = planes * rows
    vmem = pl.BlockSpec(memory_space=pltpu.VMEM)
    return pl.pallas_call(
        functools.partial(reduce_kernel, counts),
        in_specs=[vmem] * (2 * len(lefts)),
        out_specs=pl.BlockSpec(memory_space=pl.ANY),
        out_shape=jax.ShapeDtypeStruct((2, rows, sum(counts) * CHUNK), bf16),
        scratch_shapes=[
            pltpu.VMEM((RING, 2, block, CHUNK), bf16),
            pltpu.VMEM((RING, 2, block, CHUNK), bf16),
            pltpu.VMEM((RING, block, CHUNK), bf16),
            pltpu.VMEM((RING, block, CHUNK), bf16),
            pltpu.VMEM((RING, planes, rows, CHUNK), bf16),
            pltpu.VMEM((2, planes - 1, RING, rows, CHUNK), bf16),
            pltpu.VMEM((RING, rows, CHUNK), bf16),
            pltpu.SemaphoreType.DMA((2, RING)),
            pltpu.SemaphoreType.DMA((2, RING)),
            pltpu.SemaphoreType.DMA((2, planes - 1, RING)),
            pltpu.SemaphoreType.DMA((2, planes - 1, RING)),
            pltpu.SemaphoreType.DMA((3, RING)),
        ],
        compiler_params=pltpu.CompilerParams(
            collective_id=0, has_side_effects=True, vmem_limit_bytes=56 << 20
        ),
        name="reduced_gradients",
    )(*lefts, *rights)


def share_columns(share):
    if lax.axis_size("seq") != 2:
        return lax.all_gather(share, "seq", axis=0)
    return in_order(share[None], swap(share)[None], 0)


def body(
    tokens,
    lengths,
    w_query,
    w_forget,
    w_input,
    w_gate_out,
    w_output,
    w_ffn_gate,
    w_ffn_up,
    w_ffn_down,
    norm_in,
    norm_mid,
    head_gain,
    gate_gap,
    cotangent,
):
    row_count, width = tokens.shape[1:]
    seqs = lax.axis_size("seq")
    owners = lax.axis_size(SR)
    seq_index = lax.axis_index("seq")
    owner_index = lax.axis_index(SR)
    share = w_query.shape[0]
    local_width = width // seqs
    local_heads = H // seqs
    group = min(4, local_heads)
    groups = local_heads // group
    down_rows = w_ffn_down.shape[0]
    part = down_rows // seqs
    local_ff = owners * part

    inputs = tokens[0].astype(f32)
    positions = seq_index * row_count + jnp.arange(row_count)
    valid_col = (positions < lengths[0]).astype(f32)[:, None]

    def gathered(value):
        return lax.all_gather(value, SR, axis=0, tiled=True)

    def owned(value):
        return lax.psum_scatter(value, SR, scatter_dimension=0, tiled=True)

    def my_columns(weight):
        return lax.dynamic_slice_in_dim(weight, seq_index * local_width, local_width, 1)

    def my_units(weight):
        shaped = weight.reshape(share, owners, seqs, part)
        return lax.dynamic_index_in_dim(shaped, seq_index, 2, keepdims=False).reshape(share, local_ff)

    gains = jnp.stack([norm_in, norm_mid, gate_gap, jnp.pad(head_gain, (0, share - head_gain.shape[0]))])
    gains = jnp.pad(gains.astype(f32), ((0, 4), (0, 0)))
    gains = gathered(gains).reshape(owners, 8, share)
    gain_in = gains[:, 0].reshape(1, width)
    gain_mid = gains[:, 1].reshape(1, width)
    gap_full = gains[:, 2].reshape(1, width)
    gain_head = gains[:, 3, : head_gain.shape[0]].reshape(1, HD)
    gap = lax.dynamic_slice_in_dim(gap_full, seq_index * local_width, local_width, 1)

    mix_share = jnp.stack([my_columns(w) for w in (w_query, w_forget, w_input, w_gate_out)], axis=1)
    mix_share = mix_share.reshape(share, 4, groups, group * HD).transpose(0, 2, 1, 3).reshape(share, 4 * local_width)
    w_mix = gathered(mix_share)
    w_out = gathered(w_output)
    w_gate_up = gathered(jnp.concatenate([my_units(w_ffn_gate), my_units(w_ffn_up)], axis=1))
    w_down = gathered(lax.dynamic_slice_in_dim(w_ffn_down, seq_index * part, part, 0))

    scale_in = lax.rsqrt(jnp.mean(inputs * inputs, axis=-1, keepdims=True) + norm_eps)
    unit_in = inputs * scale_in
    all_tokens = gather_tokens(tokens[0]).astype(f32)
    all_scale = lax.rsqrt(jnp.mean(all_tokens * all_tokens, axis=-1, keepdims=True) + norm_eps)
    normed = (all_tokens * all_scale * gain_in).astype(bf16)
    grad_out = cotangent[0].astype(f32)
    grad_ffn = gather_tokens((valid_col * grad_out).astype(bf16))
    proj = matmul(normed, w_mix)
    branch_heads, states = mixer_forward(proj, gap, gain_head, group)
    branch_in = columns_to_tokens(branch_heads)
    hidden = inputs + valid_col * matmul(branch_in, w_out)

    scale_mid = lax.rsqrt(jnp.mean(hidden * hidden, axis=-1, keepdims=True) + norm_eps)
    unit_mid = hidden * scale_mid
    normed_mid = gather_tokens((unit_mid * gain_mid).astype(bf16))
    gate_up = matmul(normed_mid, w_gate_up)
    gate_vals = gate_up[:, :local_ff]
    up_vals = gate_up[:, local_ff:]
    gate_act = jax.nn.silu(gate_vals)
    inner = (gate_act * up_vals).astype(bf16)
    ffn_out = scatter_tokens(matmul(inner, w_down))
    layer_out = (hidden + valid_col * ffn_out).astype(bf16)[None]

    grad_inner = matmul_nt(grad_ffn, w_down)
    down_share = owned(matmul_tn(inner, grad_ffn).astype(bf16))
    grad_gate_vals = (grad_inner * up_vals * dsilu(gate_vals)).astype(bf16)
    grad_up_vals = (grad_inner * gate_act).astype(bf16)
    grad_gate_up = jnp.concatenate([grad_gate_vals, grad_up_vals], axis=1)
    grad_normed_mid = scatter_tokens(matmul_nt(grad_gate_up, w_gate_up))
    grad_gain_mid = jnp.sum(grad_normed_mid * unit_mid, axis=0)
    grad_unit_mid = grad_normed_mid * gain_mid
    grad_hidden = grad_out + scale_mid * (
        grad_unit_mid - unit_mid * jnp.mean(grad_unit_mid * unit_mid, axis=-1, keepdims=True)
    )

    grad_branch = (valid_col * grad_hidden).astype(bf16)
    grad_branch_in = tokens_to_columns(matmul_nt(grad_branch, w_out).astype(bf16))
    grad_proj, grad_gap, grad_gain_head = mixer_backward(proj, gap, gain_head, states, grad_branch_in, group)
    grad_normed = scatter_tokens(matmul_nt(grad_proj, w_mix))
    grad_gain_in = jnp.sum(grad_normed * unit_in, axis=0)
    grad_unit_in = grad_normed * gain_in
    grad_inputs = grad_hidden + scale_in * (
        grad_unit_in - unit_in * jnp.mean(grad_unit_in * unit_in, axis=-1, keepdims=True)
    )
    input_grad = grad_inputs.astype(bf16)[None]

    lefts = [value.T for value in (normed_mid, gather_tokens(branch_in), normed)]
    rights = [grad_gate_up, tokens_to_columns(grad_branch), grad_proj]
    if seqs == 2 and lax.axis_size("shard") == 4:
        reduced = reduced_gradients(lefts, rights)
    else:
        partial = jnp.concatenate([matmul(left, right).astype(bf16) for left, right in zip(lefts, rights)], axis=1)
        reduced = lax.all_gather(owned(partial), "seq", axis=0)
    reduced = reduced.astype(f32)
    ends = (2 * local_ff, 2 * local_ff + local_width)
    grad_units = reduced[:, :, : ends[0]].reshape(seqs, share, 2, owners, part).transpose(2, 1, 3, 0, 4)
    grad_gate, grad_up = grad_units.reshape(2, share, owners * down_rows)
    grad_output = reduced[:, :, ends[0] : ends[1]].transpose(1, 0, 2).reshape(share, width)
    mix_all = reduced[:, :, ends[1] :].reshape(seqs, share, groups, 4, group * HD)
    mix_all = mix_all.transpose(3, 1, 0, 2, 4).reshape(4, share, width)
    grad_down = share_columns(down_share).reshape(down_rows, width).astype(f32)

    gap_placed = lax.dynamic_update_slice_in_dim(
        jnp.zeros((width,), f32), grad_gap.reshape(local_width), seq_index * local_width, 0
    )
    head_total = jnp.sum(grad_gain_head, axis=(0, 1))
    small = jnp.concatenate([grad_gain_in, grad_gain_mid, gap_placed, head_total])
    small = lax.psum(small, ("seq",) + SR)

    def my_share(start, size):
        return lax.dynamic_slice_in_dim(small, start + owner_index * size, size, 0)

    return (
        layer_out,
        input_grad,
        mix_all[0],
        mix_all[1],
        mix_all[2],
        mix_all[3],
        grad_output,
        grad_gate,
        grad_up,
        grad_down,
        my_share(0, share),
        my_share(width, share),
        my_share(3 * width, HD // owners),
        my_share(2 * width, share),
    )


def solution(mesh):
    rows = P(SR, None)
    vector = P(SR)
    by_token = P(SR, "seq", None)
    placed = (by_token, vector) + (rows,) * 8 + (vector,) * 4 + (by_token,)
    return jax.shard_map(
        body,
        mesh=mesh,
        in_specs=placed,
        out_specs=(by_token, by_token) + (rows,) * 8 + (vector,) * 4,
        check_vma=False,
    )
```

```python
import functools

import jax
import jax.numpy as jnp
from jax import lax
from jax.experimental import pallas as pl
from jax.experimental.pallas import tpu as pltpu
from jax.sharding import PartitionSpec as P

H = 16
HD = 128
BLK = 128
SR = ("shard", "rep")
MESH = pl.DeviceIdType.MESH

norm_eps = 1e-05
head_eps = 1e-06

f32 = jnp.float32
bf16 = jnp.bfloat16


def dsilu(values_in):
    sig_vals = jax.nn.sigmoid(values_in)
    return sig_vals * (1.0 + values_in * (1.0 - sig_vals))


def matmul(left, right):
    return jnp.dot(left, right, preferred_element_type=f32)


def matmul_nt(left, right):
    return lax.dot_general(left, right, (((1,), (1,)), ((), ())), preferred_element_type=f32)


def matmul_tn(left, right):
    return lax.dot_general(left, right, (((0,), (0,)), ((), ())), preferred_element_type=f32)


def block_sums(lower, values):
    high, low = split(values)
    return matmul(lower, high) + matmul(lower, low)


def split(values):
    high = values.astype(bf16)
    return high, (values - high.astype(f32)).astype(bf16)


def head_forward(proj, gap, group_width):
    proj_query = proj[:, :group_width]
    proj_forget = proj[:, group_width : 2 * group_width]
    proj_input = proj[:, 2 * group_width : 3 * group_width]
    proj_gate = proj[:, 3 * group_width :]
    sig_query = jax.nn.sigmoid(proj_query)
    queries = (proj_query * sig_query).astype(bf16).astype(f32)
    forget_sig = jax.nn.sigmoid(-proj_forget)
    key_full = gap * forget_sig
    keys = key_full.astype(bf16).astype(f32)
    log_decay = jnp.log1p(-key_full)
    values = proj_input.astype(bf16)
    return proj_query, proj_gate, sig_query, queries, forget_sig, key_full, keys, log_decay, values


def triangle(kind, dtype):
    rows = lax.broadcasted_iota(jnp.int32, (BLK, BLK), 0)
    cols = lax.broadcasted_iota(jnp.int32, (BLK, BLK), 1)
    return (rows >= cols if kind == "lower" else rows <= cols).astype(dtype)


def forward_kernel(heads, proj_ref, gap_ref, gain_ref, branch_ref, states_ref, mixed_ref, state):
    width = heads * HD

    @pl.when(pl.program_id(1) == 0)
    def _():
        state[...] = jnp.zeros_like(state)

    proj = proj_ref[...]
    _, proj_gate, _, queries, _, _, keys, log_decay, values = head_forward(proj, gap_ref[...], width)
    lower = triangle("lower", f32)
    cumul = block_sums(lower.astype(bf16), log_decay)
    grown = jnp.exp(cumul)
    query_dec, query_low = split(queries * grown)
    key_dec, key_low = split(keys * jnp.exp(-cumul))
    last = cumul[BLK - 1 : BLK, :]
    key_tail = (keys * jnp.exp(last - cumul)).astype(bf16)
    last_decay = jnp.exp(last)
    gate_act = proj_gate * jax.nn.sigmoid(proj_gate)
    gain = gain_ref[...]
    for head in range(heads):
        span = slice(head * HD, (head + 1) * HD)
        before = state[head]
        states_ref[0, head] = before
        scores = matmul_nt(query_low[:, span], key_dec[:, span]) + matmul_nt(query_dec[:, span], key_low[:, span])
        scores = (scores + matmul_nt(query_dec[:, span], key_dec[:, span])) * lower
        scores, scores_low = split(scores)
        mixed = matmul(scores_low, values[:, span]) + matmul(scores, values[:, span])
        mixed = mixed + matmul(query_dec[:, span], before.astype(bf16))
        mixed_ref[:, span] = mixed
        decay_col = jnp.transpose(jnp.broadcast_to(last_decay[:, span], (HD, HD)))
        state[head] = decay_col * before + matmul_tn(key_tail[:, span], values[:, span])
        scale = lax.rsqrt(jnp.mean(mixed * mixed, axis=-1, keepdims=True) + head_eps)
        branch_ref[:, span] = (mixed * scale * gain * gate_act[:, span]).astype(bf16)


def backward_kernel(
    heads, proj_ref, gap_ref, gain_ref, states_ref, mixed_ref, grad_ref, out_ref, gap_out, gain_out, dstate, after
):
    width = heads * HD

    @pl.when(pl.program_id(1) == 0)
    def _():
        dstate[...] = jnp.zeros_like(dstate)
        after[...] = jnp.zeros_like(after)
        gap_out[...] = jnp.zeros_like(gap_out)
        gain_out[...] = jnp.zeros_like(gain_out)

    proj = proj_ref[...]
    gap = gap_ref[...]
    proj_query, proj_gate, sig_query, queries, forget_sig, key_full, keys, log_decay, values = head_forward(
        proj, gap, width
    )
    lower = triangle("lower", f32)
    upper = triangle("upper", bf16)
    cumul = block_sums(lower.astype(bf16), log_decay)
    grown = jnp.exp(cumul)
    shrunk = jnp.exp(-cumul)
    last = cumul[BLK - 1 : BLK, :]
    tail = jnp.exp(last - cumul)
    last_decay = jnp.exp(last)
    query_dec = (queries * grown).astype(bf16)
    key_dec = (keys * shrunk).astype(bf16)
    key_tail = (keys * tail).astype(bf16)
    sig_gate = jax.nn.sigmoid(proj_gate)
    gate_act = proj_gate * sig_gate
    gate_slope = sig_gate * (1.0 + proj_gate * (1.0 - sig_gate))
    grad_in = grad_ref[...].astype(f32)
    gain = gain_ref[...]
    gain_sum = jnp.zeros((1, HD), f32)
    query_grads, key_grads, value_grads, gate_grads, ends = [], [], [], [], []
    for head in range(heads):
        span = slice(head * HD, (head + 1) * HD)
        before = states_ref[0, head]
        before_low = before.astype(bf16)
        q_dec, k_dec, vals = query_dec[:, span], key_dec[:, span], values[:, span]
        scores = (matmul_nt(q_dec, k_dec) * lower).astype(bf16)
        mixed = mixed_ref[:, span]
        scale = lax.rsqrt(jnp.mean(mixed * mixed, axis=-1, keepdims=True) + head_eps)
        unit = mixed * scale
        grad_b = grad_in[:, span]
        gate_grads.append(grad_b * unit * gain * gate_slope[:, span])
        grad_normed = grad_b * gate_act[:, span]
        gain_sum = gain_sum + jnp.sum(grad_normed * unit, axis=0, keepdims=True)
        grad_unit = grad_normed * gain
        grad_mixed = scale * (grad_unit - unit * jnp.mean(grad_unit * unit, axis=-1, keepdims=True))
        grad_low = grad_mixed.astype(bf16)
        down = dstate[head]
        down_low = down.astype(bf16)
        grad_scores = (matmul_nt(grad_low, vals) * lower).astype(bf16)
        value_grads.append(matmul_tn(scores, grad_low) + matmul(key_tail[:, span], down_low))
        grad_q = matmul(grad_scores, k_dec) + matmul_nt(grad_low, before_low)
        grad_k = matmul_tn(grad_scores, q_dec)
        grad_t = matmul_nt(vals, down_low)
        query_grads.append(grad_q * grown[:, span])
        key_grads.append(grad_k * shrunk[:, span] + grad_t * tail[:, span])
        ends.append(jnp.transpose(jnp.sum(down * after[head], axis=1, keepdims=True)))
        after[head] = before
        decay_col = jnp.transpose(jnp.broadcast_to(last_decay[:, span], (HD, HD)))
        dstate[head] = decay_col * down + matmul_tn(q_dec, grad_low)
    grad_queries = jnp.concatenate(query_grads, axis=1)
    grad_keys = jnp.concatenate(key_grads, axis=1)
    grad_values = jnp.concatenate(value_grads, axis=1)
    end = jnp.concatenate(ends, axis=1)
    grad_decay = block_sums(upper, queries * grad_queries - keys * grad_keys) + end
    grad_key_full = grad_keys - grad_decay / (1.0 - key_full)
    gap_out[...] += jnp.sum(grad_key_full * forget_sig, axis=0, keepdims=True)
    gain_out[...] += gain_sum
    query_slope = sig_query * (1.0 + proj_query * (1.0 - sig_query))
    out_ref[:, :width] = (grad_queries * query_slope).astype(bf16)
    out_ref[:, width : 2 * width] = (-grad_key_full * gap * forget_sig * (1.0 - forget_sig)).astype(bf16)
    out_ref[:, 2 * width : 3 * width] = grad_values.astype(bf16)
    out_ref[:, 3 * width :] = jnp.concatenate(gate_grads, axis=1).astype(bf16)


def mixer_forward(proj, gap, gain, heads):
    tokens, total = proj.shape
    groups, blocks = total // (4 * heads * HD), tokens // BLK
    width = heads * HD
    return pl.pallas_call(
        functools.partial(forward_kernel, heads),
        grid=(groups, blocks),
        in_specs=[
            pl.BlockSpec((BLK, 4 * width), lambda g, b: (b, g)),
            pl.BlockSpec((1, width), lambda g, b: (0, g)),
            pl.BlockSpec((1, HD), lambda g, b: (0, 0)),
        ],
        out_specs=[
            pl.BlockSpec((BLK, width), lambda g, b: (b, g)),
            pl.BlockSpec((1, heads, HD, HD), lambda g, b: (b, g, 0, 0)),
            pl.BlockSpec((BLK, width), lambda g, b: (b, g)),
        ],
        out_shape=[
            jax.ShapeDtypeStruct((tokens, groups * width), bf16),
            jax.ShapeDtypeStruct((blocks, groups * heads, HD, HD), f32),
            jax.ShapeDtypeStruct((tokens, groups * width), f32),
        ],
        scratch_shapes=[pltpu.VMEM((heads, HD, HD), f32)],
        compiler_params=pltpu.CompilerParams(vmem_limit_bytes=48 << 20),
        name="mixer_forward",
    )(proj, gap, gain)


def mixer_backward(proj, gap, gain, states, mixed, grad, heads):
    tokens, total = proj.shape
    groups, blocks = total // (4 * heads * HD), tokens // BLK
    width = heads * HD
    return pl.pallas_call(
        functools.partial(backward_kernel, heads),
        grid=(groups, blocks),
        in_specs=[
            pl.BlockSpec((BLK, 4 * width), lambda g, b: (blocks - 1 - b, g)),
            pl.BlockSpec((1, width), lambda g, b: (0, g)),
            pl.BlockSpec((1, HD), lambda g, b: (0, 0)),
            pl.BlockSpec((1, heads, HD, HD), lambda g, b: (blocks - 1 - b, g, 0, 0)),
            pl.BlockSpec((BLK, width), lambda g, b: (blocks - 1 - b, g)),
            pl.BlockSpec((BLK, width), lambda g, b: (blocks - 1 - b, g)),
        ],
        out_specs=[
            pl.BlockSpec((BLK, 4 * width), lambda g, b: (blocks - 1 - b, g)),
            pl.BlockSpec((1, width), lambda g, b: (0, g)),
            pl.BlockSpec((1, 1, HD), lambda g, b: (g, 0, 0)),
        ],
        out_shape=[
            jax.ShapeDtypeStruct((tokens, total), bf16),
            jax.ShapeDtypeStruct((1, groups * width), f32),
            jax.ShapeDtypeStruct((groups, 1, HD), f32),
        ],
        scratch_shapes=[pltpu.VMEM((heads, HD, HD), f32), pltpu.VMEM((heads, HD, HD), f32)],
        compiler_params=pltpu.CompilerParams(vmem_limit_bytes=48 << 20),
        name="mixer_backward",
    )(proj, gap, gain, states, mixed, grad)


def swap(value):
    return lax.ppermute(value, "seq", [(0, 1), (1, 0)])


def in_order(own, other, axis):
    first = lax.axis_index("seq") == 0
    return jnp.concatenate([jnp.where(first, own, other), jnp.where(first, other, own)], axis=axis)


def gather_tokens(value):
    if lax.axis_size("seq") != 2:
        return lax.all_gather(value, "seq", axis=0, tiled=True)
    return in_order(value, swap(value), 0)


def scatter_tokens(partial):
    if lax.axis_size("seq") != 2:
        return lax.psum_scatter(partial.astype(bf16), "seq", scatter_dimension=0, tiled=True).astype(f32)
    rows = partial.shape[0] // 2
    me = lax.axis_index("seq")
    theirs = lax.dynamic_slice_in_dim(partial, (1 - me) * rows, rows, 0).astype(bf16)
    return lax.dynamic_slice_in_dim(partial, me * rows, rows, 0) + swap(theirs).astype(f32)


def columns_to_tokens(value):
    if lax.axis_size("seq") != 2:
        return lax.all_to_all(value, "seq", 0, 1, tiled=True)
    rows = value.shape[0] // 2
    me = lax.axis_index("seq")
    theirs = swap(lax.dynamic_slice_in_dim(value, (1 - me) * rows, rows, 0))
    return in_order(lax.dynamic_slice_in_dim(value, me * rows, rows, 0), theirs, 1)


def tokens_to_columns(value):
    if lax.axis_size("seq") != 2:
        return lax.all_to_all(value, "seq", 1, 0, tiled=True)
    cols = value.shape[1] // 2
    me = lax.axis_index("seq")
    theirs = swap(lax.dynamic_slice_in_dim(value, (1 - me) * cols, cols, 1))
    return in_order(lax.dynamic_slice_in_dim(value, me * cols, cols, 1), theirs, 0)


RING = 8
CHUNK = 256


def reduce_kernel(counts, *refs):
    kinds = len(counts)
    lefts, rights = refs[:kinds], refs[kinds : 2 * kinds]
    (
        small_ref,
        out_ref,
        small_out,
        core_out,
        core_in,
        pair_out,
        pair_in,
        sums,
        line_in,
        done,
        core_sems,
        pair_sems,
        line_send,
        line_recv,
        done_sems,
        small_in,
        small_sems,
    ) = refs[2 * kinds :]
    total = sum(counts)
    planes, rows = sums.shape[1:3]
    seq = lax.axis_index("seq")
    shard = lax.axis_index("shard")
    plane = lax.axis_index("rep")
    core, pair = shard % 2, shard // 2
    other_core = {"shard": shard + 1 - 2 * core}
    other_pair = {"shard": (shard + 2) % 4}
    other_seq = {"seq": 1 - seq}
    below, above = {"rep": plane - 1}, {"rep": plane + 1}
    me = shard * planes + plane
    owners = small_ref.shape[0]
    devices = small_in.shape[0]
    number = seq * owners + me

    def others():
        for step in range(1, devices):
            there = (number + step) % devices
            owner = there % owners
            yield step, owner, {"seq": there // owners, "shard": owner // planes, "rep": owner % planes}

    barrier = pltpu.get_barrier_semaphore()
    for _, _, device in others():
        pl.semaphore_signal(barrier, inc=1, device_id=device, device_id_type=MESH)
    pl.semaphore_wait(barrier, devices - 1)

    def remote(source, target, send, recv, device):
        return pltpu.make_async_remote_copy(
            src_ref=source, dst_ref=target, send_sem=send, recv_sem=recv, device_id=device, device_id_type=MESH
        )

    small_copies = [
        remote(small_ref.at[owner], small_in.at[number], small_sems.at[0, step], small_sems.at[1, step], device)
        for step, owner, device in others()
    ]
    for copy in small_copies:
        copy.start()

    def core_copy(slot):
        return remote(
            core_out.at[slot], core_in.at[slot], core_sems.at[0, slot], core_sems.at[1, slot], other_core
        )

    def pair_copy(slot):
        return remote(
            pair_out.at[slot], pair_in.at[slot], pair_sems.at[0, slot], pair_sems.at[1, slot], other_pair
        )

    def line_copy(way, step, slot, target):
        return remote(
            sums.at[slot, target],
            line_in.at[way, step - 1, slot],
            line_send.at[way, step - 1, slot],
            line_recv.at[way, step - 1, slot],
            above if way else below,
        )

    def done_copies(chunk):
        slot = chunk % RING
        place = out_ref.at[seq, :, pl.ds(pl.multiple_of(chunk * CHUNK, CHUNK), CHUNK)]
        kept = pltpu.make_async_copy(done.at[slot], place, done_sems.at[2, slot])
        sent = remote(done.at[slot], place, done_sems.at[0, slot], done_sems.at[1, slot], other_seq)
        return kept, sent

    def product(kind, chunk, half, which):
        first = (half * 2 + which) * planes * rows
        left = lefts[kind][pl.ds(pl.multiple_of(first, planes * rows), planes * rows), :]
        start = (chunk - sum(counts[:kind])) * CHUNK
        return matmul(left, rights[kind][:, pl.ds(pl.multiple_of(start, CHUNK), CHUNK)])

    def line_target(way, step):
        return plane + planes - step if way else plane - planes + step

    def sends(way, step):
        return plane < step if way else plane >= planes - step

    def receives(way, step):
        return jnp.logical_and(plane > 0, plane <= step) if way else jnp.logical_and(plane < planes - 1, plane >= planes - step - 1)

    def front(kind, chunk):
        slot = chunk % RING

        @pl.when(chunk >= RING)
        def _():
            core_copy(slot).wait_send()

        for half in range(2):
            core_out[slot, half] = product(kind, chunk, half, 1 - core).astype(bf16)
        core_copy(slot).start()

    def middle(kind, chunk):
        slot = chunk % RING

        @pl.when(chunk >= RING)
        def _():
            pair_copy(slot).wait_send()

        theirs = product(kind, chunk, 1 - pair, core)
        mine = product(kind, chunk, pair, core)
        core_copy(slot).wait_recv()
        pair_out[slot] = (theirs + core_in[slot, 1 - pair].astype(f32)).astype(bf16)
        pair_copy(slot).start()
        mine = mine + core_in[slot, pair].astype(f32)
        sums[slot] = mine.astype(bf16).reshape(planes, rows, CHUNK)

    def line_start(chunk, step):
        slot = chunk % RING
        for way in range(2):

            @pl.when(sends(way, step))
            def _(way=way):
                target = line_target(way, step)
                if step > 1:

                    @pl.when(receives(way, step - 1))
                    def _():
                        line_copy(way, step - 1, slot, 0).wait_recv()
                        got = line_in[way, step - 2, slot].astype(f32)
                        sums[slot, target] = (sums[slot, target].astype(f32) + got).astype(bf16)

                line_copy(way, step, slot, target).start()

    def pair_done(chunk):
        slot = chunk % RING
        pair_copy(slot).wait_recv()
        got = pair_in[slot].reshape(planes, rows, CHUNK).astype(f32)
        sums[slot] = (sums[slot].astype(f32) + got).astype(bf16)
        line_start(chunk, 1)

    def finish(chunk):
        slot = chunk % RING
        kept, sent = done_copies(chunk)

        @pl.when(chunk >= RING)
        def _():
            kept.wait()
            sent.wait_send()

        last = planes - 1
        for way in range(2):

            @pl.when(receives(way, last))
            def _(way=way):
                line_copy(way, last, slot, 0).wait_recv()
                got = line_in[way, last - 1, slot].astype(f32)
                sums[slot, plane] = (sums[slot, plane].astype(f32) + got).astype(bf16)

        done[slot] = sums[slot, plane]
        kept.start()
        sent.start()
        for way in range(2):
            for step in range(1, planes):

                @pl.when(sends(way, step))
                def _(way=way, step=step):
                    line_copy(way, step, slot, 0).wait_send()

    def received(chunk):
        done_copies(chunk)[1].wait_recv()

    later = [(pair_done, 3)] + [
        (functools.partial(line_start, step=step), 2 + step) for step in range(2, planes)
    ] + [(finish, 2 + planes), (received, 4 + planes)]
    first = 0
    for kind, count in enumerate(counts):

        def step(turn, _, kind=kind, first=first):
            front(kind, turn)
            if kind == 0:
                pl.when(turn >= 1)(lambda: middle(0, turn - 1))
            else:
                pl.when(turn == first)(lambda: middle(kind - 1, turn - 1))
                pl.when(turn > first)(lambda: middle(kind, turn - 1))
            for act, lag in later:
                pl.when(turn >= lag)(lambda act=act, lag=lag: act(turn - lag))
            return 0

        lax.fori_loop(first, first + count, step, 0)
        first += count

    def drain(turn, _):
        pl.when(turn == total)(lambda: middle(kinds - 1, turn - 1))
        for act, lag in later:
            pl.when(turn - lag < total)(lambda act=act, lag=lag: act(turn - lag))
        return 0

    lax.fori_loop(total, total + later[-1][1], drain, 0)
    for chunk in range(total - RING, total):
        slot = chunk % RING
        core_copy(slot).wait_send()
        pair_copy(slot).wait_send()
        kept, sent = done_copies(chunk)
        kept.wait()
        sent.wait_send()
    small_in[number] = small_ref[me]
    for copy in small_copies:
        copy.wait()
    small_out[...] = jnp.sum(small_in[...], axis=0)


def reduced_gradients(lefts, rights, small):
    counts = [right.shape[1] // CHUNK for right in rights]
    planes = lax.axis_size("rep")
    rows = lefts[0].shape[0] // lax.axis_size(SR)
    block = planes * rows
    devices = lax.axis_size(("seq",) + SR)
    vmem = pl.BlockSpec(memory_space=pltpu.VMEM)
    return pl.pallas_call(
        functools.partial(reduce_kernel, counts),
        in_specs=[vmem] * (2 * len(lefts) + 1),
        out_specs=[pl.BlockSpec(memory_space=pl.ANY), vmem],
        out_shape=[
            jax.ShapeDtypeStruct((2, rows, sum(counts) * CHUNK), bf16),
            jax.ShapeDtypeStruct(small.shape[1:], f32),
        ],
        scratch_shapes=[
            pltpu.VMEM((RING, 2, block, CHUNK), bf16),
            pltpu.VMEM((RING, 2, block, CHUNK), bf16),
            pltpu.VMEM((RING, block, CHUNK), bf16),
            pltpu.VMEM((RING, block, CHUNK), bf16),
            pltpu.VMEM((RING, planes, rows, CHUNK), bf16),
            pltpu.VMEM((2, planes - 1, RING, rows, CHUNK), bf16),
            pltpu.VMEM((RING, rows, CHUNK), bf16),
            pltpu.SemaphoreType.DMA((2, RING)),
            pltpu.SemaphoreType.DMA((2, RING)),
            pltpu.SemaphoreType.DMA((2, planes - 1, RING)),
            pltpu.SemaphoreType.DMA((2, planes - 1, RING)),
            pltpu.SemaphoreType.DMA((3, RING)),
            pltpu.VMEM((devices,) + small.shape[1:], f32),
            pltpu.SemaphoreType.DMA((2, devices)),
        ],
        compiler_params=pltpu.CompilerParams(
            collective_id=0, has_side_effects=True, vmem_limit_bytes=56 << 20
        ),
        name="reduced_gradients",
    )(*lefts, *rights, small)


def gather_kernel(
    tokens_ref,
    gains_ref,
    w_query,
    w_forget,
    w_input,
    w_gate_out,
    w_output,
    proj_ref,
    normed_ref,
    mix_ref,
    out_ref,
    all_gains_ref,
    pieces,
    all_tokens,
    normed,
    all_gains,
    products,
    load_sems,
    token_sems,
    gain_sems,
    line_send,
    line_recv,
    pair_sems,
    core_sems,
    write_sems,
    last_sems,
):
    total, owners, rows = pieces.shape[:3]
    seqs, own_tokens, width = all_tokens.shape
    local_width = width // seqs
    mix_count = 4 * local_width // CHUNK
    group_width = mix_ref.shape[2] // 4 // (local_width // (4 * HD))
    planes = lax.axis_size("rep")
    seq = lax.axis_index("seq")
    shard = lax.axis_index("shard")
    plane = lax.axis_index("rep")
    core, pair = shard % 2, shard // 2
    me = shard * planes + plane
    other_core = {"shard": shard + 1 - 2 * core}
    other_pair = {"shard": (shard + 2) % 4}
    other_seq = {"seq": 1 - seq}
    below, above = {"rep": plane - 1}, {"rep": plane + 1}

    loads = []
    per_group = group_width // CHUNK
    for chunk in range(total):
        if chunk < mix_count:
            group, rest = divmod(chunk, 4 * per_group)
            kind, part = divmod(rest, per_group)
            source = (w_query, w_forget, w_input, w_gate_out)[kind]
            start = seq * local_width + group * group_width + part * CHUNK
        else:
            source, start = w_output, (chunk - mix_count) * CHUNK
        start = start if isinstance(start, int) else pl.multiple_of(start, CHUNK)
        loads.append(
            pltpu.make_async_copy(source.at[:, pl.ds(start, CHUNK)], pieces.at[chunk, me], load_sems.at[chunk])
        )
    for load in loads:
        load.start()

    def others():
        for step in range(1, owners):
            number = (me + step) % owners
            yield step, {"shard": number // planes, "rep": number % planes}

    barrier = pltpu.get_barrier_semaphore()
    for _, device in others():
        pl.semaphore_signal(barrier, inc=1, device_id=device, device_id_type=MESH)
    pl.semaphore_signal(barrier, inc=1, device_id=other_seq, device_id_type=MESH)
    pl.semaphore_wait(barrier, owners)

    def remote(source, target, send, recv, device):
        return pltpu.make_async_remote_copy(
            src_ref=source, dst_ref=target, send_sem=send, recv_sem=recv, device_id=device, device_id_type=MESH
        )

    token_copy = remote(tokens_ref, all_tokens.at[seq], token_sems.at[0], token_sems.at[1], other_seq)
    token_copy.start()
    gain_copies = [
        remote(gains_ref, all_gains.at[me], gain_sems.at[0, step], gain_sems.at[1, step], device)
        for step, device in others()
    ]
    for copy in gain_copies:
        copy.start()

    def line_copy(way, step, chunk, owner):
        slot = chunk % RING
        return remote(
            pieces.at[chunk, owner],
            pieces.at[chunk, owner],
            line_send.at[way, step - 1, slot],
            line_recv.at[way, step - 1, slot],
            above if way else below,
        )

    def block(which_pair):
        return pl.ds((which_pair * 2 + core) * planes, planes)

    def pair_copy(chunk):
        slot = chunk % RING
        place = pieces.at[chunk, block(pair)]
        return remote(place, place, pair_sems.at[0, slot], pair_sems.at[1, slot], other_pair)

    def core_copy(chunk, which):
        slot = chunk % RING
        place = pieces.at[chunk, block(pair if which == 0 else 1 - pair)]
        return remote(place, place, core_sems.at[0, which, slot], core_sems.at[1, which, slot], other_core)

    def sends(way, step):
        if way:
            return jnp.logical_and(plane < planes - 1, plane - (step - 1) >= 0)
        return jnp.logical_and(plane > 0, plane + (step - 1) <= planes - 1)

    def receives(way, step):
        return plane - step >= 0 if way else plane + step <= planes - 1

    def line(chunk, step):
        for way in range(2):
            if step > 1:

                @pl.when(receives(way, step - 1))
                def _(way=way):
                    line_copy(way, step - 1, chunk, me).wait_recv()

            if step < planes:

                @pl.when(sends(way, step))
                def _(way=way):
                    line_copy(way, step, chunk, me - (step - 1) if way else me + (step - 1)).start()

    def first(chunk):
        slot = chunk
        pltpu.make_async_copy(pieces.at[chunk, me], pieces.at[chunk, me], load_sems.at[slot]).wait()
        line(chunk, 1)

    def across(chunk):
        line(chunk, planes)
        pair_copy(chunk).start()
        core_copy(chunk, 0).start()

    def to_core(chunk):
        pair_copy(chunk).wait_recv()
        core_copy(chunk, 1).start()

    def writes(chunk):
        slot = chunk % RING

        def mix_writes():
            span = pl.ds(pl.multiple_of(chunk * CHUNK, CHUNK), CHUNK)
            return (
                pltpu.make_async_copy(pieces.at[chunk], mix_ref.at[:, :, span], write_sems.at[0, slot]),
                pltpu.make_async_copy(products.at[slot], proj_ref.at[:, span], write_sems.at[1, slot]),
            )

        def out_writes():
            span = pl.ds(pl.multiple_of((chunk - mix_count) * CHUNK, CHUNK), CHUNK)
            return (pltpu.make_async_copy(pieces.at[chunk], out_ref.at[:, :, span], write_sems.at[0, slot]),)

        return mix_writes, out_writes

    def finish(chunk):
        slot = chunk % RING
        core_copy(chunk, 0).wait_recv()
        core_copy(chunk, 1).wait_recv()
        mix_writes, out_writes = writes(chunk)

        @pl.when(chunk >= RING)
        def _():
            written(chunk - RING)

        @pl.when(chunk < mix_count)
        def _():
            weight = pieces[chunk].reshape(owners * rows, CHUNK)
            for half in range(seqs):
                products[slot, half * own_tokens : (half + 1) * own_tokens] = matmul(normed[half], weight)
            for copy in mix_writes():
                copy.start()

        @pl.when(chunk >= mix_count)
        def _():
            for copy in out_writes():
                copy.start()

        pair_copy(chunk).wait_send()
        core_copy(chunk, 0).wait_send()
        core_copy(chunk, 1).wait_send()
        for way in range(2):
            for step in range(1, planes):

                @pl.when(sends(way, step))
                def _(way=way, step=step):
                    line_copy(way, step, chunk, me).wait_send()

    def written(chunk):
        mix_writes, out_writes = writes(chunk)

        @pl.when(chunk < mix_count)
        def _():
            for copy in mix_writes():
                copy.wait()

        @pl.when(chunk >= mix_count)
        def _():
            for copy in out_writes():
                copy.wait()

    def normalize():
        all_tokens[seq] = tokens_ref[...]
        all_gains[me] = gains_ref[...]
        token_copy.wait_recv()
        for copy in gain_copies:
            copy.wait_recv()
        gain = jnp.concatenate([all_gains[owner, 0:1, :] for owner in range(owners)], axis=1)
        size = 64
        per = own_tokens // size

        def part(index, _):
            span = pl.ds((index % per) * size, size)
            values = all_tokens[index // per, span].astype(f32)
            scale = lax.rsqrt(jnp.mean(values * values, axis=-1, keepdims=True) + norm_eps)
            normed[index // per, span] = (values * scale * gain).astype(bf16)
            return 0

        lax.fori_loop(0, seqs * per, part, 0)
        pltpu.make_async_copy(normed, normed_ref, last_sems.at[0]).start()
        pltpu.make_async_copy(all_gains, all_gains_ref, last_sems.at[1]).start()

    acts = [(first, 0)] + [(functools.partial(line, step=step), step - 1) for step in range(2, planes)]
    acts += [(across, planes - 1), (to_core, planes + 1), (finish, planes + 2)]
    last_lag = acts[-1][1]

    def turn_over(turn, _):
        pl.when(turn == last_lag - 1)(normalize)
        for act, lag in acts:
            inside = jnp.logical_and(turn >= lag, turn - lag < total)
            pl.when(inside)(lambda act=act, lag=lag: act(turn - lag))
        return 0

    lax.fori_loop(0, total + last_lag, turn_over, 0)

    def end(chunk, _):
        written(chunk)
        return 0

    lax.fori_loop(total - RING, total, end, 0)
    token_copy.wait_send()
    for copy in gain_copies:
        copy.wait_send()
    pltpu.make_async_copy(normed, normed_ref, last_sems.at[0]).wait()
    pltpu.make_async_copy(all_gains, all_gains_ref, last_sems.at[1]).wait()


def gathered_mixer(tokens, gains, weights):
    own_tokens, width = tokens.shape
    rows = weights[0].shape[0]
    seqs, planes = lax.axis_size("seq"), lax.axis_size("rep")
    owners = lax.axis_size(SR)
    local_width = width // seqs
    total = (4 * local_width + width) // CHUNK
    vmem = pl.BlockSpec(memory_space=pltpu.VMEM)
    anywhere = pl.BlockSpec(memory_space=pl.ANY)
    proj, normed, mix, out, all_gains = pl.pallas_call(
        gather_kernel,
        in_specs=[vmem, vmem] + [anywhere] * 5,
        out_specs=[anywhere] * 5,
        out_shape=[
            jax.ShapeDtypeStruct((seqs * own_tokens, 4 * local_width), f32),
            jax.ShapeDtypeStruct((seqs, own_tokens, width), bf16),
            jax.ShapeDtypeStruct((owners, rows, 4 * local_width), bf16),
            jax.ShapeDtypeStruct((owners, rows, width), bf16),
            jax.ShapeDtypeStruct((owners,) + gains.shape, f32),
        ],
        scratch_shapes=[
            pltpu.VMEM((total, owners, rows, CHUNK), bf16),
            pltpu.VMEM((seqs, own_tokens, width), bf16),
            pltpu.VMEM((seqs, own_tokens, width), bf16),
            pltpu.VMEM((owners,) + gains.shape, f32),
            pltpu.VMEM((RING, seqs * own_tokens, CHUNK), f32),
            pltpu.SemaphoreType.DMA((total,)),
            pltpu.SemaphoreType.DMA((2,)),
            pltpu.SemaphoreType.DMA((2, owners)),
            pltpu.SemaphoreType.DMA((2, planes - 1, RING)),
            pltpu.SemaphoreType.DMA((2, planes - 1, RING)),
            pltpu.SemaphoreType.DMA((2, RING)),
            pltpu.SemaphoreType.DMA((2, 2, RING)),
            pltpu.SemaphoreType.DMA((2, RING)),
            pltpu.SemaphoreType.DMA((2,)),
        ],
        compiler_params=pltpu.CompilerParams(collective_id=1, has_side_effects=True, vmem_limit_bytes=56 << 20),
        name="gathered_mixer",
    )(tokens, gains, *weights)
    normed = normed.reshape(seqs * own_tokens, width)
    return proj, normed, mix.reshape(width, 4 * local_width), out.reshape(width, width), all_gains


def layout_kernel(owners, part, group_width, reduced_ref, down_ref, *outs):
    seqs = reduced_ref.shape[0]
    gate_ref, up_ref, out_ref, down_out = outs[0], outs[1], outs[2], outs[3]
    mix_outs = outs[4:]
    local_ff = owners * part
    local_width = out_ref.shape[1] // seqs
    for seq in range(seqs):
        start = 0
        for unit_ref in (gate_ref, up_ref):
            for owner in range(owners):
                place = (owner * seqs + seq) * part
                unit_ref[:, place : place + part] = reduced_ref[seq, :, start : start + part].astype(f32)
                start += part
        out_ref[:, seq * local_width : (seq + 1) * local_width] = reduced_ref[
            seq, :, start : start + local_width
        ].astype(f32)
        start += local_width
        for group in range(local_width // group_width):
            for mix_ref in mix_outs:
                place = seq * local_width + group * group_width
                mix_ref[:, place : place + group_width] = reduced_ref[seq, :, start : start + group_width].astype(f32)
                start += group_width
    down_out[...] = down_ref[...].astype(f32)


def laid_out(reduced, down, group_width):
    seqs, share, total = reduced.shape
    owners = lax.axis_size(SR)
    down_rows, width = down.shape
    part = down_rows // seqs
    steps = 4
    row_block, down_block = share // steps, down_rows // steps

    def rows_of(size, columns):
        return pl.BlockSpec((size, columns), lambda i: (i, 0))

    shapes = [(share, owners * down_rows)] * 2 + [(share, width), (down_rows, width)] + [(share, width)] * 4
    blocks = [row_block] * 3 + [down_block] + [row_block] * 4
    return pl.pallas_call(
        functools.partial(layout_kernel, owners, part, group_width),
        grid=(steps,),
        in_specs=[
            pl.BlockSpec((seqs, row_block, total), lambda i: (0, i, 0)),
            rows_of(down_block, width),
        ],
        out_specs=[rows_of(block, shape[1]) for block, shape in zip(blocks, shapes)],
        out_shape=[jax.ShapeDtypeStruct(shape, f32) for shape in shapes],
        compiler_params=pltpu.CompilerParams(vmem_limit_bytes=48 << 20),
        name="laid_out",
    )(reduced, down)


def share_columns(share):
    if lax.axis_size("seq") != 2:
        return lax.all_gather(share, "seq", axis=0)
    return in_order(share[None], swap(share)[None], 0)


def body(
    tokens,
    lengths,
    w_query,
    w_forget,
    w_input,
    w_gate_out,
    w_output,
    w_ffn_gate,
    w_ffn_up,
    w_ffn_down,
    norm_in,
    norm_mid,
    head_gain,
    gate_gap,
    cotangent,
):
    row_count, width = tokens.shape[1:]
    seqs = lax.axis_size("seq")
    owners = lax.axis_size(SR)
    seq_index = lax.axis_index("seq")
    owner_index = lax.axis_index(SR)
    share = w_query.shape[0]
    local_width = width // seqs
    local_heads = H // seqs
    group = min(4, local_heads)
    groups = local_heads // group
    down_rows = w_ffn_down.shape[0]
    part = down_rows // seqs
    local_ff = owners * part

    inputs = tokens[0].astype(f32)
    positions = seq_index * row_count + jnp.arange(row_count)
    valid_col = (positions < lengths[0]).astype(f32)[:, None]

    def gathered(value):
        return lax.all_gather(value, SR, axis=0, tiled=True)

    def owned(value):
        return lax.psum_scatter(value, SR, scatter_dimension=0, tiled=True)

    def my_columns(weight):
        return lax.dynamic_slice_in_dim(weight, seq_index * local_width, local_width, 1)

    def my_units(weight):
        shaped = weight.reshape(share, owners, seqs, part)
        return lax.dynamic_index_in_dim(shaped, seq_index, 2, keepdims=False).reshape(share, local_ff)

    gains = jnp.stack([norm_in, norm_mid, gate_gap, jnp.pad(head_gain, (0, share - head_gain.shape[0]))])
    gains = jnp.pad(gains.astype(f32), ((0, 4), (0, 0)))
    mix_weights = (w_query, w_forget, w_input, w_gate_out)
    fast = seqs == 2 and lax.axis_size("shard") == 4
    if fast:
        proj, normed, w_mix, w_out, gains = gathered_mixer(tokens[0], gains, mix_weights + (w_output,))
    else:
        gains = gathered(gains).reshape(owners, 8, share)
    gain_in = gains[:, 0].reshape(1, width)
    gain_mid = gains[:, 1].reshape(1, width)
    gap_full = gains[:, 2].reshape(1, width)
    gain_head = gains[:, 3, : head_gain.shape[0]].reshape(1, HD)
    gap = lax.dynamic_slice_in_dim(gap_full, seq_index * local_width, local_width, 1)
    scale_in = lax.rsqrt(jnp.mean(inputs * inputs, axis=-1, keepdims=True) + norm_eps)
    unit_in = inputs * scale_in
    if not fast:
        mix_share = jnp.stack([my_columns(w) for w in mix_weights], axis=1)
        mix_share = mix_share.reshape(share, 4, groups, group * HD).transpose(0, 2, 1, 3)
        w_mix = gathered(mix_share.reshape(share, 4 * local_width))
        w_out = gathered(w_output)
        normed = gather_tokens((unit_in * gain_in).astype(bf16))
        proj = matmul(normed, w_mix)

    w_gate_up = gathered(jnp.concatenate([my_units(w_ffn_gate), my_units(w_ffn_up)], axis=1))
    w_down = gathered(lax.dynamic_slice_in_dim(w_ffn_down, seq_index * part, part, 0))

    grad_out = cotangent[0].astype(f32)
    grad_ffn = gather_tokens((valid_col * grad_out).astype(bf16))
    branch_heads, states, mixed = mixer_forward(proj, gap, gain_head, group)
    branch_in = columns_to_tokens(branch_heads)
    hidden = inputs + valid_col * matmul(branch_in, w_out)

    scale_mid = lax.rsqrt(jnp.mean(hidden * hidden, axis=-1, keepdims=True) + norm_eps)
    unit_mid = hidden * scale_mid
    normed_mid = gather_tokens((unit_mid * gain_mid).astype(bf16))
    gate_up = matmul(normed_mid, w_gate_up)
    gate_vals = gate_up[:, :local_ff]
    up_vals = gate_up[:, local_ff:]
    gate_act = jax.nn.silu(gate_vals)
    inner = (gate_act * up_vals).astype(bf16)
    ffn_out = scatter_tokens(matmul(inner, w_down))
    layer_out = (hidden + valid_col * ffn_out).astype(bf16)[None]

    grad_inner = matmul_nt(grad_ffn, w_down)
    down_share = owned(matmul_tn(inner, grad_ffn).astype(bf16))
    grad_gate_vals = (grad_inner * up_vals * dsilu(gate_vals)).astype(bf16)
    grad_up_vals = (grad_inner * gate_act).astype(bf16)
    grad_gate_up = jnp.concatenate([grad_gate_vals, grad_up_vals], axis=1)
    grad_normed_mid = scatter_tokens(matmul_nt(grad_gate_up, w_gate_up))
    grad_gain_mid = jnp.sum(grad_normed_mid * unit_mid, axis=0)
    grad_unit_mid = grad_normed_mid * gain_mid
    grad_hidden = grad_out + scale_mid * (
        grad_unit_mid - unit_mid * jnp.mean(grad_unit_mid * unit_mid, axis=-1, keepdims=True)
    )

    grad_branch = (valid_col * grad_hidden).astype(bf16)
    grad_branch_in = tokens_to_columns(matmul_nt(grad_branch, w_out).astype(bf16))
    grad_proj, grad_gap, grad_gain_head = mixer_backward(proj, gap, gain_head, states, mixed, grad_branch_in, group)
    grad_normed = scatter_tokens(matmul_nt(grad_proj, w_mix))
    grad_gain_in = jnp.sum(grad_normed * unit_in, axis=0)
    grad_unit_in = grad_normed * gain_in
    grad_inputs = grad_hidden + scale_in * (
        grad_unit_in - unit_in * jnp.mean(grad_unit_in * unit_in, axis=-1, keepdims=True)
    )
    input_grad = grad_inputs.astype(bf16)[None]

    lefts = [value.T for value in (normed_mid, gather_tokens(branch_in), normed)]
    rights = [grad_gate_up, tokens_to_columns(grad_branch), grad_proj]
    gap_placed = lax.dynamic_update_slice_in_dim(
        jnp.zeros((width,), f32), grad_gap.reshape(local_width), seq_index * local_width, 0
    )
    head_total = jnp.sum(grad_gain_head, axis=(0, 1))
    small = [row.reshape(owners, share) for row in (grad_gain_in, grad_gain_mid, gap_placed)]
    small.append(jnp.pad(head_total.reshape(owners, -1), ((0, 0), (0, share - HD // owners))))
    small = jnp.pad(jnp.stack(small, axis=1), ((0, 0), (0, 4), (0, 0)))
    if fast:
        reduced, small = reduced_gradients(lefts, rights, small)
    else:
        partial = jnp.concatenate([matmul(left, right).astype(bf16) for left, right in zip(lefts, rights)], axis=1)
        reduced = lax.all_gather(owned(partial), "seq", axis=0)
        small = lax.dynamic_index_in_dim(lax.psum(small, ("seq",) + SR), owner_index, 0, keepdims=False)
    down_all = share_columns(down_share).reshape(down_rows, width)
    if fast:
        grad_gate, grad_up, grad_output, grad_down, *mix_all = laid_out(reduced, down_all, group * HD)
    else:
        reduced = reduced.astype(f32)
        ends = (2 * local_ff, 2 * local_ff + local_width)
        grad_units = reduced[:, :, : ends[0]].reshape(seqs, share, 2, owners, part).transpose(2, 1, 3, 0, 4)
        grad_gate, grad_up = grad_units.reshape(2, share, owners * down_rows)
        grad_output = reduced[:, :, ends[0] : ends[1]].transpose(1, 0, 2).reshape(share, width)
        mix_all = reduced[:, :, ends[1] :].reshape(seqs, share, groups, 4, group * HD)
        mix_all = mix_all.transpose(3, 1, 0, 2, 4).reshape(4, share, width)
        grad_down = down_all.astype(f32)

    return (
        layer_out,
        input_grad,
        mix_all[0],
        mix_all[1],
        mix_all[2],
        mix_all[3],
        grad_output,
        grad_gate,
        grad_up,
        grad_down,
        small[0],
        small[1],
        small[3, : HD // owners],
        small[2],
    )


def solution(mesh):
    rows = P(SR, None)
    vector = P(SR)
    by_token = P(SR, "seq", None)
    placed = (by_token, vector) + (rows,) * 8 + (vector,) * 4 + (by_token,)
    return jax.shard_map(
        body,
        mesh=mesh,
        in_specs=placed,
        out_specs=(by_token, by_token) + (rows,) * 8 + (vector,) * 4,
        check_vma=False,
    )
```

```python
import functools

import jax
import jax.numpy as jnp
from jax import lax
from jax.experimental import pallas as pl
from jax.experimental.pallas import tpu as pltpu
from jax.sharding import PartitionSpec as P

H = 16
HD = 128
BLK = 128
SR = ("shard", "rep")
MESH = pl.DeviceIdType.MESH

norm_eps = 1e-05
head_eps = 1e-06

f32 = jnp.float32
bf16 = jnp.bfloat16


def dsilu(values_in):
    sig_vals = jax.nn.sigmoid(values_in)
    return sig_vals * (1.0 + values_in * (1.0 - sig_vals))


def matmul(left, right):
    return jnp.dot(left, right, preferred_element_type=f32)


def matmul_nt(left, right):
    return lax.dot_general(left, right, (((1,), (1,)), ((), ())), preferred_element_type=f32)


def matmul_tn(left, right):
    return lax.dot_general(left, right, (((0,), (0,)), ((), ())), preferred_element_type=f32)


def block_sums(lower, values):
    high, low = split(values)
    return matmul(lower, high) + matmul(lower, low)


def split(values):
    high = values.astype(bf16)
    return high, (values - high.astype(f32)).astype(bf16)


def head_forward(proj, gap, group_width):
    proj_query = proj[:, :group_width]
    proj_forget = proj[:, group_width : 2 * group_width]
    proj_input = proj[:, 2 * group_width : 3 * group_width]
    proj_gate = proj[:, 3 * group_width :]
    sig_query = jax.nn.sigmoid(proj_query)
    queries = (proj_query * sig_query).astype(bf16).astype(f32)
    forget_sig = jax.nn.sigmoid(-proj_forget)
    key_full = gap * forget_sig
    keys = key_full.astype(bf16).astype(f32)
    log_decay = jnp.log1p(-key_full)
    values = proj_input.astype(bf16)
    return proj_query, proj_gate, sig_query, queries, forget_sig, key_full, keys, log_decay, values


def triangle(kind, dtype):
    rows = lax.broadcasted_iota(jnp.int32, (BLK, BLK), 0)
    cols = lax.broadcasted_iota(jnp.int32, (BLK, BLK), 1)
    return (rows >= cols if kind == "lower" else rows <= cols).astype(dtype)


def forward_kernel(heads, proj_ref, gap_ref, gain_ref, branch_ref, states_ref, mixed_ref, state):
    width = heads * HD

    @pl.when(pl.program_id(1) == 0)
    def _():
        state[...] = jnp.zeros_like(state)

    proj = proj_ref[...]
    _, proj_gate, _, queries, _, _, keys, log_decay, values = head_forward(proj, gap_ref[...], width)
    lower = triangle("lower", f32)
    cumul = block_sums(lower.astype(bf16), log_decay)
    grown = jnp.exp(cumul)
    query_dec, query_low = split(queries * grown)
    key_dec, key_low = split(keys * jnp.exp(-cumul))
    last = cumul[BLK - 1 : BLK, :]
    key_tail = (keys * jnp.exp(last - cumul)).astype(bf16)
    last_decay = jnp.exp(last)
    gate_act = proj_gate * jax.nn.sigmoid(proj_gate)
    gain = gain_ref[...]
    for head in range(heads):
        span = slice(head * HD, (head + 1) * HD)
        before = state[head]
        states_ref[0, head] = before
        scores = matmul_nt(query_low[:, span], key_dec[:, span]) + matmul_nt(query_dec[:, span], key_low[:, span])
        scores = (scores + matmul_nt(query_dec[:, span], key_dec[:, span])) * lower
        scores, scores_low = split(scores)
        mixed = matmul(scores_low, values[:, span]) + matmul(scores, values[:, span])
        mixed = mixed + matmul(query_dec[:, span], before.astype(bf16))
        mixed_ref[:, span] = mixed
        decay_col = jnp.transpose(jnp.broadcast_to(last_decay[:, span], (HD, HD)))
        state[head] = decay_col * before + matmul_tn(key_tail[:, span], values[:, span])
        scale = lax.rsqrt(jnp.mean(mixed * mixed, axis=-1, keepdims=True) + head_eps)
        branch_ref[:, span] = (mixed * scale * gain * gate_act[:, span]).astype(bf16)


def backward_block(heads, proj, gap, gain, states, mixed_all, grad_in, dstate, after):
    width = heads * HD
    proj_query, proj_gate, sig_query, queries, forget_sig, key_full, keys, log_decay, values = head_forward(
        proj, gap, width
    )
    lower = triangle("lower", f32)
    upper = triangle("upper", bf16)
    cumul = block_sums(lower.astype(bf16), log_decay)
    grown = jnp.exp(cumul)
    shrunk = jnp.exp(-cumul)
    last = cumul[BLK - 1 : BLK, :]
    tail = jnp.exp(last - cumul)
    last_decay = jnp.exp(last)
    query_dec = (queries * grown).astype(bf16)
    key_dec = (keys * shrunk).astype(bf16)
    key_tail = (keys * tail).astype(bf16)
    sig_gate = jax.nn.sigmoid(proj_gate)
    gate_act = proj_gate * sig_gate
    gate_slope = sig_gate * (1.0 + proj_gate * (1.0 - sig_gate))
    gain_sum = jnp.zeros((1, HD), f32)
    query_grads, key_grads, value_grads, gate_grads, ends = [], [], [], [], []
    for head in range(heads):
        span = slice(head * HD, (head + 1) * HD)
        before = states[head]
        before_low = before.astype(bf16)
        q_dec, k_dec, vals = query_dec[:, span], key_dec[:, span], values[:, span]
        scores = (matmul_nt(q_dec, k_dec) * lower).astype(bf16)
        mixed = mixed_all[:, span]
        scale = lax.rsqrt(jnp.mean(mixed * mixed, axis=-1, keepdims=True) + head_eps)
        unit = mixed * scale
        grad_b = grad_in[:, span]
        gate_grads.append(grad_b * unit * gain * gate_slope[:, span])
        grad_normed = grad_b * gate_act[:, span]
        gain_sum = gain_sum + jnp.sum(grad_normed * unit, axis=0, keepdims=True)
        grad_unit = grad_normed * gain
        grad_mixed = scale * (grad_unit - unit * jnp.mean(grad_unit * unit, axis=-1, keepdims=True))
        grad_low = grad_mixed.astype(bf16)
        down = dstate[head]
        down_low = down.astype(bf16)
        grad_scores = (matmul_nt(grad_low, vals) * lower).astype(bf16)
        value_grads.append(matmul_tn(scores, grad_low) + matmul(key_tail[:, span], down_low))
        grad_q = matmul(grad_scores, k_dec) + matmul_nt(grad_low, before_low)
        grad_k = matmul_tn(grad_scores, q_dec)
        grad_t = matmul_nt(vals, down_low)
        query_grads.append(grad_q * grown[:, span])
        key_grads.append(grad_k * shrunk[:, span] + grad_t * tail[:, span])
        ends.append(jnp.transpose(jnp.sum(down * after[head], axis=1, keepdims=True)))
        after[head] = before
        decay_col = jnp.transpose(jnp.broadcast_to(last_decay[:, span], (HD, HD)))
        dstate[head] = decay_col * down + matmul_tn(q_dec, grad_low)
    grad_queries = jnp.concatenate(query_grads, axis=1)
    grad_keys = jnp.concatenate(key_grads, axis=1)
    grad_values = jnp.concatenate(value_grads, axis=1)
    end = jnp.concatenate(ends, axis=1)
    grad_decay = block_sums(upper, queries * grad_queries - keys * grad_keys) + end
    grad_key_full = grad_keys - grad_decay / (1.0 - key_full)
    gap_sum = jnp.sum(grad_key_full * forget_sig, axis=0, keepdims=True)
    query_slope = sig_query * (1.0 + proj_query * (1.0 - sig_query))
    grads = (
        grad_queries * query_slope,
        -grad_key_full * gap * forget_sig * (1.0 - forget_sig),
        grad_values,
        jnp.concatenate(gate_grads, axis=1),
    )
    return [grad.astype(bf16) for grad in grads], gap_sum, gain_sum


def backward_kernel(
    heads, proj_ref, gap_ref, gain_ref, states_ref, mixed_ref, grad_ref, out_ref, gap_out, gain_out, dstate, after
):
    width = heads * HD

    @pl.when(pl.program_id(1) == 0)
    def _():
        dstate[...] = jnp.zeros_like(dstate)
        after[...] = jnp.zeros_like(after)
        gap_out[...] = jnp.zeros_like(gap_out)
        gain_out[...] = jnp.zeros_like(gain_out)

    states = [states_ref[0, head] for head in range(heads)]
    grads, gap_sum, gain_sum = backward_block(
        heads, proj_ref[...], gap_ref[...], gain_ref[...], states, mixed_ref[...], grad_ref[...].astype(f32), dstate, after
    )
    for kind, grad in enumerate(grads):
        out_ref[:, kind * width : (kind + 1) * width] = grad
    gap_out[...] += gap_sum
    gain_out[...] += gain_sum


def mixer_forward(proj, gap, gain, heads):
    tokens, total = proj.shape
    groups, blocks = total // (4 * heads * HD), tokens // BLK
    width = heads * HD
    return pl.pallas_call(
        functools.partial(forward_kernel, heads),
        grid=(groups, blocks),
        in_specs=[
            pl.BlockSpec((BLK, 4 * width), lambda g, b: (b, g)),
            pl.BlockSpec((1, width), lambda g, b: (0, g)),
            pl.BlockSpec((1, HD), lambda g, b: (0, 0)),
        ],
        out_specs=[
            pl.BlockSpec((BLK, width), lambda g, b: (b, g)),
            pl.BlockSpec((1, heads, HD, HD), lambda g, b: (b, g, 0, 0)),
            pl.BlockSpec((BLK, width), lambda g, b: (b, g)),
        ],
        out_shape=[
            jax.ShapeDtypeStruct((tokens, groups * width), bf16),
            jax.ShapeDtypeStruct((blocks, groups * heads, HD, HD), f32),
            jax.ShapeDtypeStruct((tokens, groups * width), f32),
        ],
        scratch_shapes=[pltpu.VMEM((heads, HD, HD), f32)],
        compiler_params=pltpu.CompilerParams(vmem_limit_bytes=48 << 20),
        name="mixer_forward",
    )(proj, gap, gain)


def mixer_backward(proj, gap, gain, states, mixed, grad, heads):
    tokens, total = proj.shape
    groups, blocks = total // (4 * heads * HD), tokens // BLK
    width = heads * HD
    return pl.pallas_call(
        functools.partial(backward_kernel, heads),
        grid=(groups, blocks),
        in_specs=[
            pl.BlockSpec((BLK, 4 * width), lambda g, b: (blocks - 1 - b, g)),
            pl.BlockSpec((1, width), lambda g, b: (0, g)),
            pl.BlockSpec((1, HD), lambda g, b: (0, 0)),
            pl.BlockSpec((1, heads, HD, HD), lambda g, b: (blocks - 1 - b, g, 0, 0)),
            pl.BlockSpec((BLK, width), lambda g, b: (blocks - 1 - b, g)),
            pl.BlockSpec((BLK, width), lambda g, b: (blocks - 1 - b, g)),
        ],
        out_specs=[
            pl.BlockSpec((BLK, 4 * width), lambda g, b: (blocks - 1 - b, g)),
            pl.BlockSpec((1, width), lambda g, b: (0, g)),
            pl.BlockSpec((1, 1, HD), lambda g, b: (g, 0, 0)),
        ],
        out_shape=[
            jax.ShapeDtypeStruct((tokens, total), bf16),
            jax.ShapeDtypeStruct((1, groups * width), f32),
            jax.ShapeDtypeStruct((groups, 1, HD), f32),
        ],
        scratch_shapes=[pltpu.VMEM((heads, HD, HD), f32), pltpu.VMEM((heads, HD, HD), f32)],
        compiler_params=pltpu.CompilerParams(vmem_limit_bytes=48 << 20),
        name="mixer_backward",
    )(proj, gap, gain, states, mixed, grad)


def swap(value):
    return lax.ppermute(value, "seq", [(0, 1), (1, 0)])


def in_order(own, other, axis):
    first = lax.axis_index("seq") == 0
    return jnp.concatenate([jnp.where(first, own, other), jnp.where(first, other, own)], axis=axis)


def gather_tokens(value):
    if lax.axis_size("seq") != 2:
        return lax.all_gather(value, "seq", axis=0, tiled=True)
    return in_order(value, swap(value), 0)


def scatter_tokens(partial):
    if lax.axis_size("seq") != 2:
        return lax.psum_scatter(partial.astype(bf16), "seq", scatter_dimension=0, tiled=True).astype(f32)
    rows = partial.shape[0] // 2
    me = lax.axis_index("seq")
    theirs = lax.dynamic_slice_in_dim(partial, (1 - me) * rows, rows, 0).astype(bf16)
    return lax.dynamic_slice_in_dim(partial, me * rows, rows, 0) + swap(theirs).astype(f32)


def columns_to_tokens(value):
    if lax.axis_size("seq") != 2:
        return lax.all_to_all(value, "seq", 0, 1, tiled=True)
    rows = value.shape[0] // 2
    me = lax.axis_index("seq")
    theirs = swap(lax.dynamic_slice_in_dim(value, (1 - me) * rows, rows, 0))
    return in_order(lax.dynamic_slice_in_dim(value, me * rows, rows, 0), theirs, 1)


def tokens_to_columns(value):
    if lax.axis_size("seq") != 2:
        return lax.all_to_all(value, "seq", 1, 0, tiled=True)
    cols = value.shape[1] // 2
    me = lax.axis_index("seq")
    theirs = swap(lax.dynamic_slice_in_dim(value, (1 - me) * cols, cols, 1))
    return in_order(lax.dynamic_slice_in_dim(value, me * cols, cols, 1), theirs, 0)


RING = 8
CORE_RING = 4
CHUNK = 256


def reduce_kernel(counts, heads, *refs):
    kinds = len(counts)
    lefts = refs[:kinds]
    (
        units_ref,
        branch_ref,
        proj_ref,
        gap_ref,
        gain_ref,
        states_ref,
        mixed_ref,
        grad_ref,
        mix_ref,
        tokens_ref,
        gain_in_ref,
        hidden_ref,
        small_ref,
        out_ref,
        small_out,
        input_out,
        core_out,
        core_in,
        pair_out,
        pair_in,
        sums,
        line_in,
        done,
        core_sems,
        pair_sems,
        line_send,
        line_recv,
        done_sems,
        small_in,
        small_all,
        small_sems,
        columns,
        column_sems,
        grad_proj,
        proj_in,
        proj_sems,
        dstate,
        after,
        gap_acc,
        gain_acc,
        weights_in,
        weight_sems,
        kept_normed,
        sent_normed,
        got_normed,
        normed_sems,
    ) = refs[kinds:]
    rights = (units_ref, columns, grad_proj)
    total = sum(counts)
    planes, rows = sums.shape[1:3]
    seq = lax.axis_index("seq")
    shard = lax.axis_index("shard")
    plane = lax.axis_index("rep")
    core, pair = shard % 2, shard // 2
    other_core = {"shard": shard + 1 - 2 * core}
    other_pair = {"shard": (shard + 2) % 4}
    other_seq = {"seq": 1 - seq}
    below, above = {"rep": plane - 1}, {"rep": plane + 1}
    me = shard * planes + plane
    owners = small_ref.shape[0]
    devices = small_in.shape[0]
    number = seq * owners + me

    def others():
        for step in range(1, devices):
            there = (number + step) % devices
            owner = there % owners
            yield step, owner, {"seq": there // owners, "shard": owner // planes, "rep": owner % planes}

    barrier = pltpu.get_barrier_semaphore()
    for _, _, device in others():
        pl.semaphore_signal(barrier, inc=1, device_id=device, device_id_type=MESH)
    pl.semaphore_wait(barrier, devices - 1)

    def remote(source, target, send, recv, device):
        return pltpu.make_async_remote_copy(
            src_ref=source, dst_ref=target, send_sem=send, recv_sem=recv, device_id=device, device_id_type=MESH
        )

    own_tokens, width = tokens_ref.shape
    local_width = columns.shape[1]
    group_width = heads * HD
    groups, blocks = local_width // group_width, grad_proj.shape[0] // BLK

    def aligned(start, size):
        return pl.ds(pl.multiple_of(start, size), size)

    def column_moves():
        mine = branch_ref.at[:, aligned(seq * local_width, local_width)]
        theirs = branch_ref.at[:, aligned((1 - seq) * local_width, local_width)]
        place = columns.at[aligned(seq * own_tokens, own_tokens)]
        kept = pltpu.make_async_copy(mine, place, column_sems.at[0])
        return kept, remote(theirs, place, column_sems.at[1], column_sems.at[2], other_seq)

    def proj_load(index):
        group, block = index // blocks, blocks - 1 - index % blocks
        source = proj_ref.at[aligned(block * BLK, BLK), aligned(group * 4 * group_width, 4 * group_width)]
        return pltpu.make_async_copy(source, proj_in.at[index % 2], proj_sems.at[index % 2])

    def mixer_turn(index):
        group, block = index // blocks, blocks - 1 - index % blocks
        rows_at, span = aligned(block * BLK, BLK), aligned(group * group_width, group_width)

        @pl.when(index + 1 < groups * blocks)
        def _():
            proj_load(index + 1).start()

        @pl.when(index % blocks == 0)
        def _():
            dstate[...] = jnp.zeros_like(dstate)
            after[...] = jnp.zeros_like(after)
            gap_acc[:, span] = jnp.zeros((1, group_width), f32)

        proj_load(index).wait()
        states = [states_ref[block, group * heads + head] for head in range(heads)]
        grads, gap_sum, gain_sum = backward_block(
            heads,
            proj_in[index % 2],
            gap_ref[:, span],
            gain_ref[...],
            states,
            mixed_ref[rows_at, span],
            grad_ref[rows_at, span].astype(f32),
            dstate,
            after,
        )
        for kind, grad in enumerate(grads):
            grad_proj[rows_at, aligned((group * 4 + kind) * group_width, group_width)] = grad
        gap_acc[:, span] += gap_sum
        gain_acc[...] += gain_sum

    piece = weights_in.shape[1]
    pieces = width // piece

    def weight_load(index):
        return pltpu.make_async_copy(
            mix_ref.at[aligned(index * piece, piece)], weights_in.at[index % 2], weight_sems.at[index % 2]
        )

    def normed_copy():
        return remote(sent_normed, got_normed, normed_sems.at[0], normed_sems.at[1], other_seq)

    def normed_turn(index):
        @pl.when(index + 1 < pieces)
        def _():
            weight_load(index + 1).start()

        weight_load(index).wait()
        weight = weights_in[index % 2]
        span = aligned(index * piece, piece)
        sent_normed[:, span] = matmul_nt(grad_proj[aligned((1 - seq) * own_tokens, own_tokens)], weight).astype(bf16)
        kept_normed[:, span] = matmul_nt(grad_proj[aligned(seq * own_tokens, own_tokens)], weight)

        @pl.when(index == pieces - 1)
        def _():
            normed_copy().start()

    def input_turn():
        normed_copy().wait()
        gain = gain_in_ref[...]
        size = 64

        def part(index, total_in):
            rows_at = aligned(index * size, size)
            values = tokens_ref[rows_at].astype(f32)
            scale = lax.rsqrt(jnp.mean(values * values, axis=-1, keepdims=True) + norm_eps)
            unit = values * scale
            grad = kept_normed[rows_at] + got_normed[rows_at].astype(f32)
            grad_unit = grad * gain
            moved = scale * (grad_unit - unit * jnp.mean(grad_unit * unit, axis=-1, keepdims=True))
            input_out[rows_at] = (hidden_ref[rows_at] + moved).astype(bf16)
            return total_in + jnp.sum(grad * unit, axis=0, keepdims=True)

        total_in = lax.fori_loop(0, own_tokens // size, part, jnp.zeros((1, width), f32))
        small_all[...] = small_ref[...]
        for owner in range(owners):
            small_all[owner, 0:1, :] = total_in[:, owner * rows : (owner + 1) * rows]
            small_all[owner, 3:4, :] = gain_acc[...]
        first_owner = seq * (local_width // rows)
        for index in range(local_width // rows):
            small_all[first_owner + index, 2:3, :] = gap_acc[:, index * rows : (index + 1) * rows]
        for copy in small_copies:
            copy.start()

    small_copies = [
        remote(small_all.at[owner], small_in.at[number], small_sems.at[0, step], small_sems.at[1, step], device)
        for step, owner, device in others()
    ]
    gain_acc[...] = jnp.zeros_like(gain_acc)
    proj_load(0).start()
    weight_load(0).start()
    column_copies = column_moves()
    for copy in column_copies:
        copy.start()

    def core_copy(chunk):
        slot = chunk % CORE_RING
        return remote(
            core_out.at[slot], core_in.at[slot], core_sems.at[0, slot], core_sems.at[1, slot], other_core
        )

    def pair_copy(slot):
        return remote(
            pair_out.at[slot], pair_in.at[slot], pair_sems.at[0, slot], pair_sems.at[1, slot], other_pair
        )

    def line_copy(way, step, slot, target):
        return remote(
            sums.at[slot, target],
            line_in.at[way, step - 1, slot],
            line_send.at[way, step - 1, slot],
            line_recv.at[way, step - 1, slot],
            above if way else below,
        )

    def done_copies(chunk):
        slot = chunk % RING
        place = out_ref.at[seq, :, pl.ds(pl.multiple_of(chunk * CHUNK, CHUNK), CHUNK)]
        kept = pltpu.make_async_copy(done.at[slot], place, done_sems.at[2, slot])
        sent = remote(done.at[slot], place, done_sems.at[0, slot], done_sems.at[1, slot], other_seq)
        return kept, sent

    def product(kind, chunk, half, which):
        first = (half * 2 + which) * planes * rows
        left = lefts[kind][pl.ds(pl.multiple_of(first, planes * rows), planes * rows), :]
        start = (chunk - sum(counts[:kind])) * CHUNK
        return matmul(left, rights[kind][:, pl.ds(pl.multiple_of(start, CHUNK), CHUNK)])

    def line_target(way, step):
        return plane + planes - step if way else plane - planes + step

    def sends(way, step):
        return plane < step if way else plane >= planes - step

    def receives(way, step):
        return jnp.logical_and(plane > 0, plane <= step) if way else jnp.logical_and(plane < planes - 1, plane >= planes - step - 1)

    def front(kind, chunk):
        slot = chunk % CORE_RING

        @pl.when(chunk >= CORE_RING)
        def _():
            core_copy(chunk).wait_send()

        for half in range(2):
            core_out[slot, half] = product(kind, chunk, half, 1 - core).astype(bf16)
        core_copy(chunk).start()

    def middle(kind, chunk):
        slot, core_slot = chunk % RING, chunk % CORE_RING

        @pl.when(chunk >= RING)
        def _():
            pair_copy(slot).wait_send()

        theirs = product(kind, chunk, 1 - pair, core)
        mine = product(kind, chunk, pair, core)
        core_copy(chunk).wait_recv()
        pair_out[slot] = (theirs + core_in[core_slot, 1 - pair].astype(f32)).astype(bf16)
        pair_copy(slot).start()
        mine = mine + core_in[core_slot, pair].astype(f32)
        sums[slot] = mine.astype(bf16).reshape(planes, rows, CHUNK)

    def line_start(chunk, step):
        slot = chunk % RING
        for way in range(2):

            @pl.when(sends(way, step))
            def _(way=way):
                target = line_target(way, step)
                if step > 1:

                    @pl.when(receives(way, step - 1))
                    def _():
                        line_copy(way, step - 1, slot, 0).wait_recv()
                        got = line_in[way, step - 2, slot].astype(f32)
                        sums[slot, target] = (sums[slot, target].astype(f32) + got).astype(bf16)

                line_copy(way, step, slot, target).start()

    def pair_done(chunk):
        slot = chunk % RING
        pair_copy(slot).wait_recv()
        got = pair_in[slot].reshape(planes, rows, CHUNK).astype(f32)
        sums[slot] = (sums[slot].astype(f32) + got).astype(bf16)
        line_start(chunk, 1)

    def finish(chunk):
        slot = chunk % RING
        kept, sent = done_copies(chunk)

        @pl.when(chunk >= RING)
        def _():
            kept.wait()
            sent.wait_send()

        last = planes - 1
        for way in range(2):

            @pl.when(receives(way, last))
            def _(way=way):
                line_copy(way, last, slot, 0).wait_recv()
                got = line_in[way, last - 1, slot].astype(f32)
                sums[slot, plane] = (sums[slot, plane].astype(f32) + got).astype(bf16)

        done[slot] = sums[slot, plane]
        kept.start()
        sent.start()
        for way in range(2):
            for step in range(1, planes):

                @pl.when(sends(way, step))
                def _(way=way, step=step):
                    line_copy(way, step, slot, 0).wait_send()

    def received(chunk):
        done_copies(chunk)[1].wait_recv()

    later = [(pair_done, 3)] + [
        (functools.partial(line_start, step=step), 2 + step) for step in range(2, planes)
    ] + [(finish, 2 + planes), (received, 4 + planes)]
    first = 0
    for kind, count in enumerate(counts):

        def step(turn, _, kind=kind, first=first):
            front(kind, turn)
            if kind == 0:
                pl.when(turn >= 1)(lambda: middle(0, turn - 1))
            else:
                pl.when(turn == first)(lambda: middle(kind - 1, turn - 1))
                pl.when(turn > first)(lambda: middle(kind, turn - 1))
            if kind == 0:
                steps = groups * blocks
                pl.when(jnp.logical_and(turn >= 1, turn <= steps))(lambda: mixer_turn(turn - 1))
                inside = jnp.logical_and(turn > steps, turn <= steps + pieces)
                pl.when(inside)(lambda: normed_turn(turn - 1 - steps))
            elif kind == 1:
                pl.when(turn == first)(input_turn)
            for act, lag in later:
                pl.when(turn >= lag)(lambda act=act, lag=lag: act(turn - lag))
            return 0

        if kind == 1:
            column_copies[0].wait()
            column_copies[1].wait()
        lax.fori_loop(first, first + count, step, 0)
        first += count

    def drain(turn, _):
        pl.when(turn == total)(lambda: middle(kinds - 1, turn - 1))
        for act, lag in later:
            pl.when(turn - lag < total)(lambda act=act, lag=lag: act(turn - lag))
        return 0

    lax.fori_loop(total, total + later[-1][1], drain, 0)
    for chunk in range(total - RING, total):
        slot = chunk % RING
        if chunk >= total - CORE_RING:
            core_copy(chunk).wait_send()
        pair_copy(slot).wait_send()
        kept, sent = done_copies(chunk)
        kept.wait()
        sent.wait_send()
    small_in[number] = small_all[me]
    for copy in small_copies:
        copy.wait()
    small_out[...] = jnp.sum(small_in[...], axis=0)


def reduced_gradients(lefts, grad_units, grad_branch, mixer, w_mix, tokens, gain_in, grad_hidden, small, heads):
    proj, gap, gain, states, mixed, grad_heads = mixer
    own_tokens, width = tokens.shape
    local_width = grad_heads.shape[1]
    counts = [columns // CHUNK for columns in (grad_units.shape[1], local_width, proj.shape[1])]
    planes = lax.axis_size("rep")
    rows = lefts[0].shape[0] // lax.axis_size(SR)
    block = planes * rows
    devices = lax.axis_size(("seq",) + SR)
    vmem = pl.BlockSpec(memory_space=pltpu.VMEM)
    anywhere = pl.BlockSpec(memory_space=pl.ANY)
    return pl.pallas_call(
        functools.partial(reduce_kernel, counts, heads),
        in_specs=[vmem] * 5 + [anywhere] + [vmem] * 5 + [anywhere] + [vmem] * 4,
        out_specs=[anywhere, vmem, vmem],
        out_shape=[
            jax.ShapeDtypeStruct((2, rows, sum(counts) * CHUNK), bf16),
            jax.ShapeDtypeStruct(small.shape[1:], f32),
            jax.ShapeDtypeStruct((own_tokens, width), bf16),
        ],
        scratch_shapes=[
            pltpu.VMEM((CORE_RING, 2, block, CHUNK), bf16),
            pltpu.VMEM((CORE_RING, 2, block, CHUNK), bf16),
            pltpu.VMEM((RING, block, CHUNK), bf16),
            pltpu.VMEM((RING, block, CHUNK), bf16),
            pltpu.VMEM((RING, planes, rows, CHUNK), bf16),
            pltpu.VMEM((2, planes - 1, RING, rows, CHUNK), bf16),
            pltpu.VMEM((RING, rows, CHUNK), bf16),
            pltpu.SemaphoreType.DMA((2, CORE_RING)),
            pltpu.SemaphoreType.DMA((2, RING)),
            pltpu.SemaphoreType.DMA((2, planes - 1, RING)),
            pltpu.SemaphoreType.DMA((2, planes - 1, RING)),
            pltpu.SemaphoreType.DMA((3, RING)),
            pltpu.VMEM((devices,) + small.shape[1:], f32),
            pltpu.VMEM(small.shape, f32),
            pltpu.SemaphoreType.DMA((2, devices)),
            pltpu.VMEM((2 * own_tokens, local_width), bf16),
            pltpu.SemaphoreType.DMA((3,)),
            pltpu.VMEM(proj.shape, bf16),
            pltpu.VMEM((2, BLK, 4 * heads * HD), f32),
            pltpu.SemaphoreType.DMA((2,)),
            pltpu.VMEM((heads, HD, HD), f32),
            pltpu.VMEM((heads, HD, HD), f32),
            pltpu.VMEM((1, local_width), f32),
            pltpu.VMEM((1, HD), f32),
            pltpu.VMEM((2, CHUNK, proj.shape[1]), bf16),
            pltpu.SemaphoreType.DMA((2,)),
            pltpu.VMEM((own_tokens, width), f32),
            pltpu.VMEM((own_tokens, width), bf16),
            pltpu.VMEM((own_tokens, width), bf16),
            pltpu.SemaphoreType.DMA((2,)),
        ],
        compiler_params=pltpu.CompilerParams(
            collective_id=0, has_side_effects=True, vmem_limit_bytes=62 << 20
        ),
        name="reduced_gradients",
    )(*lefts, grad_units, grad_branch, proj, gap, gain, states, mixed, grad_heads, w_mix, tokens, gain_in, grad_hidden, small)


def gather_kernel(
    tokens_ref,
    gains_ref,
    w_query,
    w_forget,
    w_input,
    w_gate_out,
    w_output,
    proj_ref,
    normed_ref,
    mix_ref,
    out_ref,
    all_gains_ref,
    pieces,
    all_tokens,
    normed,
    all_gains,
    products,
    load_sems,
    token_sems,
    gain_sems,
    line_send,
    line_recv,
    pair_sems,
    core_sems,
    write_sems,
    last_sems,
):
    total, owners, rows = pieces.shape[:3]
    seqs, own_tokens, width = all_tokens.shape
    local_width = width // seqs
    mix_count = 4 * local_width // CHUNK
    group_width = mix_ref.shape[2] // 4 // (local_width // (4 * HD))
    planes = lax.axis_size("rep")
    seq = lax.axis_index("seq")
    shard = lax.axis_index("shard")
    plane = lax.axis_index("rep")
    core, pair = shard % 2, shard // 2
    me = shard * planes + plane
    other_core = {"shard": shard + 1 - 2 * core}
    other_pair = {"shard": (shard + 2) % 4}
    other_seq = {"seq": 1 - seq}
    below, above = {"rep": plane - 1}, {"rep": plane + 1}

    loads = []
    per_group = group_width // CHUNK
    for chunk in range(total):
        if chunk < mix_count:
            group, rest = divmod(chunk, 4 * per_group)
            kind, part = divmod(rest, per_group)
            source = (w_query, w_forget, w_input, w_gate_out)[kind]
            start = seq * local_width + group * group_width + part * CHUNK
        else:
            source, start = w_output, (chunk - mix_count) * CHUNK
        start = start if isinstance(start, int) else pl.multiple_of(start, CHUNK)
        loads.append(
            pltpu.make_async_copy(source.at[:, pl.ds(start, CHUNK)], pieces.at[chunk, me], load_sems.at[chunk])
        )
    for load in loads:
        load.start()

    def others():
        for step in range(1, owners):
            number = (me + step) % owners
            yield step, {"shard": number // planes, "rep": number % planes}

    barrier = pltpu.get_barrier_semaphore()
    for _, device in others():
        pl.semaphore_signal(barrier, inc=1, device_id=device, device_id_type=MESH)
    pl.semaphore_signal(barrier, inc=1, device_id=other_seq, device_id_type=MESH)
    pl.semaphore_wait(barrier, owners)

    def remote(source, target, send, recv, device):
        return pltpu.make_async_remote_copy(
            src_ref=source, dst_ref=target, send_sem=send, recv_sem=recv, device_id=device, device_id_type=MESH
        )

    token_copy = remote(tokens_ref, all_tokens.at[seq], token_sems.at[0], token_sems.at[1], other_seq)
    token_copy.start()
    gain_copies = [
        remote(gains_ref, all_gains.at[me], gain_sems.at[0, step], gain_sems.at[1, step], device)
        for step, device in others()
    ]
    for copy in gain_copies:
        copy.start()

    def line_copy(way, step, chunk, owner):
        slot = chunk % RING
        return remote(
            pieces.at[chunk, owner],
            pieces.at[chunk, owner],
            line_send.at[way, step - 1, slot],
            line_recv.at[way, step - 1, slot],
            above if way else below,
        )

    def block(which_pair):
        return pl.ds((which_pair * 2 + core) * planes, planes)

    def pair_copy(chunk):
        slot = chunk % RING
        place = pieces.at[chunk, block(pair)]
        return remote(place, place, pair_sems.at[0, slot], pair_sems.at[1, slot], other_pair)

    def core_copy(chunk, which):
        slot = chunk % RING
        place = pieces.at[chunk, block(pair if which == 0 else 1 - pair)]
        return remote(place, place, core_sems.at[0, which, slot], core_sems.at[1, which, slot], other_core)

    def sends(way, step):
        if way:
            return jnp.logical_and(plane < planes - 1, plane - (step - 1) >= 0)
        return jnp.logical_and(plane > 0, plane + (step - 1) <= planes - 1)

    def receives(way, step):
        return plane - step >= 0 if way else plane + step <= planes - 1

    def line(chunk, step):
        for way in range(2):
            if step > 1:

                @pl.when(receives(way, step - 1))
                def _(way=way):
                    line_copy(way, step - 1, chunk, me).wait_recv()

            if step < planes:

                @pl.when(sends(way, step))
                def _(way=way):
                    line_copy(way, step, chunk, me - (step - 1) if way else me + (step - 1)).start()

    def first(chunk):
        slot = chunk
        pltpu.make_async_copy(pieces.at[chunk, me], pieces.at[chunk, me], load_sems.at[slot]).wait()
        line(chunk, 1)

    def across(chunk):
        line(chunk, planes)
        pair_copy(chunk).start()
        core_copy(chunk, 0).start()

    def to_core(chunk):
        pair_copy(chunk).wait_recv()
        core_copy(chunk, 1).start()

    def writes(chunk):
        slot = chunk % RING

        def mix_writes():
            span = pl.ds(pl.multiple_of(chunk * CHUNK, CHUNK), CHUNK)
            return (
                pltpu.make_async_copy(pieces.at[chunk], mix_ref.at[:, :, span], write_sems.at[0, slot]),
                pltpu.make_async_copy(products.at[slot], proj_ref.at[:, span], write_sems.at[1, slot]),
            )

        def out_writes():
            span = pl.ds(pl.multiple_of((chunk - mix_count) * CHUNK, CHUNK), CHUNK)
            return (pltpu.make_async_copy(pieces.at[chunk], out_ref.at[:, :, span], write_sems.at[0, slot]),)

        return mix_writes, out_writes

    def finish(chunk):
        slot = chunk % RING
        core_copy(chunk, 0).wait_recv()
        core_copy(chunk, 1).wait_recv()
        mix_writes, out_writes = writes(chunk)

        @pl.when(chunk >= RING)
        def _():
            written(chunk - RING)

        @pl.when(chunk < mix_count)
        def _():
            weight = pieces[chunk].reshape(owners * rows, CHUNK)
            for half in range(seqs):
                products[slot, half * own_tokens : (half + 1) * own_tokens] = matmul(normed[half], weight)
            for copy in mix_writes():
                copy.start()

        @pl.when(chunk >= mix_count)
        def _():
            for copy in out_writes():
                copy.start()

        pair_copy(chunk).wait_send()
        core_copy(chunk, 0).wait_send()
        core_copy(chunk, 1).wait_send()
        for way in range(2):
            for step in range(1, planes):

                @pl.when(sends(way, step))
                def _(way=way, step=step):
                    line_copy(way, step, chunk, me).wait_send()

    def written(chunk):
        mix_writes, out_writes = writes(chunk)

        @pl.when(chunk < mix_count)
        def _():
            for copy in mix_writes():
                copy.wait()

        @pl.when(chunk >= mix_count)
        def _():
            for copy in out_writes():
                copy.wait()

    def normalize():
        all_tokens[seq] = tokens_ref[...]
        all_gains[me] = gains_ref[...]
        token_copy.wait_recv()
        for copy in gain_copies:
            copy.wait_recv()
        gain = jnp.concatenate([all_gains[owner, 0:1, :] for owner in range(owners)], axis=1)
        size = 64
        per = own_tokens // size

        def part(index, _):
            span = pl.ds((index % per) * size, size)
            values = all_tokens[index // per, span].astype(f32)
            scale = lax.rsqrt(jnp.mean(values * values, axis=-1, keepdims=True) + norm_eps)
            normed[index // per, span] = (values * scale * gain).astype(bf16)
            return 0

        lax.fori_loop(0, seqs * per, part, 0)
        pltpu.make_async_copy(normed, normed_ref, last_sems.at[0]).start()
        pltpu.make_async_copy(all_gains, all_gains_ref, last_sems.at[1]).start()

    acts = [(first, 0)] + [(functools.partial(line, step=step), step - 1) for step in range(2, planes)]
    acts += [(across, planes - 1), (to_core, planes + 1), (finish, planes + 2)]
    last_lag = acts[-1][1]

    def turn_over(turn, _):
        pl.when(turn == last_lag - 1)(normalize)
        for act, lag in acts:
            inside = jnp.logical_and(turn >= lag, turn - lag < total)
            pl.when(inside)(lambda act=act, lag=lag: act(turn - lag))
        return 0

    lax.fori_loop(0, total + last_lag, turn_over, 0)

    def end(chunk, _):
        written(chunk)
        return 0

    lax.fori_loop(total - RING, total, end, 0)
    token_copy.wait_send()
    for copy in gain_copies:
        copy.wait_send()
    pltpu.make_async_copy(normed, normed_ref, last_sems.at[0]).wait()
    pltpu.make_async_copy(all_gains, all_gains_ref, last_sems.at[1]).wait()


def gathered_mixer(tokens, gains, weights):
    own_tokens, width = tokens.shape
    rows = weights[0].shape[0]
    seqs, planes = lax.axis_size("seq"), lax.axis_size("rep")
    owners = lax.axis_size(SR)
    local_width = width // seqs
    total = (4 * local_width + width) // CHUNK
    vmem = pl.BlockSpec(memory_space=pltpu.VMEM)
    anywhere = pl.BlockSpec(memory_space=pl.ANY)
    proj, normed, mix, out, all_gains = pl.pallas_call(
        gather_kernel,
        in_specs=[vmem, vmem] + [anywhere] * 5,
        out_specs=[anywhere] * 5,
        out_shape=[
            jax.ShapeDtypeStruct((seqs * own_tokens, 4 * local_width), f32),
            jax.ShapeDtypeStruct((seqs, own_tokens, width), bf16),
            jax.ShapeDtypeStruct((owners, rows, 4 * local_width), bf16),
            jax.ShapeDtypeStruct((owners, rows, width), bf16),
            jax.ShapeDtypeStruct((owners,) + gains.shape, f32),
        ],
        scratch_shapes=[
            pltpu.VMEM((total, owners, rows, CHUNK), bf16),
            pltpu.VMEM((seqs, own_tokens, width), bf16),
            pltpu.VMEM((seqs, own_tokens, width), bf16),
            pltpu.VMEM((owners,) + gains.shape, f32),
            pltpu.VMEM((RING, seqs * own_tokens, CHUNK), f32),
            pltpu.SemaphoreType.DMA((total,)),
            pltpu.SemaphoreType.DMA((2,)),
            pltpu.SemaphoreType.DMA((2, owners)),
            pltpu.SemaphoreType.DMA((2, planes - 1, RING)),
            pltpu.SemaphoreType.DMA((2, planes - 1, RING)),
            pltpu.SemaphoreType.DMA((2, RING)),
            pltpu.SemaphoreType.DMA((2, 2, RING)),
            pltpu.SemaphoreType.DMA((2, RING)),
            pltpu.SemaphoreType.DMA((2,)),
        ],
        compiler_params=pltpu.CompilerParams(collective_id=1, has_side_effects=True, vmem_limit_bytes=56 << 20),
        name="gathered_mixer",
    )(tokens, gains, *weights)
    normed = normed.reshape(seqs * own_tokens, width)
    return proj, normed, mix.reshape(width, 4 * local_width), out.reshape(width, width), all_gains


def layout_kernel(owners, part, group_width, reduced_ref, down_ref, *outs):
    seqs = reduced_ref.shape[0]
    gate_ref, up_ref, out_ref, down_out = outs[0], outs[1], outs[2], outs[3]
    mix_outs = outs[4:]
    local_ff = owners * part
    local_width = out_ref.shape[1] // seqs
    for seq in range(seqs):
        start = 0
        for unit_ref in (gate_ref, up_ref):
            for owner in range(owners):
                place = (owner * seqs + seq) * part
                unit_ref[:, place : place + part] = reduced_ref[seq, :, start : start + part].astype(f32)
                start += part
        out_ref[:, seq * local_width : (seq + 1) * local_width] = reduced_ref[
            seq, :, start : start + local_width
        ].astype(f32)
        start += local_width
        for group in range(local_width // group_width):
            for mix_ref in mix_outs:
                place = seq * local_width + group * group_width
                mix_ref[:, place : place + group_width] = reduced_ref[seq, :, start : start + group_width].astype(f32)
                start += group_width
    down_out[...] = down_ref[...].astype(f32)


def laid_out(reduced, down, group_width):
    seqs, share, total = reduced.shape
    owners = lax.axis_size(SR)
    down_rows, width = down.shape
    part = down_rows // seqs
    steps = 4
    row_block, down_block = share // steps, down_rows // steps

    def rows_of(size, columns):
        return pl.BlockSpec((size, columns), lambda i: (i, 0))

    shapes = [(share, owners * down_rows)] * 2 + [(share, width), (down_rows, width)] + [(share, width)] * 4
    blocks = [row_block] * 3 + [down_block] + [row_block] * 4
    return pl.pallas_call(
        functools.partial(layout_kernel, owners, part, group_width),
        grid=(steps,),
        in_specs=[
            pl.BlockSpec((seqs, row_block, total), lambda i: (0, i, 0)),
            rows_of(down_block, width),
        ],
        out_specs=[rows_of(block, shape[1]) for block, shape in zip(blocks, shapes)],
        out_shape=[jax.ShapeDtypeStruct(shape, f32) for shape in shapes],
        compiler_params=pltpu.CompilerParams(vmem_limit_bytes=48 << 20),
        name="laid_out",
    )(reduced, down)


def share_columns(share):
    if lax.axis_size("seq") != 2:
        return lax.all_gather(share, "seq", axis=0)
    return in_order(share[None], swap(share)[None], 0)


def body(
    tokens,
    lengths,
    w_query,
    w_forget,
    w_input,
    w_gate_out,
    w_output,
    w_ffn_gate,
    w_ffn_up,
    w_ffn_down,
    norm_in,
    norm_mid,
    head_gain,
    gate_gap,
    cotangent,
):
    row_count, width = tokens.shape[1:]
    seqs = lax.axis_size("seq")
    owners = lax.axis_size(SR)
    seq_index = lax.axis_index("seq")
    owner_index = lax.axis_index(SR)
    share = w_query.shape[0]
    local_width = width // seqs
    local_heads = H // seqs
    group = min(4, local_heads)
    groups = local_heads // group
    down_rows = w_ffn_down.shape[0]
    part = down_rows // seqs
    local_ff = owners * part

    inputs = tokens[0].astype(f32)
    positions = seq_index * row_count + jnp.arange(row_count)
    valid_col = (positions < lengths[0]).astype(f32)[:, None]

    def gathered(value):
        return lax.all_gather(value, SR, axis=0, tiled=True)

    def owned(value):
        return lax.psum_scatter(value, SR, scatter_dimension=0, tiled=True)

    def my_columns(weight):
        return lax.dynamic_slice_in_dim(weight, seq_index * local_width, local_width, 1)

    def my_units(weight):
        shaped = weight.reshape(share, owners, seqs, part)
        return lax.dynamic_index_in_dim(shaped, seq_index, 2, keepdims=False).reshape(share, local_ff)

    gains = jnp.stack([norm_in, norm_mid, gate_gap, jnp.pad(head_gain, (0, share - head_gain.shape[0]))])
    gains = jnp.pad(gains.astype(f32), ((0, 4), (0, 0)))
    mix_weights = (w_query, w_forget, w_input, w_gate_out)
    fast = seqs == 2 and lax.axis_size("shard") == 4
    if fast:
        proj, normed, w_mix, w_out, gains = gathered_mixer(tokens[0], gains, mix_weights + (w_output,))
    else:
        gains = gathered(gains).reshape(owners, 8, share)
    gain_in = gains[:, 0].reshape(1, width)
    gain_mid = gains[:, 1].reshape(1, width)
    gap_full = gains[:, 2].reshape(1, width)
    gain_head = gains[:, 3, : head_gain.shape[0]].reshape(1, HD)
    gap = lax.dynamic_slice_in_dim(gap_full, seq_index * local_width, local_width, 1)
    scale_in = lax.rsqrt(jnp.mean(inputs * inputs, axis=-1, keepdims=True) + norm_eps)
    unit_in = inputs * scale_in
    if not fast:
        mix_share = jnp.stack([my_columns(w) for w in mix_weights], axis=1)
        mix_share = mix_share.reshape(share, 4, groups, group * HD).transpose(0, 2, 1, 3)
        w_mix = gathered(mix_share.reshape(share, 4 * local_width))
        w_out = gathered(w_output)
        normed = gather_tokens((unit_in * gain_in).astype(bf16))
        proj = matmul(normed, w_mix)

    w_gate_up = gathered(jnp.concatenate([my_units(w_ffn_gate), my_units(w_ffn_up)], axis=1))
    w_down = gathered(lax.dynamic_slice_in_dim(w_ffn_down, seq_index * part, part, 0))

    grad_out = cotangent[0].astype(f32)
    grad_ffn = gather_tokens((valid_col * grad_out).astype(bf16))
    branch_heads, states, mixed = mixer_forward(proj, gap, gain_head, group)
    branch_in = columns_to_tokens(branch_heads)
    hidden = inputs + valid_col * matmul(branch_in, w_out)

    scale_mid = lax.rsqrt(jnp.mean(hidden * hidden, axis=-1, keepdims=True) + norm_eps)
    unit_mid = hidden * scale_mid
    normed_mid = gather_tokens((unit_mid * gain_mid).astype(bf16))
    branch_all = gather_tokens(branch_in)
    normed_mid, branch_all = lax.optimization_barrier((normed_mid, branch_all))
    early_lefts = [value.T for value in (normed_mid, branch_all, normed)]
    gate_up = matmul(normed_mid, w_gate_up)
    gate_up, early_lefts = lax.optimization_barrier((gate_up, early_lefts))
    gate_vals = gate_up[:, :local_ff]
    up_vals = gate_up[:, local_ff:]
    gate_act = jax.nn.silu(gate_vals)
    inner = (gate_act * up_vals).astype(bf16)

    grad_inner = matmul_nt(grad_ffn, w_down)
    down_share = owned(matmul_tn(inner, grad_ffn).astype(bf16))
    grad_gate_vals = (grad_inner * up_vals * dsilu(gate_vals)).astype(bf16)
    grad_up_vals = (grad_inner * gate_act).astype(bf16)
    grad_gate_up = jnp.concatenate([grad_gate_vals, grad_up_vals], axis=1)
    grad_normed_mid = scatter_tokens(matmul_nt(grad_gate_up, w_gate_up))
    grad_gain_mid = jnp.sum(grad_normed_mid * unit_mid, axis=0)
    grad_unit_mid = grad_normed_mid * gain_mid
    grad_hidden = grad_out + scale_mid * (
        grad_unit_mid - unit_mid * jnp.mean(grad_unit_mid * unit_mid, axis=-1, keepdims=True)
    )

    grad_branch = (valid_col * grad_hidden).astype(bf16)
    grad_branch_in = tokens_to_columns(matmul_nt(grad_branch, w_out).astype(bf16))
    small = jnp.zeros((owners, 8, share), f32).at[:, 1].set(grad_gain_mid.reshape(owners, share))
    lefts = early_lefts
    if fast:
        partial_out = matmul(inner, w_down)
        partial_out, grad_branch_in = lax.optimization_barrier((partial_out, grad_branch_in))
        mixer = (proj, gap, gain_head, states, mixed, grad_branch_in)
        reduced, small, input_grad = reduced_gradients(
            lefts, grad_gate_up, grad_branch, mixer, w_mix, tokens[0], gain_in, grad_hidden, small, group
        )
        small_share = small.at[3].set(jnp.roll(small[3], -owner_index * (HD // owners)))
        ffn_out = scatter_tokens(partial_out)
        down_all = share_columns(down_share).reshape(down_rows, width)
        grad_gate, grad_up, grad_output, grad_down, *mix_all = laid_out(reduced, down_all, group * HD)
    else:
        grad_proj, grad_gap, grad_gain_head = mixer_backward(
            proj, gap, gain_head, states, mixed, grad_branch_in, group
        )
        grad_normed = scatter_tokens(matmul_nt(grad_proj, w_mix))
        grad_unit_in = grad_normed * gain_in
        grad_inputs = grad_hidden + scale_in * (
            grad_unit_in - unit_in * jnp.mean(grad_unit_in * unit_in, axis=-1, keepdims=True)
        )
        input_grad = grad_inputs.astype(bf16)
        ffn_out = scatter_tokens(matmul(inner, w_down))
        rights = [grad_gate_up, tokens_to_columns(grad_branch), grad_proj]
        partial = jnp.concatenate([matmul(left, right).astype(bf16) for left, right in zip(lefts, rights)], axis=1)
        reduced = lax.all_gather(owned(partial), "seq", axis=0).astype(f32)
        small = small.at[:, 0].set(jnp.sum(grad_normed * unit_in, axis=0).reshape(owners, share))
        gap_placed = lax.dynamic_update_slice_in_dim(
            jnp.zeros((width,), f32), grad_gap.reshape(local_width), seq_index * local_width, 0
        )
        small = small.at[:, 2].set(gap_placed.reshape(owners, share))
        head_total = jnp.sum(grad_gain_head, axis=(0, 1))
        small = small.at[:, 3, : HD // owners].set(head_total.reshape(owners, -1))
        small_share = lax.dynamic_index_in_dim(lax.psum(small, ("seq",) + SR), owner_index, 0, keepdims=False)
        ends = (2 * local_ff, 2 * local_ff + local_width)
        grad_units = reduced[:, :, : ends[0]].reshape(seqs, share, 2, owners, part).transpose(2, 1, 3, 0, 4)
        grad_gate, grad_up = grad_units.reshape(2, share, owners * down_rows)
        grad_output = reduced[:, :, ends[0] : ends[1]].transpose(1, 0, 2).reshape(share, width)
        mix_all = reduced[:, :, ends[1] :].reshape(seqs, share, groups, 4, group * HD)
        mix_all = mix_all.transpose(3, 1, 0, 2, 4).reshape(4, share, width)
        grad_down = share_columns(down_share).reshape(down_rows, width).astype(f32)
    layer_out = (hidden + valid_col * ffn_out).astype(bf16)[None]
    input_grad = input_grad[None]

    return (
        layer_out,
        input_grad,
        mix_all[0],
        mix_all[1],
        mix_all[2],
        mix_all[3],
        grad_output,
        grad_gate,
        grad_up,
        grad_down,
        small_share[0],
        small_share[1],
        small_share[3, : HD // owners],
        small_share[2],
    )


def solution(mesh):
    rows = P(SR, None)
    vector = P(SR)
    by_token = P(SR, "seq", None)
    placed = (by_token, vector) + (rows,) * 8 + (vector,) * 4 + (by_token,)
    return jax.shard_map(
        body,
        mesh=mesh,
        in_specs=placed,
        out_specs=(by_token, by_token) + (rows,) * 8 + (vector,) * 4,
        check_vma=False,
    )
```

```python
import functools

import jax
import jax.numpy as jnp
from jax import lax
from jax.experimental import pallas as pl
from jax.experimental.pallas import tpu as pltpu
from jax.sharding import PartitionSpec as P

H = 16
HD = 128
BLK = 128
SR = ("shard", "rep")
MESH = pl.DeviceIdType.MESH

norm_eps = 1e-05
head_eps = 1e-06

f32 = jnp.float32
bf16 = jnp.bfloat16


def dsilu(values_in):
    sig_vals = jax.nn.sigmoid(values_in)
    return sig_vals * (1.0 + values_in * (1.0 - sig_vals))


def matmul(left, right):
    return jnp.dot(left, right, preferred_element_type=f32)


def matmul_nt(left, right):
    return lax.dot_general(left, right, (((1,), (1,)), ((), ())), preferred_element_type=f32)


def matmul_tn(left, right):
    return lax.dot_general(left, right, (((0,), (0,)), ((), ())), preferred_element_type=f32)


def block_sums(lower, values):
    high, low = split(values)
    return matmul(lower, high) + matmul(lower, low)


def split(values):
    high = values.astype(bf16)
    return high, (values - high.astype(f32)).astype(bf16)


def head_forward(proj, gap, group_width):
    proj_query = proj[:, :group_width]
    proj_forget = proj[:, group_width : 2 * group_width]
    proj_input = proj[:, 2 * group_width : 3 * group_width]
    proj_gate = proj[:, 3 * group_width :]
    sig_query = jax.nn.sigmoid(proj_query)
    queries = (proj_query * sig_query).astype(bf16).astype(f32)
    forget_sig = jax.nn.sigmoid(-proj_forget)
    key_full = gap * forget_sig
    keys = key_full.astype(bf16).astype(f32)
    log_decay = jnp.log1p(-key_full)
    values = proj_input.astype(bf16)
    return proj_query, proj_gate, sig_query, queries, forget_sig, key_full, keys, log_decay, values


def triangle(kind, dtype):
    rows = lax.broadcasted_iota(jnp.int32, (BLK, BLK), 0)
    cols = lax.broadcasted_iota(jnp.int32, (BLK, BLK), 1)
    return (rows >= cols if kind == "lower" else rows <= cols).astype(dtype)


def forward_kernel(heads, proj_ref, gap_ref, gain_ref, branch_ref, states_ref, mixed_ref, state):
    width = heads * HD

    @pl.when(pl.program_id(1) == 0)
    def _():
        state[...] = jnp.zeros_like(state)

    proj = proj_ref[...]
    _, proj_gate, _, queries, _, _, keys, log_decay, values = head_forward(proj, gap_ref[...], width)
    lower = triangle("lower", f32)
    cumul = block_sums(lower.astype(bf16), log_decay)
    grown = jnp.exp(cumul)
    query_dec, query_low = split(queries * grown)
    key_dec, key_low = split(keys * jnp.exp(-cumul))
    last = cumul[BLK - 1 : BLK, :]
    key_tail = (keys * jnp.exp(last - cumul)).astype(bf16)
    last_decay = jnp.exp(last)
    gate_act = proj_gate * jax.nn.sigmoid(proj_gate)
    gain = gain_ref[...]
    for head in range(heads):
        span = slice(head * HD, (head + 1) * HD)
        before = state[head]
        states_ref[0, head] = before
        scores = matmul_nt(query_low[:, span], key_dec[:, span]) + matmul_nt(query_dec[:, span], key_low[:, span])
        scores = (scores + matmul_nt(query_dec[:, span], key_dec[:, span])) * lower
        scores, scores_low = split(scores)
        mixed = matmul(scores_low, values[:, span]) + matmul(scores, values[:, span])
        mixed = mixed + matmul(query_dec[:, span], before.astype(bf16))
        mixed_ref[:, span] = mixed
        decay_col = jnp.transpose(jnp.broadcast_to(last_decay[:, span], (HD, HD)))
        state[head] = decay_col * before + matmul_tn(key_tail[:, span], values[:, span])
        scale = lax.rsqrt(jnp.mean(mixed * mixed, axis=-1, keepdims=True) + head_eps)
        branch_ref[:, span] = (mixed * scale * gain * gate_act[:, span]).astype(bf16)


def backward_block(heads, proj, gap, gain, states, mixed_all, grad_in, dstate, after):
    width = heads * HD
    proj_query, proj_gate, sig_query, queries, forget_sig, key_full, keys, log_decay, values = head_forward(
        proj, gap, width
    )
    lower = triangle("lower", f32)
    upper = triangle("upper", bf16)
    cumul = block_sums(lower.astype(bf16), log_decay)
    grown = jnp.exp(cumul)
    shrunk = jnp.exp(-cumul)
    last = cumul[BLK - 1 : BLK, :]
    tail = jnp.exp(last - cumul)
    last_decay = jnp.exp(last)
    query_dec = (queries * grown).astype(bf16)
    key_dec = (keys * shrunk).astype(bf16)
    key_tail = (keys * tail).astype(bf16)
    sig_gate = jax.nn.sigmoid(proj_gate)
    gate_act = proj_gate * sig_gate
    gate_slope = sig_gate * (1.0 + proj_gate * (1.0 - sig_gate))
    gain_sum = jnp.zeros((1, HD), f32)
    query_grads, key_grads, value_grads, gate_grads, ends = [], [], [], [], []
    for head in range(heads):
        span = slice(head * HD, (head + 1) * HD)
        before = states[head]
        before_low = before.astype(bf16)
        q_dec, k_dec, vals = query_dec[:, span], key_dec[:, span], values[:, span]
        scores = (matmul_nt(q_dec, k_dec) * lower).astype(bf16)
        mixed = mixed_all[:, span]
        scale = lax.rsqrt(jnp.mean(mixed * mixed, axis=-1, keepdims=True) + head_eps)
        unit = mixed * scale
        grad_b = grad_in[:, span]
        gate_grads.append(grad_b * unit * gain * gate_slope[:, span])
        grad_normed = grad_b * gate_act[:, span]
        gain_sum = gain_sum + jnp.sum(grad_normed * unit, axis=0, keepdims=True)
        grad_unit = grad_normed * gain
        grad_mixed = scale * (grad_unit - unit * jnp.mean(grad_unit * unit, axis=-1, keepdims=True))
        grad_low = grad_mixed.astype(bf16)
        down = dstate[head]
        down_low = down.astype(bf16)
        grad_scores = (matmul_nt(grad_low, vals) * lower).astype(bf16)
        value_grads.append(matmul_tn(scores, grad_low) + matmul(key_tail[:, span], down_low))
        grad_q = matmul(grad_scores, k_dec) + matmul_nt(grad_low, before_low)
        grad_k = matmul_tn(grad_scores, q_dec)
        grad_t = matmul_nt(vals, down_low)
        query_grads.append(grad_q * grown[:, span])
        key_grads.append(grad_k * shrunk[:, span] + grad_t * tail[:, span])
        ends.append(jnp.transpose(jnp.sum(down * after[head], axis=1, keepdims=True)))
        after[head] = before
        decay_col = jnp.transpose(jnp.broadcast_to(last_decay[:, span], (HD, HD)))
        dstate[head] = decay_col * down + matmul_tn(q_dec, grad_low)
    grad_queries = jnp.concatenate(query_grads, axis=1)
    grad_keys = jnp.concatenate(key_grads, axis=1)
    grad_values = jnp.concatenate(value_grads, axis=1)
    end = jnp.concatenate(ends, axis=1)
    grad_decay = block_sums(upper, queries * grad_queries - keys * grad_keys) + end
    grad_key_full = grad_keys - grad_decay / (1.0 - key_full)
    gap_sum = jnp.sum(grad_key_full * forget_sig, axis=0, keepdims=True)
    query_slope = sig_query * (1.0 + proj_query * (1.0 - sig_query))
    grads = (
        grad_queries * query_slope,
        -grad_key_full * gap * forget_sig * (1.0 - forget_sig),
        grad_values,
        jnp.concatenate(gate_grads, axis=1),
    )
    return [grad.astype(bf16) for grad in grads], gap_sum, gain_sum


def backward_kernel(
    heads, proj_ref, gap_ref, gain_ref, states_ref, mixed_ref, grad_ref, out_ref, gap_out, gain_out, dstate, after
):
    width = heads * HD

    @pl.when(pl.program_id(1) == 0)
    def _():
        dstate[...] = jnp.zeros_like(dstate)
        after[...] = jnp.zeros_like(after)
        gap_out[...] = jnp.zeros_like(gap_out)
        gain_out[...] = jnp.zeros_like(gain_out)

    states = [states_ref[0, head] for head in range(heads)]
    grads, gap_sum, gain_sum = backward_block(
        heads, proj_ref[...], gap_ref[...], gain_ref[...], states, mixed_ref[...], grad_ref[...].astype(f32), dstate, after
    )
    for kind, grad in enumerate(grads):
        out_ref[:, kind * width : (kind + 1) * width] = grad
    gap_out[...] += gap_sum
    gain_out[...] += gain_sum


def mixer_forward(proj, gap, gain, heads):
    tokens, total = proj.shape
    groups, blocks = total // (4 * heads * HD), tokens // BLK
    width = heads * HD
    return pl.pallas_call(
        functools.partial(forward_kernel, heads),
        grid=(groups, blocks),
        in_specs=[
            pl.BlockSpec((BLK, 4 * width), lambda g, b: (b, g)),
            pl.BlockSpec((1, width), lambda g, b: (0, g)),
            pl.BlockSpec((1, HD), lambda g, b: (0, 0)),
        ],
        out_specs=[
            pl.BlockSpec((BLK, width), lambda g, b: (b, g)),
            pl.BlockSpec((1, heads, HD, HD), lambda g, b: (b, g, 0, 0)),
            pl.BlockSpec((BLK, width), lambda g, b: (b, g)),
        ],
        out_shape=[
            jax.ShapeDtypeStruct((tokens, groups * width), bf16),
            jax.ShapeDtypeStruct((blocks, groups * heads, HD, HD), f32),
            jax.ShapeDtypeStruct((tokens, groups * width), f32),
        ],
        scratch_shapes=[pltpu.VMEM((heads, HD, HD), f32)],
        compiler_params=pltpu.CompilerParams(vmem_limit_bytes=48 << 20),
        name="mixer_forward",
    )(proj, gap, gain)


def mixer_backward(proj, gap, gain, states, mixed, grad, heads):
    tokens, total = proj.shape
    groups, blocks = total // (4 * heads * HD), tokens // BLK
    width = heads * HD
    return pl.pallas_call(
        functools.partial(backward_kernel, heads),
        grid=(groups, blocks),
        in_specs=[
            pl.BlockSpec((BLK, 4 * width), lambda g, b: (blocks - 1 - b, g)),
            pl.BlockSpec((1, width), lambda g, b: (0, g)),
            pl.BlockSpec((1, HD), lambda g, b: (0, 0)),
            pl.BlockSpec((1, heads, HD, HD), lambda g, b: (blocks - 1 - b, g, 0, 0)),
            pl.BlockSpec((BLK, width), lambda g, b: (blocks - 1 - b, g)),
            pl.BlockSpec((BLK, width), lambda g, b: (blocks - 1 - b, g)),
        ],
        out_specs=[
            pl.BlockSpec((BLK, 4 * width), lambda g, b: (blocks - 1 - b, g)),
            pl.BlockSpec((1, width), lambda g, b: (0, g)),
            pl.BlockSpec((1, 1, HD), lambda g, b: (g, 0, 0)),
        ],
        out_shape=[
            jax.ShapeDtypeStruct((tokens, total), bf16),
            jax.ShapeDtypeStruct((1, groups * width), f32),
            jax.ShapeDtypeStruct((groups, 1, HD), f32),
        ],
        scratch_shapes=[pltpu.VMEM((heads, HD, HD), f32), pltpu.VMEM((heads, HD, HD), f32)],
        compiler_params=pltpu.CompilerParams(vmem_limit_bytes=48 << 20),
        name="mixer_backward",
    )(proj, gap, gain, states, mixed, grad)


def swap(value):
    return lax.ppermute(value, "seq", [(0, 1), (1, 0)])


def in_order(own, other, axis):
    first = lax.axis_index("seq") == 0
    return jnp.concatenate([jnp.where(first, own, other), jnp.where(first, other, own)], axis=axis)


def gather_tokens(value):
    if lax.axis_size("seq") != 2:
        return lax.all_gather(value, "seq", axis=0, tiled=True)
    return in_order(value, swap(value), 0)


def scatter_tokens(partial):
    if lax.axis_size("seq") != 2:
        return lax.psum_scatter(partial.astype(bf16), "seq", scatter_dimension=0, tiled=True).astype(f32)
    rows = partial.shape[0] // 2
    me = lax.axis_index("seq")
    theirs = lax.dynamic_slice_in_dim(partial, (1 - me) * rows, rows, 0).astype(bf16)
    return lax.dynamic_slice_in_dim(partial, me * rows, rows, 0) + swap(theirs).astype(f32)


def columns_to_tokens(value):
    if lax.axis_size("seq") != 2:
        return lax.all_to_all(value, "seq", 0, 1, tiled=True)
    rows = value.shape[0] // 2
    me = lax.axis_index("seq")
    theirs = swap(lax.dynamic_slice_in_dim(value, (1 - me) * rows, rows, 0))
    return in_order(lax.dynamic_slice_in_dim(value, me * rows, rows, 0), theirs, 1)


def tokens_to_columns(value):
    if lax.axis_size("seq") != 2:
        return lax.all_to_all(value, "seq", 1, 0, tiled=True)
    cols = value.shape[1] // 2
    me = lax.axis_index("seq")
    theirs = swap(lax.dynamic_slice_in_dim(value, (1 - me) * cols, cols, 1))
    return in_order(lax.dynamic_slice_in_dim(value, me * cols, cols, 1), theirs, 0)


RING = 8
CORE_RING = 4
CHUNK = 256


def reduce_kernel(counts, heads, *refs):
    kinds = len(counts)
    lefts = refs[:kinds]
    (
        units_ref,
        own_mid,
        other_mid,
        hidden_ref,
        cotangent_ref,
        valid_ref,
        gain_mid_ref,
        wout_ref,
        proj_ref,
        gap_ref,
        gain_ref,
        states_ref,
        mixed_ref,
        mix_ref,
        tokens_ref,
        gain_in_ref,
        out_ref,
        small_out,
        input_out,
        core_out,
        core_in,
        pair_out,
        pair_in,
        sums,
        line_in,
        done,
        core_sems,
        pair_sems,
        line_send,
        line_recv,
        done_sems,
        small_in,
        small_all,
        small_sems,
        columns,
        column_sems,
        grad_proj,
        proj_in,
        proj_sems,
        dstate,
        after,
        gap_acc,
        gain_acc,
        weights_in,
        weight_sems,
        kept_normed,
        sent_normed,
        got_normed,
        normed_sems,
        got_mid,
        mid_sems,
        grad_hidden,
        branch_ref,
        grad_ref,
        sent_heads,
        head_sems,
        mid_sum,
    ) = refs[kinds:]
    rights = (units_ref, columns, grad_proj)
    total = sum(counts)
    planes, rows = sums.shape[1:3]
    seq = lax.axis_index("seq")
    shard = lax.axis_index("shard")
    plane = lax.axis_index("rep")
    core, pair = shard % 2, shard // 2
    other_core = {"shard": shard + 1 - 2 * core}
    other_pair = {"shard": (shard + 2) % 4}
    other_seq = {"seq": 1 - seq}
    below, above = {"rep": plane - 1}, {"rep": plane + 1}
    me = shard * planes + plane
    owners = small_all.shape[0]
    devices = small_in.shape[0]
    number = seq * owners + me

    def others():
        for step in range(1, devices):
            there = (number + step) % devices
            owner = there % owners
            yield step, owner, {"seq": there // owners, "shard": owner // planes, "rep": owner % planes}

    barrier = pltpu.get_barrier_semaphore()
    for _, _, device in others():
        pl.semaphore_signal(barrier, inc=1, device_id=device, device_id_type=MESH)
    pl.semaphore_wait(barrier, devices - 1)

    def remote(source, target, send, recv, device):
        return pltpu.make_async_remote_copy(
            src_ref=source, dst_ref=target, send_sem=send, recv_sem=recv, device_id=device, device_id_type=MESH
        )

    own_tokens, width = tokens_ref.shape
    local_width = columns.shape[1]
    group_width = heads * HD
    groups, blocks = local_width // group_width, grad_proj.shape[0] // BLK

    piece = weights_in.shape[1]
    pieces = width // piece

    def aligned(start, size):
        return pl.ds(pl.multiple_of(start, size), size)

    def mid_copy():
        return remote(other_mid, got_mid, mid_sems.at[0], mid_sems.at[1], other_seq)

    def mid_turn():
        mid_copy().wait()
        gain = gain_mid_ref[...]
        size = 64

        def part(index, total_mid):
            rows_at = aligned(index * size, size)
            values = hidden_ref[rows_at]
            scale = lax.rsqrt(jnp.mean(values * values, axis=-1, keepdims=True) + norm_eps)
            unit = values * scale
            grad = own_mid[rows_at] + got_mid[rows_at].astype(f32)
            grad_unit = grad * gain
            moved = scale * (grad_unit - unit * jnp.mean(grad_unit * unit, axis=-1, keepdims=True))
            both = cotangent_ref[rows_at].astype(f32) + moved
            grad_hidden[rows_at] = both
            branch_ref[rows_at] = (valid_ref[rows_at] * both).astype(bf16)
            return total_mid + jnp.sum(grad * unit, axis=0, keepdims=True)

        mid_sum[...] = lax.fori_loop(0, own_tokens // size, part, jnp.zeros((1, width), f32))

    def wout_load(index):
        return pltpu.make_async_copy(
            wout_ref.at[aligned(index * piece, piece)],
            weights_in.at[index % 2, :, pl.ds(0, width)],
            weight_sems.at[index % 2],
        )

    def head_copy():
        place = grad_ref.at[aligned(seq * own_tokens, own_tokens)]
        return remote(sent_heads, place, head_sems.at[0], head_sems.at[1], other_seq)

    def heads_turn():
        def part(index, _):
            @pl.when(index + 1 < pieces)
            def _():
                wout_load(index + 1).start()

            wout_load(index).wait()
            grad = matmul_nt(branch_ref[...], weights_in[index % 2, :, :width]).astype(bf16)
            span = aligned((index % per_seq) * piece, piece)

            @pl.when(index // per_seq == seq)
            def _():
                grad_ref[aligned(seq * own_tokens, own_tokens), span] = grad

            @pl.when(index // per_seq != seq)
            def _():
                sent_heads[:, span] = grad

            return 0

        per_seq = local_width // piece
        lax.fori_loop(0, pieces, part, 0)
        head_copy().start()
        for copy in column_moves():
            copy.start()
        weight_load(0).start()

    def column_moves():
        mine = branch_ref.at[:, aligned(seq * local_width, local_width)]
        theirs = branch_ref.at[:, aligned((1 - seq) * local_width, local_width)]
        place = columns.at[aligned(seq * own_tokens, own_tokens)]
        kept = pltpu.make_async_copy(mine, place, column_sems.at[0])
        return kept, remote(theirs, place, column_sems.at[1], column_sems.at[2], other_seq)

    def proj_load(index):
        group, block = index // blocks, blocks - 1 - index % blocks
        source = proj_ref.at[aligned(block * BLK, BLK), aligned(group * 4 * group_width, 4 * group_width)]
        return pltpu.make_async_copy(source, proj_in.at[index % 2], proj_sems.at[index % 2])

    def mixer_turn(index):
        group, block = index // blocks, blocks - 1 - index % blocks
        rows_at, span = aligned(block * BLK, BLK), aligned(group * group_width, group_width)

        @pl.when(index + 1 < groups * blocks)
        def _():
            proj_load(index + 1).start()

        @pl.when(index % blocks == 0)
        def _():
            dstate[...] = jnp.zeros_like(dstate)
            after[...] = jnp.zeros_like(after)
            gap_acc[:, span] = jnp.zeros((1, group_width), f32)

        proj_load(index).wait()
        states = [states_ref[block, group * heads + head] for head in range(heads)]
        grads, gap_sum, gain_sum = backward_block(
            heads,
            proj_in[index % 2],
            gap_ref[:, span],
            gain_ref[...],
            states,
            mixed_ref[rows_at, span],
            grad_ref[rows_at, span].astype(f32),
            dstate,
            after,
        )
        for kind, grad in enumerate(grads):
            grad_proj[rows_at, aligned((group * 4 + kind) * group_width, group_width)] = grad
        gap_acc[:, span] += gap_sum
        gain_acc[...] += gain_sum

    def weight_load(index):
        return pltpu.make_async_copy(
            mix_ref.at[aligned(index * piece, piece)], weights_in.at[index % 2], weight_sems.at[index % 2]
        )

    def normed_copy():
        return remote(sent_normed, got_normed, normed_sems.at[0], normed_sems.at[1], other_seq)

    def normed_turn(index):
        @pl.when(index + 1 < pieces)
        def _():
            weight_load(index + 1).start()

        weight_load(index).wait()
        weight = weights_in[index % 2]
        span = aligned(index * piece, piece)
        sent_normed[:, span] = matmul_nt(grad_proj[aligned((1 - seq) * own_tokens, own_tokens)], weight).astype(bf16)
        kept_normed[:, span] = matmul_nt(grad_proj[aligned(seq * own_tokens, own_tokens)], weight)

        @pl.when(index == pieces - 1)
        def _():
            normed_copy().start()

    def input_turn():
        normed_copy().wait()
        gain = gain_in_ref[...]
        size = 64

        def part(index, total_in):
            rows_at = aligned(index * size, size)
            values = tokens_ref[rows_at].astype(f32)
            scale = lax.rsqrt(jnp.mean(values * values, axis=-1, keepdims=True) + norm_eps)
            unit = values * scale
            grad = kept_normed[rows_at] + got_normed[rows_at].astype(f32)
            grad_unit = grad * gain
            moved = scale * (grad_unit - unit * jnp.mean(grad_unit * unit, axis=-1, keepdims=True))
            input_out[rows_at] = (grad_hidden[rows_at] + moved).astype(bf16)
            return total_in + jnp.sum(grad * unit, axis=0, keepdims=True)

        total_in = lax.fori_loop(0, own_tokens // size, part, jnp.zeros((1, width), f32))
        small_all[...] = jnp.zeros_like(small_all)
        for owner in range(owners):
            small_all[owner, 1:2, :] = mid_sum[:, owner * rows : (owner + 1) * rows]
            small_all[owner, 0:1, :] = total_in[:, owner * rows : (owner + 1) * rows]
            small_all[owner, 3:4, :] = gain_acc[...]
        first_owner = seq * (local_width // rows)
        for index in range(local_width // rows):
            small_all[first_owner + index, 2:3, :] = gap_acc[:, index * rows : (index + 1) * rows]
        for copy in small_copies:
            copy.start()

    small_copies = [
        remote(small_all.at[owner], small_in.at[number], small_sems.at[0, step], small_sems.at[1, step], device)
        for step, owner, device in others()
    ]
    gain_acc[...] = jnp.zeros_like(gain_acc)
    proj_load(0).start()
    wout_load(0).start()
    mid_copy().start()

    def core_copy(chunk):
        slot = chunk % CORE_RING
        return remote(
            core_out.at[slot], core_in.at[slot], core_sems.at[0, slot], core_sems.at[1, slot], other_core
        )

    def pair_copy(slot):
        return remote(
            pair_out.at[slot], pair_in.at[slot], pair_sems.at[0, slot], pair_sems.at[1, slot], other_pair
        )

    def line_copy(way, step, slot, target):
        return remote(
            sums.at[slot, target],
            line_in.at[way, step - 1, slot],
            line_send.at[way, step - 1, slot],
            line_recv.at[way, step - 1, slot],
            above if way else below,
        )

    def done_copies(chunk):
        slot = chunk % RING
        place = out_ref.at[seq, :, pl.ds(pl.multiple_of(chunk * CHUNK, CHUNK), CHUNK)]
        kept = pltpu.make_async_copy(done.at[slot], place, done_sems.at[2, slot])
        sent = remote(done.at[slot], place, done_sems.at[0, slot], done_sems.at[1, slot], other_seq)
        return kept, sent

    def product(kind, chunk, half, which):
        first = (half * 2 + which) * planes * rows
        left = lefts[kind][pl.ds(pl.multiple_of(first, planes * rows), planes * rows), :]
        start = (chunk - sum(counts[:kind])) * CHUNK
        return matmul(left, rights[kind][:, pl.ds(pl.multiple_of(start, CHUNK), CHUNK)])

    def line_target(way, step):
        return plane + planes - step if way else plane - planes + step

    def sends(way, step):
        return plane < step if way else plane >= planes - step

    def receives(way, step):
        return jnp.logical_and(plane > 0, plane <= step) if way else jnp.logical_and(plane < planes - 1, plane >= planes - step - 1)

    def front(kind, chunk):
        slot = chunk % CORE_RING

        @pl.when(chunk >= CORE_RING)
        def _():
            core_copy(chunk).wait_send()

        for half in range(2):
            core_out[slot, half] = product(kind, chunk, half, 1 - core).astype(bf16)
        core_copy(chunk).start()

    def middle(kind, chunk):
        slot, core_slot = chunk % RING, chunk % CORE_RING

        @pl.when(chunk >= RING)
        def _():
            pair_copy(slot).wait_send()

        theirs = product(kind, chunk, 1 - pair, core)
        mine = product(kind, chunk, pair, core)
        core_copy(chunk).wait_recv()
        pair_out[slot] = (theirs + core_in[core_slot, 1 - pair].astype(f32)).astype(bf16)
        pair_copy(slot).start()
        mine = mine + core_in[core_slot, pair].astype(f32)
        sums[slot] = mine.astype(bf16).reshape(planes, rows, CHUNK)

    def line_start(chunk, step):
        slot = chunk % RING
        for way in range(2):

            @pl.when(sends(way, step))
            def _(way=way):
                target = line_target(way, step)
                if step > 1:

                    @pl.when(receives(way, step - 1))
                    def _():
                        line_copy(way, step - 1, slot, 0).wait_recv()
                        got = line_in[way, step - 2, slot].astype(f32)
                        sums[slot, target] = (sums[slot, target].astype(f32) + got).astype(bf16)

                line_copy(way, step, slot, target).start()

    def pair_done(chunk):
        slot = chunk % RING
        pair_copy(slot).wait_recv()
        got = pair_in[slot].reshape(planes, rows, CHUNK).astype(f32)
        sums[slot] = (sums[slot].astype(f32) + got).astype(bf16)
        line_start(chunk, 1)

    def finish(chunk):
        slot = chunk % RING
        kept, sent = done_copies(chunk)

        @pl.when(chunk >= RING)
        def _():
            kept.wait()
            sent.wait_send()

        last = planes - 1
        for way in range(2):

            @pl.when(receives(way, last))
            def _(way=way):
                line_copy(way, last, slot, 0).wait_recv()
                got = line_in[way, last - 1, slot].astype(f32)
                sums[slot, plane] = (sums[slot, plane].astype(f32) + got).astype(bf16)

        done[slot] = sums[slot, plane]
        kept.start()
        sent.start()
        for way in range(2):
            for step in range(1, planes):

                @pl.when(sends(way, step))
                def _(way=way, step=step):
                    line_copy(way, step, slot, 0).wait_send()

    def received(chunk):
        done_copies(chunk)[1].wait_recv()

    later = [(pair_done, 3)] + [
        (functools.partial(line_start, step=step), 2 + step) for step in range(2, planes)
    ] + [(finish, 2 + planes), (received, 4 + planes)]
    mid_at, mixer_at = 6, 10
    normed_at = mixer_at + groups * blocks
    assert normed_at + pieces // 2 <= counts[0]
    first = 0
    for kind, count in enumerate(counts):

        def step(turn, _, kind=kind, first=first):
            front(kind, turn)
            if kind == 0:
                pl.when(turn >= 1)(lambda: middle(0, turn - 1))
            else:
                pl.when(turn == first)(lambda: middle(kind - 1, turn - 1))
                pl.when(turn > first)(lambda: middle(kind, turn - 1))
            if kind == 0:
                pl.when(turn == mid_at)(mid_turn)
                pl.when(turn == mid_at + 1)(heads_turn)
                pl.when(turn == mixer_at)(lambda: head_copy().wait())
                inside = jnp.logical_and(turn >= mixer_at, turn < normed_at)
                pl.when(inside)(lambda: mixer_turn(turn - mixer_at))

                @pl.when(jnp.logical_and(turn >= normed_at, turn < normed_at + pieces // 2))
                def _():
                    normed_turn(2 * (turn - normed_at))
                    normed_turn(2 * (turn - normed_at) + 1)

            elif kind == kinds - 1:
                pl.when(turn == first + 1)(input_turn)
            for act, lag in later:
                pl.when(turn >= lag)(lambda act=act, lag=lag: act(turn - lag))
            return 0

        if kind == 1:
            for copy in column_moves():
                copy.wait()
        lax.fori_loop(first, first + count, step, 0)
        first += count

    def drain(turn, _):
        pl.when(turn == total)(lambda: middle(kinds - 1, turn - 1))
        for act, lag in later:
            pl.when(turn - lag < total)(lambda act=act, lag=lag: act(turn - lag))
        return 0

    lax.fori_loop(total, total + later[-1][1], drain, 0)
    for chunk in range(total - RING, total):
        slot = chunk % RING
        if chunk >= total - CORE_RING:
            core_copy(chunk).wait_send()
        pair_copy(slot).wait_send()
        kept, sent = done_copies(chunk)
        kept.wait()
        sent.wait_send()
    small_in[number] = small_all[me]
    for copy in small_copies:
        copy.wait()
    small_out[...] = jnp.sum(small_in[...], axis=0)


def reduced_gradients(lefts, grad_units, middle, mixer, w_out, w_mix, tokens, gain_in, heads):
    proj, gap, gain, states, mixed = mixer
    own_tokens, width = tokens.shape
    local_width = mixed.shape[1]
    counts = [columns // CHUNK for columns in (grad_units.shape[1], local_width, proj.shape[1])]
    planes = lax.axis_size("rep")
    rows = lefts[0].shape[0] // lax.axis_size(SR)
    block = planes * rows
    owners = lax.axis_size(SR)
    devices = lax.axis_size(("seq",) + SR)
    vmem = pl.BlockSpec(memory_space=pltpu.VMEM)
    anywhere = pl.BlockSpec(memory_space=pl.ANY)
    return pl.pallas_call(
        functools.partial(reduce_kernel, counts, heads),
        in_specs=[vmem] * 10 + [anywhere] * 2 + [vmem] * 4 + [anywhere] + [vmem] * 2,
        out_specs=[anywhere, vmem, vmem],
        out_shape=[
            jax.ShapeDtypeStruct((2, rows, sum(counts) * CHUNK), bf16),
            jax.ShapeDtypeStruct((8, rows), f32),
            jax.ShapeDtypeStruct((own_tokens, width), bf16),
        ],
        scratch_shapes=[
            pltpu.VMEM((CORE_RING, 2, block, CHUNK), bf16),
            pltpu.VMEM((CORE_RING, 2, block, CHUNK), bf16),
            pltpu.VMEM((RING, block, CHUNK), bf16),
            pltpu.VMEM((RING, block, CHUNK), bf16),
            pltpu.VMEM((RING, planes, rows, CHUNK), bf16),
            pltpu.VMEM((2, planes - 1, RING, rows, CHUNK), bf16),
            pltpu.VMEM((RING, rows, CHUNK), bf16),
            pltpu.SemaphoreType.DMA((2, CORE_RING)),
            pltpu.SemaphoreType.DMA((2, RING)),
            pltpu.SemaphoreType.DMA((2, planes - 1, RING)),
            pltpu.SemaphoreType.DMA((2, planes - 1, RING)),
            pltpu.SemaphoreType.DMA((3, RING)),
            pltpu.VMEM((devices, 8, rows), f32),
            pltpu.VMEM((owners, 8, rows), f32),
            pltpu.SemaphoreType.DMA((2, devices)),
            pltpu.VMEM((2 * own_tokens, local_width), bf16),
            pltpu.SemaphoreType.DMA((3,)),
            pltpu.VMEM(proj.shape, bf16),
            pltpu.VMEM((2, BLK, 4 * heads * HD), f32),
            pltpu.SemaphoreType.DMA((2,)),
            pltpu.VMEM((heads, HD, HD), f32),
            pltpu.VMEM((heads, HD, HD), f32),
            pltpu.VMEM((1, local_width), f32),
            pltpu.VMEM((1, HD), f32),
            pltpu.VMEM((2, CHUNK, proj.shape[1]), bf16),
            pltpu.SemaphoreType.DMA((2,)),
            pltpu.VMEM((own_tokens, width), f32),
            pltpu.VMEM((own_tokens, width), bf16),
            pltpu.VMEM((own_tokens, width), bf16),
            pltpu.SemaphoreType.DMA((2,)),
            pltpu.VMEM((own_tokens, width), bf16),
            pltpu.SemaphoreType.DMA((2,)),
            pltpu.VMEM((own_tokens, width), f32),
            pltpu.VMEM((own_tokens, width), bf16),
            pltpu.VMEM((2 * own_tokens, local_width), bf16),
            pltpu.VMEM((own_tokens, local_width), bf16),
            pltpu.SemaphoreType.DMA((2,)),
            pltpu.VMEM((1, width), f32),
        ],
        compiler_params=pltpu.CompilerParams(
            collective_id=0, has_side_effects=True, vmem_limit_bytes=62 << 20
        ),
        name="reduced_gradients",
    )(*lefts, grad_units, *middle, w_out, proj, gap, gain, states, mixed, w_mix, tokens, gain_in)


def gather_kernel(
    tokens_ref,
    gains_ref,
    w_query,
    w_forget,
    w_input,
    w_gate_out,
    w_output,
    proj_ref,
    normed_ref,
    mix_ref,
    out_ref,
    all_gains_ref,
    pieces,
    all_tokens,
    normed,
    all_gains,
    products,
    load_sems,
    token_sems,
    gain_sems,
    line_send,
    line_recv,
    pair_sems,
    core_sems,
    write_sems,
    half_sems,
    last_sems,
):
    total, owners, rows = pieces.shape[:3]
    seqs, own_tokens, width = all_tokens.shape
    local_width = width // seqs
    out_count = local_width // CHUNK
    group_width = mix_ref.shape[2] // 4 // (local_width // (4 * HD))
    planes = lax.axis_size("rep")
    seq = lax.axis_index("seq")
    shard = lax.axis_index("shard")
    plane = lax.axis_index("rep")
    core, pair = shard % 2, shard // 2
    me = shard * planes + plane
    other_core = {"shard": shard + 1 - 2 * core}
    other_pair = {"shard": (shard + 2) % 4}
    other_seq = {"seq": 1 - seq}
    below, above = {"rep": plane - 1}, {"rep": plane + 1}

    loads = []
    per_group = group_width // CHUNK
    for chunk in range(total):
        if chunk < out_count:
            source, start = w_output, chunk * CHUNK
        else:
            group, rest = divmod(chunk - out_count, 4 * per_group)
            kind, part = divmod(rest, per_group)
            source = (w_query, w_forget, w_input, w_gate_out)[kind]
            start = group * group_width + part * CHUNK
        start = pl.multiple_of(seq * local_width + start, CHUNK)
        loads.append(
            pltpu.make_async_copy(source.at[:, pl.ds(start, CHUNK)], pieces.at[chunk, me], load_sems.at[chunk])
        )
    for load in loads:
        load.start()

    def others():
        for step in range(1, owners):
            number = (me + step) % owners
            yield step, {"shard": number // planes, "rep": number % planes}

    barrier = pltpu.get_barrier_semaphore()
    for _, device in others():
        pl.semaphore_signal(barrier, inc=1, device_id=device, device_id_type=MESH)
    pl.semaphore_signal(barrier, inc=1, device_id=other_seq, device_id_type=MESH)
    pl.semaphore_wait(barrier, owners)

    def remote(source, target, send, recv, device):
        return pltpu.make_async_remote_copy(
            src_ref=source, dst_ref=target, send_sem=send, recv_sem=recv, device_id=device, device_id_type=MESH
        )

    token_copy = remote(tokens_ref, all_tokens.at[seq], token_sems.at[0], token_sems.at[1], other_seq)
    token_copy.start()
    gain_copies = [
        remote(gains_ref, all_gains.at[me], gain_sems.at[0, step], gain_sems.at[1, step], device)
        for step, device in others()
    ]
    for copy in gain_copies:
        copy.start()

    def line_copy(way, step, chunk, owner):
        slot = chunk % RING
        return remote(
            pieces.at[chunk, owner],
            pieces.at[chunk, owner],
            line_send.at[way, step - 1, slot],
            line_recv.at[way, step - 1, slot],
            above if way else below,
        )

    def block(which_pair):
        return pl.ds((which_pair * 2 + core) * planes, planes)

    def pair_copy(chunk):
        slot = chunk % RING
        place = pieces.at[chunk, block(pair)]
        return remote(place, place, pair_sems.at[0, slot], pair_sems.at[1, slot], other_pair)

    def core_copy(chunk, which):
        slot = chunk % RING
        place = pieces.at[chunk, block(pair if which == 0 else 1 - pair)]
        return remote(place, place, core_sems.at[0, which, slot], core_sems.at[1, which, slot], other_core)

    def sends(way, step):
        if way:
            return jnp.logical_and(plane < planes - 1, plane - (step - 1) >= 0)
        return jnp.logical_and(plane > 0, plane + (step - 1) <= planes - 1)

    def receives(way, step):
        return plane - step >= 0 if way else plane + step <= planes - 1

    def line(chunk, step):
        for way in range(2):
            if step > 1:

                @pl.when(receives(way, step - 1))
                def _(way=way):
                    line_copy(way, step - 1, chunk, me).wait_recv()

            if step < planes:

                @pl.when(sends(way, step))
                def _(way=way):
                    line_copy(way, step, chunk, me - (step - 1) if way else me + (step - 1)).start()

    def first(chunk):
        slot = chunk
        pltpu.make_async_copy(pieces.at[chunk, me], pieces.at[chunk, me], load_sems.at[slot]).wait()
        line(chunk, 1)

    def across(chunk):
        line(chunk, planes)
        pair_copy(chunk).start()
        core_copy(chunk, 0).start()

    def to_core(chunk):
        pair_copy(chunk).wait_recv()
        core_copy(chunk, 1).start()

    def writes(chunk):
        slot = chunk % RING

        def mix_writes():
            span = pl.ds(pl.multiple_of((chunk - out_count) * CHUNK, CHUNK), CHUNK)
            return (
                pltpu.make_async_copy(pieces.at[chunk], mix_ref.at[:, :, span], write_sems.at[0, slot]),
                pltpu.make_async_copy(products.at[slot], proj_ref.at[:, span], write_sems.at[1, slot]),
            )

        def out_writes():
            place = out_ref.at[:, :, pl.ds(pl.multiple_of(seq * local_width + chunk * CHUNK, CHUNK), CHUNK)]
            return (
                pltpu.make_async_copy(pieces.at[chunk], place, half_sems.at[2, slot]),
                remote(pieces.at[chunk], place, half_sems.at[0, slot], half_sems.at[1, slot], other_seq),
            )

        return mix_writes, out_writes

    def finish(chunk):
        slot = chunk % RING
        core_copy(chunk, 0).wait_recv()
        core_copy(chunk, 1).wait_recv()
        mix_writes, out_writes = writes(chunk)

        @pl.when(chunk >= out_count + RING)
        def _():
            written(chunk - RING)

        @pl.when(chunk >= out_count)
        def _():
            weight = pieces[chunk].reshape(owners * rows, CHUNK)
            for half in range(seqs):
                products[slot, half * own_tokens : (half + 1) * own_tokens] = matmul(normed[half], weight)
            for copy in mix_writes():
                copy.start()

        @pl.when(chunk < out_count)
        def _():
            for copy in out_writes():
                copy.start()

        pair_copy(chunk).wait_send()
        core_copy(chunk, 0).wait_send()
        core_copy(chunk, 1).wait_send()
        for way in range(2):
            for step in range(1, planes):

                @pl.when(sends(way, step))
                def _(way=way, step=step):
                    line_copy(way, step, chunk, me).wait_send()

    def written(chunk):
        for copy in writes(chunk)[0]():
            copy.wait()

    def normalize():
        all_tokens[seq] = tokens_ref[...]
        all_gains[me] = gains_ref[...]
        token_copy.wait_recv()
        for copy in gain_copies:
            copy.wait_recv()
        gain = jnp.concatenate([all_gains[owner, 0:1, :] for owner in range(owners)], axis=1)
        size = 64
        per = own_tokens // size

        def part(index, _):
            span = pl.ds((index % per) * size, size)
            values = all_tokens[index // per, span].astype(f32)
            scale = lax.rsqrt(jnp.mean(values * values, axis=-1, keepdims=True) + norm_eps)
            normed[index // per, span] = (values * scale * gain).astype(bf16)
            return 0

        lax.fori_loop(0, seqs * per, part, 0)
        pltpu.make_async_copy(normed, normed_ref, last_sems.at[0]).start()
        pltpu.make_async_copy(all_gains, all_gains_ref, last_sems.at[1]).start()

    acts = [(first, 0)] + [(functools.partial(line, step=step), step - 1) for step in range(2, planes)]
    acts += [(across, planes - 1), (to_core, planes + 1), (finish, planes + 2)]
    last_lag = acts[-1][1]

    def turn_over(turn, _):
        pl.when(turn == last_lag - 1)(normalize)
        for act, lag in acts:
            inside = jnp.logical_and(turn >= lag, turn - lag < total)
            pl.when(inside)(lambda act=act, lag=lag: act(turn - lag))
        return 0

    lax.fori_loop(0, total + last_lag, turn_over, 0)

    def end(chunk, _):
        written(chunk)
        return 0

    lax.fori_loop(total - RING, total, end, 0)
    for chunk in range(out_count):
        for copy in writes(chunk)[1]():
            copy.wait()
    token_copy.wait_send()
    for copy in gain_copies:
        copy.wait_send()
    pltpu.make_async_copy(normed, normed_ref, last_sems.at[0]).wait()
    pltpu.make_async_copy(all_gains, all_gains_ref, last_sems.at[1]).wait()


def gathered_mixer(tokens, gains, weights):
    own_tokens, width = tokens.shape
    rows = weights[0].shape[0]
    seqs, planes = lax.axis_size("seq"), lax.axis_size("rep")
    owners = lax.axis_size(SR)
    local_width = width // seqs
    total = 5 * local_width // CHUNK
    vmem = pl.BlockSpec(memory_space=pltpu.VMEM)
    anywhere = pl.BlockSpec(memory_space=pl.ANY)
    proj, normed, mix, out, all_gains = pl.pallas_call(
        gather_kernel,
        in_specs=[vmem, vmem] + [anywhere] * 5,
        out_specs=[anywhere] * 5,
        out_shape=[
            jax.ShapeDtypeStruct((seqs * own_tokens, 4 * local_width), f32),
            jax.ShapeDtypeStruct((seqs, own_tokens, width), bf16),
            jax.ShapeDtypeStruct((owners, rows, 4 * local_width), bf16),
            jax.ShapeDtypeStruct((owners, rows, width), bf16),
            jax.ShapeDtypeStruct((owners,) + gains.shape, f32),
        ],
        scratch_shapes=[
            pltpu.VMEM((total, owners, rows, CHUNK), bf16),
            pltpu.VMEM((seqs, own_tokens, width), bf16),
            pltpu.VMEM((seqs, own_tokens, width), bf16),
            pltpu.VMEM((owners,) + gains.shape, f32),
            pltpu.VMEM((RING, seqs * own_tokens, CHUNK), f32),
            pltpu.SemaphoreType.DMA((total,)),
            pltpu.SemaphoreType.DMA((2,)),
            pltpu.SemaphoreType.DMA((2, owners)),
            pltpu.SemaphoreType.DMA((2, planes - 1, RING)),
            pltpu.SemaphoreType.DMA((2, planes - 1, RING)),
            pltpu.SemaphoreType.DMA((2, RING)),
            pltpu.SemaphoreType.DMA((2, 2, RING)),
            pltpu.SemaphoreType.DMA((2, RING)),
            pltpu.SemaphoreType.DMA((3, RING)),
            pltpu.SemaphoreType.DMA((2,)),
        ],
        compiler_params=pltpu.CompilerParams(collective_id=1, has_side_effects=True, vmem_limit_bytes=56 << 20),
        name="gathered_mixer",
    )(tokens, gains, *weights)
    normed = normed.reshape(seqs * own_tokens, width)
    return proj, normed, mix.reshape(width, 4 * local_width), out.reshape(width, width), all_gains


def layout_kernel(owners, part, group_width, reduced_ref, *outs):
    seqs = reduced_ref.shape[0]
    gate_ref, up_ref, out_ref = outs[:3]
    mix_outs = outs[3:]
    local_ff = owners * part
    local_width = out_ref.shape[1] // seqs
    for seq in range(seqs):
        start = 0
        for unit_ref in (gate_ref, up_ref):
            for owner in range(owners):
                place = (owner * seqs + seq) * part
                unit_ref[:, place : place + part] = reduced_ref[seq, :, start : start + part].astype(f32)
                start += part
        out_ref[:, seq * local_width : (seq + 1) * local_width] = reduced_ref[
            seq, :, start : start + local_width
        ].astype(f32)
        start += local_width
        for group in range(local_width // group_width):
            for mix_ref in mix_outs:
                place = seq * local_width + group * group_width
                mix_ref[:, place : place + group_width] = reduced_ref[seq, :, start : start + group_width].astype(f32)
                start += group_width


def laid_out(reduced, down_rows, group_width):
    seqs, share, total = reduced.shape
    owners = lax.axis_size(SR)
    width = share * owners
    steps = 4
    block = share // steps

    def rows_of(columns):
        return pl.BlockSpec((block, columns), lambda i: (i, 0))

    columns = [owners * down_rows] * 2 + [width] * 5
    return pl.pallas_call(
        functools.partial(layout_kernel, owners, down_rows // seqs, group_width),
        grid=(steps,),
        in_specs=[pl.BlockSpec((seqs, block, total), lambda i: (0, i, 0))],
        out_specs=[rows_of(count) for count in columns],
        out_shape=[jax.ShapeDtypeStruct((share, count), f32) for count in columns],
        compiler_params=pltpu.CompilerParams(vmem_limit_bytes=48 << 20),
        name="laid_out",
    )(reduced)


def share_columns(share):
    if lax.axis_size("seq") != 2:
        return lax.all_gather(share, "seq", axis=0)
    return in_order(share[None], swap(share)[None], 0)


def body(
    tokens,
    lengths,
    w_query,
    w_forget,
    w_input,
    w_gate_out,
    w_output,
    w_ffn_gate,
    w_ffn_up,
    w_ffn_down,
    norm_in,
    norm_mid,
    head_gain,
    gate_gap,
    cotangent,
):
    row_count, width = tokens.shape[1:]
    seqs = lax.axis_size("seq")
    owners = lax.axis_size(SR)
    seq_index = lax.axis_index("seq")
    owner_index = lax.axis_index(SR)
    share = w_query.shape[0]
    local_width = width // seqs
    local_heads = H // seqs
    group = min(4, local_heads)
    groups = local_heads // group
    down_rows = w_ffn_down.shape[0]
    part = down_rows // seqs
    local_ff = owners * part

    inputs = tokens[0].astype(f32)
    positions = seq_index * row_count + jnp.arange(row_count)
    valid_col = (positions < lengths[0]).astype(f32)[:, None]

    def gathered(value):
        return lax.all_gather(value, SR, axis=0, tiled=True)

    def owned(value):
        return lax.psum_scatter(value, SR, scatter_dimension=0, tiled=True)

    def my_columns(weight):
        return lax.dynamic_slice_in_dim(weight, seq_index * local_width, local_width, 1)

    def my_units(weight):
        shaped = weight.reshape(share, owners, seqs, part)
        return lax.dynamic_index_in_dim(shaped, seq_index, 2, keepdims=False).reshape(share, local_ff)

    gains = jnp.stack([norm_in, norm_mid, gate_gap, jnp.pad(head_gain, (0, share - head_gain.shape[0]))])
    gains = jnp.pad(gains.astype(f32), ((0, 4), (0, 0)))
    mix_weights = (w_query, w_forget, w_input, w_gate_out)
    fast = seqs == 2 and lax.axis_size("shard") == 4
    if fast:
        proj, normed, w_mix, w_out, gains = gathered_mixer(tokens[0], gains, mix_weights + (w_output,))
    else:
        gains = gathered(gains).reshape(owners, 8, share)
    gain_in = gains[:, 0].reshape(1, width)
    gain_mid = gains[:, 1].reshape(1, width)
    gap_full = gains[:, 2].reshape(1, width)
    gain_head = gains[:, 3, : head_gain.shape[0]].reshape(1, HD)
    gap = lax.dynamic_slice_in_dim(gap_full, seq_index * local_width, local_width, 1)
    scale_in = lax.rsqrt(jnp.mean(inputs * inputs, axis=-1, keepdims=True) + norm_eps)
    unit_in = inputs * scale_in
    if not fast:
        mix_share = jnp.stack([my_columns(w) for w in mix_weights], axis=1)
        mix_share = mix_share.reshape(share, 4, groups, group * HD).transpose(0, 2, 1, 3)
        w_mix = gathered(mix_share.reshape(share, 4 * local_width))
        w_out = gathered(w_output)
        normed = gather_tokens((unit_in * gain_in).astype(bf16))
        proj = matmul(normed, w_mix)

    w_gate_up = gathered(jnp.concatenate([my_units(w_ffn_gate), my_units(w_ffn_up)], axis=1))
    w_down = gathered(lax.dynamic_slice_in_dim(w_ffn_down, seq_index * part, part, 0))

    grad_out = cotangent[0].astype(f32)
    grad_ffn = gather_tokens((valid_col * grad_out).astype(bf16))
    branch_heads, states, mixed = mixer_forward(proj, gap, gain_head, group)
    branch_in = columns_to_tokens(branch_heads)
    hidden = inputs + valid_col * matmul(branch_in, w_out)

    scale_mid = lax.rsqrt(jnp.mean(hidden * hidden, axis=-1, keepdims=True) + norm_eps)
    unit_mid = hidden * scale_mid
    normed_mid = gather_tokens((unit_mid * gain_mid).astype(bf16))
    branch_all = gather_tokens(branch_in)
    normed_mid, branch_all = lax.optimization_barrier((normed_mid, branch_all))
    early_lefts = [value.T for value in (normed_mid, branch_all, normed)]
    gate_up = matmul(normed_mid, w_gate_up)
    gate_up, early_lefts = lax.optimization_barrier((gate_up, early_lefts))
    gate_vals = gate_up[:, :local_ff]
    up_vals = gate_up[:, local_ff:]
    gate_act = jax.nn.silu(gate_vals)
    inner = (gate_act * up_vals).astype(bf16)

    partial_out = matmul(inner, w_down)
    partial_out, grad_ffn = lax.optimization_barrier((partial_out, grad_ffn))
    ffn_out = scatter_tokens(partial_out)

    grad_inner = matmul_nt(grad_ffn, w_down)
    down_share = owned(matmul_tn(inner, grad_ffn).astype(bf16))
    grad_gate_vals = (grad_inner * up_vals * dsilu(gate_vals)).astype(bf16)
    grad_up_vals = (grad_inner * gate_act).astype(bf16)
    grad_gate_up = jnp.concatenate([grad_gate_vals, grad_up_vals], axis=1)
    lefts = early_lefts
    if fast:
        mid = matmul_nt(grad_gate_up, w_gate_up)
        own_mid = lax.dynamic_slice_in_dim(mid, seq_index * row_count, row_count, 0)
        other_mid = lax.dynamic_slice_in_dim(mid, (1 - seq_index) * row_count, row_count, 0).astype(bf16)
        middle = (own_mid, other_mid, hidden, cotangent[0], valid_col, gain_mid)
        mixer = (proj, gap, gain_head, states, mixed)
        reduced, small, input_grad = reduced_gradients(
            lefts, grad_gate_up, middle, mixer, w_out, w_mix, tokens[0], gain_in, group
        )
        head_share = lax.dynamic_slice_in_dim(small[3], owner_index * (HD // owners), HD // owners)
        grad_gate, grad_up, grad_output, *mix_all = laid_out(reduced, down_rows, group * HD)
    else:
        grad_normed_mid = scatter_tokens(matmul_nt(grad_gate_up, w_gate_up))
        grad_gain_mid = jnp.sum(grad_normed_mid * unit_mid, axis=0)
        grad_unit_mid = grad_normed_mid * gain_mid
        grad_hidden = grad_out + scale_mid * (
            grad_unit_mid - unit_mid * jnp.mean(grad_unit_mid * unit_mid, axis=-1, keepdims=True)
        )
        grad_branch = (valid_col * grad_hidden).astype(bf16)
        grad_branch_in = tokens_to_columns(matmul_nt(grad_branch, w_out).astype(bf16))
        small = jnp.zeros((owners, 8, share), f32).at[:, 1].set(grad_gain_mid.reshape(owners, share))
        grad_proj, grad_gap, grad_gain_head = mixer_backward(
            proj, gap, gain_head, states, mixed, grad_branch_in, group
        )
        grad_normed = scatter_tokens(matmul_nt(grad_proj, w_mix))
        grad_unit_in = grad_normed * gain_in
        grad_inputs = grad_hidden + scale_in * (
            grad_unit_in - unit_in * jnp.mean(grad_unit_in * unit_in, axis=-1, keepdims=True)
        )
        input_grad = grad_inputs.astype(bf16)
        rights = [grad_gate_up, tokens_to_columns(grad_branch), grad_proj]
        partial = jnp.concatenate([matmul(left, right).astype(bf16) for left, right in zip(lefts, rights)], axis=1)
        reduced = lax.all_gather(owned(partial), "seq", axis=0).astype(f32)
        small = small.at[:, 0].set(jnp.sum(grad_normed * unit_in, axis=0).reshape(owners, share))
        gap_placed = lax.dynamic_update_slice_in_dim(
            jnp.zeros((width,), f32), grad_gap.reshape(local_width), seq_index * local_width, 0
        )
        small = small.at[:, 2].set(gap_placed.reshape(owners, share))
        head_total = jnp.sum(grad_gain_head, axis=(0, 1))
        small = small.at[:, 3, : HD // owners].set(head_total.reshape(owners, -1))
        small = lax.dynamic_index_in_dim(lax.psum(small, ("seq",) + SR), owner_index, 0, keepdims=False)
        head_share = small[3, : HD // owners]
        ends = (2 * local_ff, 2 * local_ff + local_width)
        grad_units = reduced[:, :, : ends[0]].reshape(seqs, share, 2, owners, part).transpose(2, 1, 3, 0, 4)
        grad_gate, grad_up = grad_units.reshape(2, share, owners * down_rows)
        grad_output = reduced[:, :, ends[0] : ends[1]].transpose(1, 0, 2).reshape(share, width)
        mix_all = reduced[:, :, ends[1] :].reshape(seqs, share, groups, 4, group * HD)
        mix_all = mix_all.transpose(3, 1, 0, 2, 4).reshape(4, share, width)
    grad_down = share_columns(down_share).reshape(down_rows, width).astype(f32)
    layer_out = (hidden + valid_col * ffn_out).astype(bf16)[None]
    input_grad = input_grad[None]

    return (
        layer_out,
        input_grad,
        mix_all[0],
        mix_all[1],
        mix_all[2],
        mix_all[3],
        grad_output,
        grad_gate,
        grad_up,
        grad_down,
        small[0],
        small[1],
        head_share,
        small[2],
    )


def solution(mesh):
    rows = P(SR, None)
    vector = P(SR)
    by_token = P(SR, "seq", None)
    placed = (by_token, vector) + (rows,) * 8 + (vector,) * 4 + (by_token,)
    return jax.shard_map(
        body,
        mesh=mesh,
        in_specs=placed,
        out_specs=(by_token, by_token) + (rows,) * 8 + (vector,) * 4,
        check_vma=False,
    )
```

```python
import functools

import jax
import jax.numpy as jnp
from jax import lax
from jax.experimental import pallas as pl
from jax.experimental.pallas import tpu as pltpu
from jax.sharding import PartitionSpec as P

H = 16
HD = 128
BLK = 128
SR = ("shard", "rep")
MESH = pl.DeviceIdType.MESH

norm_eps = 1e-05
head_eps = 1e-06

f32 = jnp.float32
bf16 = jnp.bfloat16


def dsilu(values_in):
    sig_vals = jax.nn.sigmoid(values_in)
    return sig_vals * (1.0 + values_in * (1.0 - sig_vals))


def matmul(left, right):
    return jnp.dot(left, right, preferred_element_type=f32)


def matmul_nt(left, right):
    return lax.dot_general(left, right, (((1,), (1,)), ((), ())), preferred_element_type=f32)


def matmul_tn(left, right):
    return lax.dot_general(left, right, (((0,), (0,)), ((), ())), preferred_element_type=f32)


def block_sums(lower, values):
    high, low = split(values)
    return matmul(lower, high) + matmul(lower, low)


def split(values):
    high = values.astype(bf16)
    return high, (values - high.astype(f32)).astype(bf16)


def head_forward(proj, gap, group_width):
    proj_query = proj[:, :group_width]
    proj_forget = proj[:, group_width : 2 * group_width]
    proj_input = proj[:, 2 * group_width : 3 * group_width]
    proj_gate = proj[:, 3 * group_width :]
    sig_query = jax.nn.sigmoid(proj_query)
    queries = (proj_query * sig_query).astype(bf16).astype(f32)
    forget_sig = jax.nn.sigmoid(-proj_forget)
    key_full = gap * forget_sig
    keys = key_full.astype(bf16).astype(f32)
    log_decay = jnp.log1p(-key_full)
    values = proj_input.astype(bf16)
    return proj_query, proj_gate, sig_query, queries, forget_sig, key_full, keys, log_decay, values


def triangle(kind, dtype):
    rows = lax.broadcasted_iota(jnp.int32, (BLK, BLK), 0)
    cols = lax.broadcasted_iota(jnp.int32, (BLK, BLK), 1)
    return (rows >= cols if kind == "lower" else rows <= cols).astype(dtype)


def forward_kernel(heads, proj_ref, gap_ref, gain_ref, branch_ref, states_ref, mixed_ref, state):
    width = heads * HD

    @pl.when(pl.program_id(1) == 0)
    def _():
        state[...] = jnp.zeros_like(state)

    proj = proj_ref[...]
    _, proj_gate, _, queries, _, _, keys, log_decay, values = head_forward(proj, gap_ref[...], width)
    lower = triangle("lower", f32)
    cumul = block_sums(lower.astype(bf16), log_decay)
    grown = jnp.exp(cumul)
    query_dec, query_low = split(queries * grown)
    key_dec, key_low = split(keys * jnp.exp(-cumul))
    last = cumul[BLK - 1 : BLK, :]
    key_tail = (keys * jnp.exp(last - cumul)).astype(bf16)
    last_decay = jnp.exp(last)
    gate_act = proj_gate * jax.nn.sigmoid(proj_gate)
    gain = gain_ref[...]
    for head in range(heads):
        span = slice(head * HD, (head + 1) * HD)
        before = state[head]
        states_ref[0, head] = before
        scores = matmul_nt(query_low[:, span], key_dec[:, span]) + matmul_nt(query_dec[:, span], key_low[:, span])
        scores = (scores + matmul_nt(query_dec[:, span], key_dec[:, span])) * lower
        scores, scores_low = split(scores)
        mixed = matmul(scores_low, values[:, span]) + matmul(scores, values[:, span])
        mixed = mixed + matmul(query_dec[:, span], before.astype(bf16))
        mixed_ref[:, span] = mixed
        decay_col = jnp.transpose(jnp.broadcast_to(last_decay[:, span], (HD, HD)))
        state[head] = decay_col * before + matmul_tn(key_tail[:, span], values[:, span])
        scale = lax.rsqrt(jnp.mean(mixed * mixed, axis=-1, keepdims=True) + head_eps)
        branch_ref[:, span] = (mixed * scale * gain * gate_act[:, span]).astype(bf16)


def backward_block(heads, proj, gap, gain, states, mixed_all, grad_in, dstate, after):
    width = heads * HD
    proj_query, proj_gate, sig_query, queries, forget_sig, key_full, keys, log_decay, values = head_forward(
        proj, gap, width
    )
    lower = triangle("lower", f32)
    upper = triangle("upper", bf16)
    cumul = block_sums(lower.astype(bf16), log_decay)
    grown = jnp.exp(cumul)
    shrunk = jnp.exp(-cumul)
    last = cumul[BLK - 1 : BLK, :]
    tail = jnp.exp(last - cumul)
    last_decay = jnp.exp(last)
    query_dec = (queries * grown).astype(bf16)
    key_dec = (keys * shrunk).astype(bf16)
    key_tail = (keys * tail).astype(bf16)
    sig_gate = jax.nn.sigmoid(proj_gate)
    gate_act = proj_gate * sig_gate
    gate_slope = sig_gate * (1.0 + proj_gate * (1.0 - sig_gate))
    gain_sum = jnp.zeros((1, HD), f32)
    query_grads, key_grads, value_grads, gate_grads, ends = [], [], [], [], []
    for head in range(heads):
        span = slice(head * HD, (head + 1) * HD)
        before = states[head]
        before_low = before.astype(bf16)
        q_dec, k_dec, vals = query_dec[:, span], key_dec[:, span], values[:, span]
        scores = (matmul_nt(q_dec, k_dec) * lower).astype(bf16)
        mixed = mixed_all[:, span]
        scale = lax.rsqrt(jnp.mean(mixed * mixed, axis=-1, keepdims=True) + head_eps)
        unit = mixed * scale
        grad_b = grad_in[:, span]
        gate_grads.append(grad_b * unit * gain * gate_slope[:, span])
        grad_normed = grad_b * gate_act[:, span]
        gain_sum = gain_sum + jnp.sum(grad_normed * unit, axis=0, keepdims=True)
        grad_unit = grad_normed * gain
        grad_mixed = scale * (grad_unit - unit * jnp.mean(grad_unit * unit, axis=-1, keepdims=True))
        grad_low = grad_mixed.astype(bf16)
        down = dstate[head]
        down_low = down.astype(bf16)
        grad_scores = (matmul_nt(grad_low, vals) * lower).astype(bf16)
        value_grads.append(matmul_tn(scores, grad_low) + matmul(key_tail[:, span], down_low))
        grad_q = matmul(grad_scores, k_dec) + matmul_nt(grad_low, before_low)
        grad_k = matmul_tn(grad_scores, q_dec)
        grad_t = matmul_nt(vals, down_low)
        query_grads.append(grad_q * grown[:, span])
        key_grads.append(grad_k * shrunk[:, span] + grad_t * tail[:, span])
        ends.append(jnp.transpose(jnp.sum(down * after[head], axis=1, keepdims=True)))
        after[head] = before
        decay_col = jnp.transpose(jnp.broadcast_to(last_decay[:, span], (HD, HD)))
        dstate[head] = decay_col * down + matmul_tn(q_dec, grad_low)
    grad_queries = jnp.concatenate(query_grads, axis=1)
    grad_keys = jnp.concatenate(key_grads, axis=1)
    grad_values = jnp.concatenate(value_grads, axis=1)
    end = jnp.concatenate(ends, axis=1)
    grad_decay = block_sums(upper, queries * grad_queries - keys * grad_keys) + end
    grad_key_full = grad_keys - grad_decay / (1.0 - key_full)
    gap_sum = jnp.sum(grad_key_full * forget_sig, axis=0, keepdims=True)
    query_slope = sig_query * (1.0 + proj_query * (1.0 - sig_query))
    grads = (
        grad_queries * query_slope,
        -grad_key_full * gap * forget_sig * (1.0 - forget_sig),
        grad_values,
        jnp.concatenate(gate_grads, axis=1),
    )
    return [grad.astype(bf16) for grad in grads], gap_sum, gain_sum


def backward_kernel(
    heads, proj_ref, gap_ref, gain_ref, states_ref, mixed_ref, grad_ref, out_ref, gap_out, gain_out, dstate, after
):
    width = heads * HD

    @pl.when(pl.program_id(1) == 0)
    def _():
        dstate[...] = jnp.zeros_like(dstate)
        after[...] = jnp.zeros_like(after)
        gap_out[...] = jnp.zeros_like(gap_out)
        gain_out[...] = jnp.zeros_like(gain_out)

    states = [states_ref[0, head] for head in range(heads)]
    grads, gap_sum, gain_sum = backward_block(
        heads, proj_ref[...], gap_ref[...], gain_ref[...], states, mixed_ref[...], grad_ref[...].astype(f32), dstate, after
    )
    for kind, grad in enumerate(grads):
        out_ref[:, kind * width : (kind + 1) * width] = grad
    gap_out[...] += gap_sum
    gain_out[...] += gain_sum


def mixer_forward(proj, gap, gain, heads):
    tokens, total = proj.shape
    groups, blocks = total // (4 * heads * HD), tokens // BLK
    width = heads * HD
    return pl.pallas_call(
        functools.partial(forward_kernel, heads),
        grid=(groups, blocks),
        in_specs=[
            pl.BlockSpec((BLK, 4 * width), lambda g, b: (b, g)),
            pl.BlockSpec((1, width), lambda g, b: (0, g)),
            pl.BlockSpec((1, HD), lambda g, b: (0, 0)),
        ],
        out_specs=[
            pl.BlockSpec((BLK, width), lambda g, b: (b, g)),
            pl.BlockSpec((1, heads, HD, HD), lambda g, b: (b, g, 0, 0)),
            pl.BlockSpec((BLK, width), lambda g, b: (b, g)),
        ],
        out_shape=[
            jax.ShapeDtypeStruct((tokens, groups * width), bf16),
            jax.ShapeDtypeStruct((blocks, groups * heads, HD, HD), f32),
            jax.ShapeDtypeStruct((tokens, groups * width), f32),
        ],
        scratch_shapes=[pltpu.VMEM((heads, HD, HD), f32)],
        compiler_params=pltpu.CompilerParams(vmem_limit_bytes=48 << 20),
        name="mixer_forward",
    )(proj, gap, gain)


def mixer_backward(proj, gap, gain, states, mixed, grad, heads):
    tokens, total = proj.shape
    groups, blocks = total // (4 * heads * HD), tokens // BLK
    width = heads * HD
    return pl.pallas_call(
        functools.partial(backward_kernel, heads),
        grid=(groups, blocks),
        in_specs=[
            pl.BlockSpec((BLK, 4 * width), lambda g, b: (blocks - 1 - b, g)),
            pl.BlockSpec((1, width), lambda g, b: (0, g)),
            pl.BlockSpec((1, HD), lambda g, b: (0, 0)),
            pl.BlockSpec((1, heads, HD, HD), lambda g, b: (blocks - 1 - b, g, 0, 0)),
            pl.BlockSpec((BLK, width), lambda g, b: (blocks - 1 - b, g)),
            pl.BlockSpec((BLK, width), lambda g, b: (blocks - 1 - b, g)),
        ],
        out_specs=[
            pl.BlockSpec((BLK, 4 * width), lambda g, b: (blocks - 1 - b, g)),
            pl.BlockSpec((1, width), lambda g, b: (0, g)),
            pl.BlockSpec((1, 1, HD), lambda g, b: (g, 0, 0)),
        ],
        out_shape=[
            jax.ShapeDtypeStruct((tokens, total), bf16),
            jax.ShapeDtypeStruct((1, groups * width), f32),
            jax.ShapeDtypeStruct((groups, 1, HD), f32),
        ],
        scratch_shapes=[pltpu.VMEM((heads, HD, HD), f32), pltpu.VMEM((heads, HD, HD), f32)],
        compiler_params=pltpu.CompilerParams(vmem_limit_bytes=48 << 20),
        name="mixer_backward",
    )(proj, gap, gain, states, mixed, grad)


def swap(value):
    return lax.ppermute(value, "seq", [(0, 1), (1, 0)])


def in_order(own, other, axis):
    first = lax.axis_index("seq") == 0
    return jnp.concatenate([jnp.where(first, own, other), jnp.where(first, other, own)], axis=axis)


def gather_tokens(value):
    if lax.axis_size("seq") != 2:
        return lax.all_gather(value, "seq", axis=0, tiled=True)
    return in_order(value, swap(value), 0)


def scatter_tokens(partial):
    if lax.axis_size("seq") != 2:
        return lax.psum_scatter(partial.astype(bf16), "seq", scatter_dimension=0, tiled=True).astype(f32)
    rows = partial.shape[0] // 2
    me = lax.axis_index("seq")
    theirs = lax.dynamic_slice_in_dim(partial, (1 - me) * rows, rows, 0).astype(bf16)
    return lax.dynamic_slice_in_dim(partial, me * rows, rows, 0) + swap(theirs).astype(f32)


def columns_to_tokens(value):
    if lax.axis_size("seq") != 2:
        return lax.all_to_all(value, "seq", 0, 1, tiled=True)
    rows = value.shape[0] // 2
    me = lax.axis_index("seq")
    theirs = swap(lax.dynamic_slice_in_dim(value, (1 - me) * rows, rows, 0))
    return in_order(lax.dynamic_slice_in_dim(value, me * rows, rows, 0), theirs, 1)


def tokens_to_columns(value):
    if lax.axis_size("seq") != 2:
        return lax.all_to_all(value, "seq", 1, 0, tiled=True)
    cols = value.shape[1] // 2
    me = lax.axis_index("seq")
    theirs = swap(lax.dynamic_slice_in_dim(value, (1 - me) * cols, cols, 1))
    return in_order(lax.dynamic_slice_in_dim(value, me * cols, cols, 1), theirs, 0)


RING = 8
CORE_RING = 4
CHUNK = 256


def reduce_kernel(counts, heads, *refs):
    kinds = len(counts)
    lefts = refs[:kinds]
    (
        units_ref,
        own_mid,
        other_mid,
        hidden_ref,
        cotangent_ref,
        valid_ref,
        gain_mid_ref,
        wout_ref,
        proj_ref,
        gap_ref,
        gain_ref,
        states_ref,
        mixed_ref,
        mix_ref,
        tokens_ref,
        gain_in_ref,
        inner_ref,
        down_ref,
        out_ref,
        small_out,
        input_out,
        layer_out,
        core_out,
        core_in,
        pair_out,
        pair_in,
        sums,
        line_in,
        done,
        core_sems,
        pair_sems,
        line_send,
        line_recv,
        done_sems,
        got_sems,
        small_in,
        small_all,
        small_sems,
        columns,
        column_sems,
        grad_proj,
        proj_in,
        proj_sems,
        dstate,
        after,
        gap_acc,
        gain_acc,
        weights_in,
        weight_sems,
        kept_normed,
        sent_normed,
        got_normed,
        normed_sems,
        got_mid,
        mid_sems,
        grad_hidden,
        branch_ref,
        grad_ref,
        sent_heads,
        head_sems,
        mid_sum,
        inner_in,
        inner_sems,
        output_sems,
        load_sems,
    ) = refs[kinds:]
    rights = (units_ref, columns, grad_proj)
    total = sum(counts)
    planes, rows = sums.shape[1:3]
    seq = lax.axis_index("seq")
    shard = lax.axis_index("shard")
    plane = lax.axis_index("rep")
    core, pair = shard % 2, shard // 2
    other_core = {"shard": shard + 1 - 2 * core}
    other_pair = {"shard": (shard + 2) % 4}
    other_seq = {"seq": 1 - seq}
    below, above = {"rep": plane - 1}, {"rep": plane + 1}
    me = shard * planes + plane
    owners = small_all.shape[0]
    devices = small_in.shape[0]
    number = seq * owners + me

    def others():
        for step in range(1, devices):
            there = (number + step) % devices
            owner = there % owners
            yield step, owner, {"seq": there // owners, "shard": owner // planes, "rep": owner % planes}

    barrier = pltpu.get_barrier_semaphore()
    for _, _, device in others():
        pl.semaphore_signal(barrier, inc=1, device_id=device, device_id_type=MESH)
    pl.semaphore_wait(barrier, devices - 1)

    def remote(source, target, send, recv, device):
        return pltpu.make_async_remote_copy(
            src_ref=source, dst_ref=target, send_sem=send, recv_sem=recv, device_id=device, device_id_type=MESH
        )

    own_tokens, width = tokens_ref.shape
    local_width = columns.shape[1]
    group_width = heads * HD
    groups, blocks = local_width // group_width, grad_proj.shape[0] // BLK

    piece = weights_in.shape[1]
    pieces = width // piece

    def aligned(start, size):
        return pl.ds(pl.multiple_of(start, size), size)

    def mid_copy():
        return remote(sent_normed, got_mid, mid_sems.at[0], mid_sems.at[1], other_seq)

    def mid_turn():
        mid_copy().wait()
        mid_loads[1].wait()
        gain = gain_mid_ref[...]
        size = 64

        def part(index, total_mid):
            rows_at = aligned(index * size, size)
            values = hidden_ref[rows_at]
            scale = lax.rsqrt(jnp.mean(values * values, axis=-1, keepdims=True) + norm_eps)
            unit = values * scale
            grad = kept_normed[rows_at] + got_mid[rows_at].astype(f32)
            grad_unit = grad * gain
            moved = scale * (grad_unit - unit * jnp.mean(grad_unit * unit, axis=-1, keepdims=True))
            both = cotangent_ref[rows_at].astype(f32) + moved
            grad_hidden[rows_at] = both
            branch_ref[rows_at] = (valid_ref[rows_at] * both).astype(bf16)
            return total_mid + jnp.sum(grad * unit, axis=0, keepdims=True)

        mid_sum[...] = lax.fori_loop(0, own_tokens // size, part, jnp.zeros((1, width), f32))

    def wout_load(index):
        return pltpu.make_async_copy(
            wout_ref.at[aligned(index * piece, piece)],
            weights_in.at[index % 2, :, pl.ds(0, width)],
            weight_sems.at[index % 2],
        )

    def head_copy():
        place = grad_ref.at[aligned(seq * own_tokens, own_tokens)]
        return remote(sent_heads, place, head_sems.at[0], head_sems.at[1], other_seq)

    def heads_turn():
        def part(index, _):
            @pl.when(index + 1 < pieces)
            def _():
                wout_load(index + 1).start()

            wout_load(index).wait()
            grad = matmul_nt(branch_ref[...], weights_in[index % 2, :, :width]).astype(bf16)
            span = aligned((index % per_seq) * piece, piece)

            @pl.when(index // per_seq == seq)
            def _():
                grad_ref[aligned(seq * own_tokens, own_tokens), span] = grad

            @pl.when(index // per_seq != seq)
            def _():
                sent_heads[:, span] = grad

            return 0

        per_seq = local_width // piece
        lax.fori_loop(0, pieces, part, 0)
        head_copy().start()
        weight_load(0).start()

    def heads_end():
        head_copy().wait()
        for copy in column_moves():
            copy.start()

    def column_moves():
        mine = branch_ref.at[:, aligned(seq * local_width, local_width)]
        theirs = branch_ref.at[:, aligned((1 - seq) * local_width, local_width)]
        place = columns.at[aligned(seq * own_tokens, own_tokens)]
        kept = pltpu.make_async_copy(mine, place, column_sems.at[0])
        return kept, remote(theirs, place, column_sems.at[1], column_sems.at[2], other_seq)

    def proj_load(index):
        group, block = index // blocks, blocks - 1 - index % blocks
        source = proj_ref.at[aligned(block * BLK, BLK), aligned(group * 4 * group_width, 4 * group_width)]
        return pltpu.make_async_copy(source, proj_in.at[index % 2], proj_sems.at[index % 2])

    def mixer_turn(index):
        group, block = index // blocks, blocks - 1 - index % blocks
        rows_at, span = aligned(block * BLK, BLK), aligned(group * group_width, group_width)

        @pl.when(index + 1 < groups * blocks)
        def _():
            proj_load(index + 1).start()

        @pl.when(index % blocks == 0)
        def _():
            dstate[...] = jnp.zeros_like(dstate)
            after[...] = jnp.zeros_like(after)
            gap_acc[:, span] = jnp.zeros((1, group_width), f32)

        proj_load(index).wait()
        states = [states_ref[block, group * heads + head] for head in range(heads)]
        grads, gap_sum, gain_sum = backward_block(
            heads,
            proj_in[index % 2],
            gap_ref[:, span],
            gain_ref[...],
            states,
            mixed_ref[rows_at, span],
            grad_ref[rows_at, span].astype(f32),
            dstate,
            after,
        )
        for kind, grad in enumerate(grads):
            grad_proj[rows_at, aligned((group * 4 + kind) * group_width, group_width)] = grad
        gap_acc[:, span] += gap_sum
        gain_acc[...] += gain_sum

    def weight_load(index):
        return pltpu.make_async_copy(
            mix_ref.at[aligned(index * piece, piece)], weights_in.at[index % 2], weight_sems.at[index % 2]
        )

    def normed_copy():
        return remote(sent_normed, got_normed, normed_sems.at[0], normed_sems.at[1], other_seq)

    def normed_turn(index):
        @pl.when(index + 1 < pieces)
        def _():
            weight_load(index + 1).start()

        weight_load(index).wait()
        weight = weights_in[index % 2]
        span = aligned(index * piece, piece)
        sent_normed[:, span] = matmul_nt(grad_proj[aligned((1 - seq) * own_tokens, own_tokens)], weight).astype(bf16)
        kept_normed[:, span] = matmul_nt(grad_proj[aligned(seq * own_tokens, own_tokens)], weight)

        @pl.when(index == pieces - 1)
        def _():
            normed_copy().start()

    unit_pieces = down_ref.shape[0] // piece

    def unit_loads(index):
        span = aligned(index * piece, piece)
        return (
            pltpu.make_async_copy(inner_ref.at[:, span], inner_in.at[index % 2], inner_sems.at[index % 2]),
            pltpu.make_async_copy(
                down_ref.at[span], weights_in.at[index % 2, :, pl.ds(0, width)], weight_sems.at[index % 2]
            ),
        )

    def output_copy():
        return remote(sent_normed, got_mid, output_sems.at[0], output_sems.at[1], other_seq)

    def output_turn(index):
        @pl.when(index == 0)
        def _():
            for copy in unit_loads(0):
                copy.start()
            kept_normed[...] = jnp.zeros_like(kept_normed)
            grad_hidden[...] = jnp.zeros_like(grad_hidden)

        @pl.when(index + 1 < unit_pieces)
        def _():
            for copy in unit_loads(index + 1):
                copy.start()

        for copy in unit_loads(index):
            copy.wait()
        weight = weights_in[index % 2, :, :width]
        for total_ref, which in ((grad_hidden, 1 - seq), (kept_normed, seq)):
            total_ref[...] += matmul(inner_in[index % 2, aligned(which * own_tokens, own_tokens)], weight)

        @pl.when(index == unit_pieces - 1)
        def _():
            sent_normed[...] = grad_hidden[...].astype(bf16)
            output_copy().start()

    def output_end():
        output_copy().wait()
        size = 64

        def part(index, _):
            rows_at = aligned(index * size, size)
            both = kept_normed[rows_at] + got_mid[rows_at].astype(f32)
            layer_out[rows_at] = (hidden_ref[rows_at] + valid_ref[rows_at] * both).astype(bf16)
            return 0

        lax.fori_loop(0, own_tokens // size, part, 0)

    def input_turn():
        normed_copy().wait()
        gain = gain_in_ref[...]
        size = 64

        def part(index, total_in):
            rows_at = aligned(index * size, size)
            values = tokens_ref[rows_at].astype(f32)
            scale = lax.rsqrt(jnp.mean(values * values, axis=-1, keepdims=True) + norm_eps)
            unit = values * scale
            grad = kept_normed[rows_at] + got_normed[rows_at].astype(f32)
            grad_unit = grad * gain
            moved = scale * (grad_unit - unit * jnp.mean(grad_unit * unit, axis=-1, keepdims=True))
            input_out[rows_at] = (grad_hidden[rows_at] + moved).astype(bf16)
            return total_in + jnp.sum(grad * unit, axis=0, keepdims=True)

        total_in = lax.fori_loop(0, own_tokens // size, part, jnp.zeros((1, width), f32))
        small_all[...] = jnp.zeros_like(small_all)
        for owner in range(owners):
            small_all[owner, 1:2, :] = mid_sum[:, owner * rows : (owner + 1) * rows]
            small_all[owner, 0:1, :] = total_in[:, owner * rows : (owner + 1) * rows]
            small_all[owner, 3:4, :] = gain_acc[...]
        first_owner = seq * (local_width // rows)
        for index in range(local_width // rows):
            small_all[first_owner + index, 2:3, :] = gap_acc[:, index * rows : (index + 1) * rows]
        for copy in small_copies:
            copy.start()

    small_copies = [
        remote(small_all.at[owner], small_in.at[number], small_sems.at[0, step], small_sems.at[1, step], device)
        for step, owner, device in others()
    ]
    gain_acc[...] = jnp.zeros_like(gain_acc)
    proj_load(0).start()
    wout_load(0).start()
    mid_loads = (
        pltpu.make_async_copy(other_mid, sent_normed, load_sems.at[0]),
        pltpu.make_async_copy(own_mid, kept_normed, load_sems.at[1]),
    )
    for copy in mid_loads:
        copy.start()
    mid_loads[0].wait()
    mid_copy().start()

    def core_copy(chunk):
        slot = chunk % CORE_RING
        return remote(
            core_out.at[slot], core_in.at[slot], core_sems.at[0, slot], core_sems.at[1, slot], other_core
        )

    def pair_copy(chunk):
        sent, got = chunk % CORE_RING, chunk % RING
        return remote(
            pair_out.at[sent], pair_in.at[got], pair_sems.at[0, sent], pair_sems.at[1, got], other_pair
        )

    def line_copy(way, step, slot, target):
        return remote(
            sums.at[slot, target],
            line_in.at[way, step - 1, slot],
            line_send.at[way, step - 1, slot],
            line_recv.at[way, step - 1, slot],
            above if way else below,
        )

    def done_copies(chunk):
        slot = chunk % RING
        place = out_ref.at[seq, :, pl.ds(pl.multiple_of(chunk * CHUNK, CHUNK), CHUNK)]
        kept = pltpu.make_async_copy(done.at[slot], place, done_sems.at[1, slot])
        sent = remote(done.at[slot], place, done_sems.at[0, slot], got_sems.at[chunk], other_seq)
        return kept, sent

    def product(kind, chunk, half, which):
        first = (half * 2 + which) * planes * rows
        left = lefts[kind][pl.ds(pl.multiple_of(first, planes * rows), planes * rows), :]
        start = (chunk - sum(counts[:kind])) * CHUNK
        return matmul(left, rights[kind][:, pl.ds(pl.multiple_of(start, CHUNK), CHUNK)])

    def line_target(way, step):
        return plane + planes - step if way else plane - planes + step

    def sends(way, step):
        return plane < step if way else plane >= planes - step

    def receives(way, step):
        return jnp.logical_and(plane > 0, plane <= step) if way else jnp.logical_and(plane < planes - 1, plane >= planes - step - 1)

    def front(kind, chunk):
        slot = chunk % CORE_RING

        @pl.when(chunk >= CORE_RING)
        def _():
            core_copy(chunk).wait_send()

        for half in range(2):
            core_out[slot, half] = product(kind, chunk, half, 1 - core).astype(bf16)
        core_copy(chunk).start()

    def middle(kind, chunk):
        slot, core_slot = chunk % RING, chunk % CORE_RING

        @pl.when(chunk >= CORE_RING)
        def _():
            pair_copy(chunk).wait_send()

        theirs = product(kind, chunk, 1 - pair, core)
        mine = product(kind, chunk, pair, core)
        core_copy(chunk).wait_recv()
        pair_out[core_slot] = (theirs + core_in[core_slot, 1 - pair].astype(f32)).astype(bf16)
        pair_copy(chunk).start()
        mine = mine + core_in[core_slot, pair].astype(f32)
        sums[slot] = mine.astype(bf16).reshape(planes, rows, CHUNK)

    def line_start(chunk, step):
        slot = chunk % RING
        for way in range(2):

            @pl.when(sends(way, step))
            def _(way=way):
                target = line_target(way, step)
                if step > 1:

                    @pl.when(receives(way, step - 1))
                    def _():
                        line_copy(way, step - 1, slot, 0).wait_recv()
                        got = line_in[way, step - 2, slot].astype(f32)
                        sums[slot, target] = (sums[slot, target].astype(f32) + got).astype(bf16)

                line_copy(way, step, slot, target).start()

    def pair_done(chunk):
        slot = chunk % RING
        pair_copy(chunk).wait_recv()
        got = pair_in[slot].reshape(planes, rows, CHUNK).astype(f32)
        sums[slot] = (sums[slot].astype(f32) + got).astype(bf16)
        line_start(chunk, 1)

    def finish(chunk):
        slot = chunk % RING
        kept, sent = done_copies(chunk)

        @pl.when(chunk >= RING)
        def _():
            kept.wait()
            sent.wait_send()

        last = planes - 1
        for way in range(2):

            @pl.when(receives(way, last))
            def _(way=way):
                line_copy(way, last, slot, 0).wait_recv()
                got = line_in[way, last - 1, slot].astype(f32)
                sums[slot, plane] = (sums[slot, plane].astype(f32) + got).astype(bf16)

        done[slot] = sums[slot, plane]
        kept.start()
        sent.start()
        for way in range(2):
            for step in range(1, planes):

                @pl.when(sends(way, step))
                def _(way=way, step=step):
                    line_copy(way, step, slot, 0).wait_send()

    def received(chunk, _):
        done_copies(chunk)[1].wait_recv()
        return 0

    later = [(pair_done, 3)] + [
        (functools.partial(line_start, step=step), 2 + step) for step in range(2, planes)
    ] + [(finish, 2 + planes)]
    mid_at, mixer_at = 6, 10
    normed_at = mixer_at + groups * blocks
    assert normed_at + pieces // 2 <= counts[0] and unit_pieces + 2 <= counts[-1]
    first = 0
    for kind, count in enumerate(counts):

        def step(turn, _, kind=kind, first=first):
            front(kind, turn)
            if kind == 0:
                pl.when(turn >= 1)(lambda: middle(0, turn - 1))
            else:
                pl.when(turn == first)(lambda: middle(kind - 1, turn - 1))
                pl.when(turn > first)(lambda: middle(kind, turn - 1))
            if kind == 0:
                pl.when(turn == mid_at)(mid_turn)
                pl.when(turn == mid_at + 1)(heads_turn)
                pl.when(turn == mixer_at)(heads_end)
                inside = jnp.logical_and(turn >= mixer_at, turn < normed_at)
                pl.when(inside)(lambda: mixer_turn(turn - mixer_at))

                @pl.when(jnp.logical_and(turn >= normed_at, turn < normed_at + pieces // 2))
                def _():
                    normed_turn(2 * (turn - normed_at))
                    normed_turn(2 * (turn - normed_at) + 1)

            elif kind == kinds - 1:
                pl.when(turn == first + 1)(input_turn)
                inside = jnp.logical_and(turn >= first + 2, turn < first + 2 + unit_pieces)
                pl.when(inside)(lambda: output_turn(turn - first - 2))
            for act, lag in later:
                pl.when(turn >= lag)(lambda act=act, lag=lag: act(turn - lag))
            return 0

        if kind == 1:
            for copy in column_moves():
                copy.wait()
        lax.fori_loop(first, first + count, step, 0)
        first += count

    def drain(turn, _):
        pl.when(turn == total)(lambda: middle(kinds - 1, turn - 1))
        for act, lag in later:
            pl.when(turn - lag < total)(lambda act=act, lag=lag: act(turn - lag))
        return 0

    lax.fori_loop(total, total + later[-1][1], drain, 0)
    for chunk in range(total - RING, total):
        slot = chunk % RING
        if chunk >= total - CORE_RING:
            core_copy(chunk).wait_send()
            pair_copy(chunk).wait_send()
        kept, sent = done_copies(chunk)
        kept.wait()
        sent.wait_send()
    lax.fori_loop(0, total, received, 0)
    output_end()
    small_in[number] = small_all[me]
    for copy in small_copies:
        copy.wait()
    small_out[...] = jnp.sum(small_in[...], axis=0)


def reduced_gradients(lefts, grad_units, middle, mixer, w_out, w_mix, tokens, gain_in, inner, w_down, heads):
    proj, gap, gain, states, mixed = mixer
    own_tokens, width = tokens.shape
    local_width = mixed.shape[1]
    counts = [columns // CHUNK for columns in (grad_units.shape[1], local_width, proj.shape[1])]
    planes = lax.axis_size("rep")
    rows = lefts[0].shape[0] // lax.axis_size(SR)
    block = planes * rows
    owners = lax.axis_size(SR)
    devices = lax.axis_size(("seq",) + SR)
    vmem = pl.BlockSpec(memory_space=pltpu.VMEM)
    anywhere = pl.BlockSpec(memory_space=pl.ANY)
    return pl.pallas_call(
        functools.partial(reduce_kernel, counts, heads),
        in_specs=[vmem] * 4 + [anywhere] * 2 + [vmem] * 4 + [anywhere] * 2 + [vmem] * 4 + [anywhere] + [vmem] * 2 + [anywhere] * 2,
        out_specs=[anywhere, vmem, vmem, vmem],
        out_shape=[
            jax.ShapeDtypeStruct((2, rows, sum(counts) * CHUNK), bf16),
            jax.ShapeDtypeStruct((8, rows), f32),
            jax.ShapeDtypeStruct((own_tokens, width), bf16),
            jax.ShapeDtypeStruct((own_tokens, width), bf16),
        ],
        scratch_shapes=[
            pltpu.VMEM((CORE_RING, 2, block, CHUNK), bf16),
            pltpu.VMEM((CORE_RING, 2, block, CHUNK), bf16),
            pltpu.VMEM((CORE_RING, block, CHUNK), bf16),
            pltpu.VMEM((RING, block, CHUNK), bf16),
            pltpu.VMEM((RING, planes, rows, CHUNK), bf16),
            pltpu.VMEM((2, planes - 1, RING, rows, CHUNK), bf16),
            pltpu.VMEM((RING, rows, CHUNK), bf16),
            pltpu.SemaphoreType.DMA((2, CORE_RING)),
            pltpu.SemaphoreType.DMA((2, RING)),
            pltpu.SemaphoreType.DMA((2, planes - 1, RING)),
            pltpu.SemaphoreType.DMA((2, planes - 1, RING)),
            pltpu.SemaphoreType.DMA((2, RING)),
            pltpu.SemaphoreType.DMA((sum(counts),)),
            pltpu.VMEM((devices, 8, rows), f32),
            pltpu.VMEM((owners, 8, rows), f32),
            pltpu.SemaphoreType.DMA((2, devices)),
            pltpu.VMEM((2 * own_tokens, local_width), bf16),
            pltpu.SemaphoreType.DMA((3,)),
            pltpu.VMEM(proj.shape, bf16),
            pltpu.VMEM((2, BLK, 4 * heads * HD), f32),
            pltpu.SemaphoreType.DMA((2,)),
            pltpu.VMEM((heads, HD, HD), f32),
            pltpu.VMEM((heads, HD, HD), f32),
            pltpu.VMEM((1, local_width), f32),
            pltpu.VMEM((1, HD), f32),
            pltpu.VMEM((2, CHUNK, proj.shape[1]), bf16),
            pltpu.SemaphoreType.DMA((2,)),
            pltpu.VMEM((own_tokens, width), f32),
            pltpu.VMEM((own_tokens, width), bf16),
            pltpu.VMEM((own_tokens, width), bf16),
            pltpu.SemaphoreType.DMA((2,)),
            pltpu.VMEM((own_tokens, width), bf16),
            pltpu.SemaphoreType.DMA((2,)),
            pltpu.VMEM((own_tokens, width), f32),
            pltpu.VMEM((own_tokens, width), bf16),
            pltpu.VMEM((2 * own_tokens, local_width), bf16),
            pltpu.VMEM((own_tokens, local_width), bf16),
            pltpu.SemaphoreType.DMA((2,)),
            pltpu.VMEM((1, width), f32),
            pltpu.VMEM((2, 2 * own_tokens, CHUNK), bf16),
            pltpu.SemaphoreType.DMA((2,)),
            pltpu.SemaphoreType.DMA((2,)),
            pltpu.SemaphoreType.DMA((2,)),
        ],
        compiler_params=pltpu.CompilerParams(
            collective_id=0, has_side_effects=True, vmem_limit_bytes=62 << 20
        ),
        name="reduced_gradients",
    )(*lefts, grad_units, *middle, w_out, proj, gap, gain, states, mixed, w_mix, tokens, gain_in, inner, w_down)


def gather_kernel(
    tokens_ref,
    gains_ref,
    w_query,
    w_forget,
    w_input,
    w_gate_out,
    w_output,
    proj_ref,
    normed_ref,
    mix_ref,
    out_ref,
    all_gains_ref,
    pieces,
    all_tokens,
    normed,
    all_gains,
    products,
    load_sems,
    token_sems,
    gain_sems,
    line_send,
    line_recv,
    pair_sems,
    core_sems,
    write_sems,
    half_sems,
    last_sems,
):
    total, owners, rows = pieces.shape[:3]
    seqs, own_tokens, width = all_tokens.shape
    local_width = width // seqs
    out_count = local_width // CHUNK
    group_width = mix_ref.shape[2] // 4 // (local_width // (4 * HD))
    planes = lax.axis_size("rep")
    seq = lax.axis_index("seq")
    shard = lax.axis_index("shard")
    plane = lax.axis_index("rep")
    core, pair = shard % 2, shard // 2
    me = shard * planes + plane
    other_core = {"shard": shard + 1 - 2 * core}
    other_pair = {"shard": (shard + 2) % 4}
    other_seq = {"seq": 1 - seq}
    below, above = {"rep": plane - 1}, {"rep": plane + 1}

    loads = []
    per_group = group_width // CHUNK
    for chunk in range(total):
        if chunk < out_count:
            source, start = w_output, chunk * CHUNK
        else:
            group, rest = divmod(chunk - out_count, 4 * per_group)
            kind, part = divmod(rest, per_group)
            source = (w_query, w_forget, w_input, w_gate_out)[kind]
            start = group * group_width + part * CHUNK
        start = pl.multiple_of(seq * local_width + start, CHUNK)
        loads.append(
            pltpu.make_async_copy(source.at[:, pl.ds(start, CHUNK)], pieces.at[chunk, me], load_sems.at[chunk])
        )
    for load in loads:
        load.start()

    def others():
        for step in range(1, owners):
            number = (me + step) % owners
            yield step, {"shard": number // planes, "rep": number % planes}

    barrier = pltpu.get_barrier_semaphore()
    for _, device in others():
        pl.semaphore_signal(barrier, inc=1, device_id=device, device_id_type=MESH)
    pl.semaphore_signal(barrier, inc=1, device_id=other_seq, device_id_type=MESH)
    pl.semaphore_wait(barrier, owners)

    def remote(source, target, send, recv, device):
        return pltpu.make_async_remote_copy(
            src_ref=source, dst_ref=target, send_sem=send, recv_sem=recv, device_id=device, device_id_type=MESH
        )

    token_copy = remote(tokens_ref, all_tokens.at[seq], token_sems.at[0], token_sems.at[1], other_seq)
    token_copy.start()
    gain_copies = [
        remote(gains_ref, all_gains.at[me], gain_sems.at[0, step], gain_sems.at[1, step], device)
        for step, device in others()
    ]
    for copy in gain_copies:
        copy.start()

    def line_copy(way, step, chunk, owner):
        slot = chunk % RING
        return remote(
            pieces.at[chunk, owner],
            pieces.at[chunk, owner],
            line_send.at[way, step - 1, slot],
            line_recv.at[way, step - 1, slot],
            above if way else below,
        )

    def block(which_pair):
        return pl.ds((which_pair * 2 + core) * planes, planes)

    def pair_copy(chunk):
        slot = chunk % RING
        place = pieces.at[chunk, block(pair)]
        return remote(place, place, pair_sems.at[0, slot], pair_sems.at[1, slot], other_pair)

    def core_copy(chunk, which):
        slot = chunk % RING
        place = pieces.at[chunk, block(pair if which == 0 else 1 - pair)]
        return remote(place, place, core_sems.at[0, which, slot], core_sems.at[1, which, slot], other_core)

    def sends(way, step):
        if way:
            return jnp.logical_and(plane < planes - 1, plane - (step - 1) >= 0)
        return jnp.logical_and(plane > 0, plane + (step - 1) <= planes - 1)

    def receives(way, step):
        return plane - step >= 0 if way else plane + step <= planes - 1

    def line(chunk, step):
        for way in range(2):
            if step > 1:

                @pl.when(receives(way, step - 1))
                def _(way=way):
                    line_copy(way, step - 1, chunk, me).wait_recv()

            if step < planes:

                @pl.when(sends(way, step))
                def _(way=way):
                    line_copy(way, step, chunk, me - (step - 1) if way else me + (step - 1)).start()

    def first(chunk):
        slot = chunk
        pltpu.make_async_copy(pieces.at[chunk, me], pieces.at[chunk, me], load_sems.at[slot]).wait()
        line(chunk, 1)

    def across(chunk):
        line(chunk, planes)
        pair_copy(chunk).start()
        core_copy(chunk, 0).start()

    def to_core(chunk):
        pair_copy(chunk).wait_recv()
        core_copy(chunk, 1).start()

    def writes(chunk):
        slot = chunk % RING

        def mix_writes():
            span = pl.ds(pl.multiple_of((chunk - out_count) * CHUNK, CHUNK), CHUNK)
            return (
                pltpu.make_async_copy(pieces.at[chunk], mix_ref.at[:, :, span], write_sems.at[0, slot]),
                pltpu.make_async_copy(products.at[slot], proj_ref.at[:, span], write_sems.at[1, slot]),
            )

        def out_writes():
            place = out_ref.at[:, :, pl.ds(pl.multiple_of(seq * local_width + chunk * CHUNK, CHUNK), CHUNK)]
            return (
                pltpu.make_async_copy(pieces.at[chunk], place, half_sems.at[2, slot]),
                remote(pieces.at[chunk], place, half_sems.at[0, slot], half_sems.at[1, slot], other_seq),
            )

        return mix_writes, out_writes

    def finish(chunk):
        slot = chunk % RING
        core_copy(chunk, 0).wait_recv()
        core_copy(chunk, 1).wait_recv()
        mix_writes, out_writes = writes(chunk)

        @pl.when(chunk >= out_count + RING)
        def _():
            written(chunk - RING)

        @pl.when(chunk >= out_count)
        def _():
            weight = pieces[chunk].reshape(owners * rows, CHUNK)
            for half in range(seqs):
                products[slot, half * own_tokens : (half + 1) * own_tokens] = matmul(normed[half], weight)
            for copy in mix_writes():
                copy.start()

        @pl.when(chunk < out_count)
        def _():
            for copy in out_writes():
                copy.start()

        pair_copy(chunk).wait_send()
        core_copy(chunk, 0).wait_send()
        core_copy(chunk, 1).wait_send()
        for way in range(2):
            for step in range(1, planes):

                @pl.when(sends(way, step))
                def _(way=way, step=step):
                    line_copy(way, step, chunk, me).wait_send()

    def written(chunk):
        for copy in writes(chunk)[0]():
            copy.wait()

    def normalize():
        all_tokens[seq] = tokens_ref[...]
        all_gains[me] = gains_ref[...]
        token_copy.wait_recv()
        for copy in gain_copies:
            copy.wait_recv()
        gain = jnp.concatenate([all_gains[owner, 0:1, :] for owner in range(owners)], axis=1)
        size = 64
        per = own_tokens // size

        def part(index, _):
            span = pl.ds((index % per) * size, size)
            values = all_tokens[index // per, span].astype(f32)
            scale = lax.rsqrt(jnp.mean(values * values, axis=-1, keepdims=True) + norm_eps)
            normed[index // per, span] = (values * scale * gain).astype(bf16)
            return 0

        lax.fori_loop(0, seqs * per, part, 0)
        pltpu.make_async_copy(normed, normed_ref, last_sems.at[0]).start()
        pltpu.make_async_copy(all_gains, all_gains_ref, last_sems.at[1]).start()

    acts = [(first, 0)] + [(functools.partial(line, step=step), step - 1) for step in range(2, planes)]
    acts += [(across, planes - 1), (to_core, planes + 1), (finish, planes + 2)]
    last_lag = acts[-1][1]

    def turn_over(turn, _):
        pl.when(turn == last_lag - 1)(normalize)
        for act, lag in acts:
            inside = jnp.logical_and(turn >= lag, turn - lag < total)
            pl.when(inside)(lambda act=act, lag=lag: act(turn - lag))
        return 0

    lax.fori_loop(0, total + last_lag, turn_over, 0)

    def end(chunk, _):
        written(chunk)
        return 0

    lax.fori_loop(total - RING, total, end, 0)
    for chunk in range(out_count):
        for copy in writes(chunk)[1]():
            copy.wait()
    token_copy.wait_send()
    for copy in gain_copies:
        copy.wait_send()
    pltpu.make_async_copy(normed, normed_ref, last_sems.at[0]).wait()
    pltpu.make_async_copy(all_gains, all_gains_ref, last_sems.at[1]).wait()


def gathered_mixer(tokens, gains, weights):
    own_tokens, width = tokens.shape
    rows = weights[0].shape[0]
    seqs, planes = lax.axis_size("seq"), lax.axis_size("rep")
    owners = lax.axis_size(SR)
    local_width = width // seqs
    total = 5 * local_width // CHUNK
    vmem = pl.BlockSpec(memory_space=pltpu.VMEM)
    anywhere = pl.BlockSpec(memory_space=pl.ANY)
    proj, normed, mix, out, all_gains = pl.pallas_call(
        gather_kernel,
        in_specs=[vmem, vmem] + [anywhere] * 5,
        out_specs=[anywhere] * 5,
        out_shape=[
            jax.ShapeDtypeStruct((seqs * own_tokens, 4 * local_width), f32),
            jax.ShapeDtypeStruct((seqs, own_tokens, width), bf16),
            jax.ShapeDtypeStruct((owners, rows, 4 * local_width), bf16),
            jax.ShapeDtypeStruct((owners, rows, width), bf16),
            jax.ShapeDtypeStruct((owners,) + gains.shape, f32),
        ],
        scratch_shapes=[
            pltpu.VMEM((total, owners, rows, CHUNK), bf16),
            pltpu.VMEM((seqs, own_tokens, width), bf16),
            pltpu.VMEM((seqs, own_tokens, width), bf16),
            pltpu.VMEM((owners,) + gains.shape, f32),
            pltpu.VMEM((RING, seqs * own_tokens, CHUNK), f32),
            pltpu.SemaphoreType.DMA((total,)),
            pltpu.SemaphoreType.DMA((2,)),
            pltpu.SemaphoreType.DMA((2, owners)),
            pltpu.SemaphoreType.DMA((2, planes - 1, RING)),
            pltpu.SemaphoreType.DMA((2, planes - 1, RING)),
            pltpu.SemaphoreType.DMA((2, RING)),
            pltpu.SemaphoreType.DMA((2, 2, RING)),
            pltpu.SemaphoreType.DMA((2, RING)),
            pltpu.SemaphoreType.DMA((3, RING)),
            pltpu.SemaphoreType.DMA((2,)),
        ],
        compiler_params=pltpu.CompilerParams(collective_id=1, has_side_effects=True, vmem_limit_bytes=56 << 20),
        name="gathered_mixer",
    )(tokens, gains, *weights)
    normed = normed.reshape(seqs * own_tokens, width)
    return proj, normed, mix.reshape(width, 4 * local_width), out.reshape(width, width), all_gains


def layout_kernel(owners, part, group_width, reduced_ref, *outs):
    seqs = reduced_ref.shape[0]
    gate_ref, up_ref, out_ref = outs[:3]
    mix_outs = outs[3:]
    local_ff = owners * part
    local_width = out_ref.shape[1] // seqs
    for seq in range(seqs):
        start = 0
        for unit_ref in (gate_ref, up_ref):
            for owner in range(owners):
                place = (owner * seqs + seq) * part
                unit_ref[:, place : place + part] = reduced_ref[seq, :, start : start + part].astype(f32)
                start += part
        out_ref[:, seq * local_width : (seq + 1) * local_width] = reduced_ref[
            seq, :, start : start + local_width
        ].astype(f32)
        start += local_width
        for group in range(local_width // group_width):
            for mix_ref in mix_outs:
                place = seq * local_width + group * group_width
                mix_ref[:, place : place + group_width] = reduced_ref[seq, :, start : start + group_width].astype(f32)
                start += group_width


def laid_out(reduced, down_rows, group_width):
    seqs, share, total = reduced.shape
    owners = lax.axis_size(SR)
    width = share * owners
    steps = 4
    block = share // steps

    def rows_of(columns):
        return pl.BlockSpec((block, columns), lambda i: (i, 0))

    columns = [owners * down_rows] * 2 + [width] * 5
    return pl.pallas_call(
        functools.partial(layout_kernel, owners, down_rows // seqs, group_width),
        grid=(steps,),
        in_specs=[pl.BlockSpec((seqs, block, total), lambda i: (0, i, 0))],
        out_specs=[rows_of(count) for count in columns],
        out_shape=[jax.ShapeDtypeStruct((share, count), f32) for count in columns],
        compiler_params=pltpu.CompilerParams(vmem_limit_bytes=48 << 20),
        name="laid_out",
    )(reduced)


def share_columns(share):
    if lax.axis_size("seq") != 2:
        return lax.all_gather(share, "seq", axis=0)
    return in_order(share[None], swap(share)[None], 0)


def body(
    tokens,
    lengths,
    w_query,
    w_forget,
    w_input,
    w_gate_out,
    w_output,
    w_ffn_gate,
    w_ffn_up,
    w_ffn_down,
    norm_in,
    norm_mid,
    head_gain,
    gate_gap,
    cotangent,
):
    row_count, width = tokens.shape[1:]
    seqs = lax.axis_size("seq")
    owners = lax.axis_size(SR)
    seq_index = lax.axis_index("seq")
    owner_index = lax.axis_index(SR)
    share = w_query.shape[0]
    local_width = width // seqs
    local_heads = H // seqs
    group = min(4, local_heads)
    groups = local_heads // group
    down_rows = w_ffn_down.shape[0]
    part = down_rows // seqs
    local_ff = owners * part

    inputs = tokens[0].astype(f32)
    positions = seq_index * row_count + jnp.arange(row_count)
    valid_col = (positions < lengths[0]).astype(f32)[:, None]

    def gathered(value):
        return lax.all_gather(value, SR, axis=0, tiled=True)

    def owned(value):
        return lax.psum_scatter(value, SR, scatter_dimension=0, tiled=True)

    def my_columns(weight):
        return lax.dynamic_slice_in_dim(weight, seq_index * local_width, local_width, 1)

    def my_units(weight):
        shaped = weight.reshape(share, owners, seqs, part)
        return lax.dynamic_index_in_dim(shaped, seq_index, 2, keepdims=False).reshape(share, local_ff)

    gains = jnp.stack([norm_in, norm_mid, gate_gap, jnp.pad(head_gain, (0, share - head_gain.shape[0]))])
    gains = jnp.pad(gains.astype(f32), ((0, 4), (0, 0)))
    mix_weights = (w_query, w_forget, w_input, w_gate_out)
    fast = seqs == 2 and lax.axis_size("shard") == 4
    if fast:
        proj, normed, w_mix, w_out, gains = gathered_mixer(tokens[0], gains, mix_weights + (w_output,))
    else:
        gains = gathered(gains).reshape(owners, 8, share)
    gain_in = gains[:, 0].reshape(1, width)
    gain_mid = gains[:, 1].reshape(1, width)
    gap_full = gains[:, 2].reshape(1, width)
    gain_head = gains[:, 3, : head_gain.shape[0]].reshape(1, HD)
    gap = lax.dynamic_slice_in_dim(gap_full, seq_index * local_width, local_width, 1)
    scale_in = lax.rsqrt(jnp.mean(inputs * inputs, axis=-1, keepdims=True) + norm_eps)
    unit_in = inputs * scale_in
    if not fast:
        mix_share = jnp.stack([my_columns(w) for w in mix_weights], axis=1)
        mix_share = mix_share.reshape(share, 4, groups, group * HD).transpose(0, 2, 1, 3)
        w_mix = gathered(mix_share.reshape(share, 4 * local_width))
        w_out = gathered(w_output)
        normed = gather_tokens((unit_in * gain_in).astype(bf16))
        proj = matmul(normed, w_mix)

    w_gate_up = gathered(jnp.concatenate([my_units(w_ffn_gate), my_units(w_ffn_up)], axis=1))
    w_down = gathered(lax.dynamic_slice_in_dim(w_ffn_down, seq_index * part, part, 0))

    grad_out = cotangent[0].astype(f32)
    grad_ffn = gather_tokens((valid_col * grad_out).astype(bf16))
    branch_heads, states, mixed = mixer_forward(proj, gap, gain_head, group)
    branch_in = columns_to_tokens(branch_heads)
    hidden = inputs + valid_col * matmul(branch_in, w_out)

    scale_mid = lax.rsqrt(jnp.mean(hidden * hidden, axis=-1, keepdims=True) + norm_eps)
    unit_mid = hidden * scale_mid
    normed_mid = gather_tokens((unit_mid * gain_mid).astype(bf16))
    branch_all = gather_tokens(branch_in)
    normed_mid, branch_all = lax.optimization_barrier((normed_mid, branch_all))
    early_lefts = [value.T for value in (normed_mid, branch_all, normed)]
    gate_up = matmul(normed_mid, w_gate_up)
    gate_up, early_lefts = lax.optimization_barrier((gate_up, early_lefts))
    gate_vals = gate_up[:, :local_ff]
    up_vals = gate_up[:, local_ff:]
    gate_act = jax.nn.silu(gate_vals)
    inner = (gate_act * up_vals).astype(bf16)

    grad_inner = matmul_nt(grad_ffn, w_down)
    down_share = owned(matmul_tn(inner, grad_ffn).astype(bf16))
    grad_gate_vals = (grad_inner * up_vals * dsilu(gate_vals)).astype(bf16)
    grad_up_vals = (grad_inner * gate_act).astype(bf16)
    grad_gate_up = jnp.concatenate([grad_gate_vals, grad_up_vals], axis=1)
    lefts = early_lefts
    if fast:
        mid = matmul_nt(grad_gate_up, w_gate_up)
        own_mid = lax.dynamic_slice_in_dim(mid, seq_index * row_count, row_count, 0)
        other_mid = lax.dynamic_slice_in_dim(mid, (1 - seq_index) * row_count, row_count, 0).astype(bf16)
        middle = (own_mid, other_mid, hidden, cotangent[0], valid_col, gain_mid)
        mixer = (proj, gap, gain_head, states, mixed)
        reduced, small, input_grad, layer_out = reduced_gradients(
            lefts, grad_gate_up, middle, mixer, w_out, w_mix, tokens[0], gain_in, inner, w_down, group
        )
        small, down_share = lax.optimization_barrier((small, down_share))
        head_share = lax.dynamic_slice_in_dim(small[3], owner_index * (HD // owners), HD // owners)
        grad_gate, grad_up, grad_output, *mix_all = laid_out(reduced, down_rows, group * HD)
    else:
        grad_normed_mid = scatter_tokens(matmul_nt(grad_gate_up, w_gate_up))
        grad_gain_mid = jnp.sum(grad_normed_mid * unit_mid, axis=0)
        grad_unit_mid = grad_normed_mid * gain_mid
        grad_hidden = grad_out + scale_mid * (
            grad_unit_mid - unit_mid * jnp.mean(grad_unit_mid * unit_mid, axis=-1, keepdims=True)
        )
        grad_branch = (valid_col * grad_hidden).astype(bf16)
        grad_branch_in = tokens_to_columns(matmul_nt(grad_branch, w_out).astype(bf16))
        small = jnp.zeros((owners, 8, share), f32).at[:, 1].set(grad_gain_mid.reshape(owners, share))
        grad_proj, grad_gap, grad_gain_head = mixer_backward(
            proj, gap, gain_head, states, mixed, grad_branch_in, group
        )
        grad_normed = scatter_tokens(matmul_nt(grad_proj, w_mix))
        grad_unit_in = grad_normed * gain_in
        grad_inputs = grad_hidden + scale_in * (
            grad_unit_in - unit_in * jnp.mean(grad_unit_in * unit_in, axis=-1, keepdims=True)
        )
        input_grad = grad_inputs.astype(bf16)
        layer_out = (hidden + valid_col * scatter_tokens(matmul(inner, w_down))).astype(bf16)
        rights = [grad_gate_up, tokens_to_columns(grad_branch), grad_proj]
        partial = jnp.concatenate([matmul(left, right).astype(bf16) for left, right in zip(lefts, rights)], axis=1)
        reduced = lax.all_gather(owned(partial), "seq", axis=0).astype(f32)
        small = small.at[:, 0].set(jnp.sum(grad_normed * unit_in, axis=0).reshape(owners, share))
        gap_placed = lax.dynamic_update_slice_in_dim(
            jnp.zeros((width,), f32), grad_gap.reshape(local_width), seq_index * local_width, 0
        )
        small = small.at[:, 2].set(gap_placed.reshape(owners, share))
        head_total = jnp.sum(grad_gain_head, axis=(0, 1))
        small = small.at[:, 3, : HD // owners].set(head_total.reshape(owners, -1))
        small = lax.dynamic_index_in_dim(lax.psum(small, ("seq",) + SR), owner_index, 0, keepdims=False)
        head_share = small[3, : HD // owners]
        ends = (2 * local_ff, 2 * local_ff + local_width)
        grad_units = reduced[:, :, : ends[0]].reshape(seqs, share, 2, owners, part).transpose(2, 1, 3, 0, 4)
        grad_gate, grad_up = grad_units.reshape(2, share, owners * down_rows)
        grad_output = reduced[:, :, ends[0] : ends[1]].transpose(1, 0, 2).reshape(share, width)
        mix_all = reduced[:, :, ends[1] :].reshape(seqs, share, groups, 4, group * HD)
        mix_all = mix_all.transpose(3, 1, 0, 2, 4).reshape(4, share, width)
    grad_down = share_columns(down_share).reshape(down_rows, width).astype(f32)

    return (
        layer_out[None],
        input_grad[None],
        mix_all[0],
        mix_all[1],
        mix_all[2],
        mix_all[3],
        grad_output,
        grad_gate,
        grad_up,
        grad_down,
        small[0],
        small[1],
        head_share,
        small[2],
    )


def solution(mesh):
    rows = P(SR, None)
    vector = P(SR)
    by_token = P(SR, "seq", None)
    placed = (by_token, vector) + (rows,) * 8 + (vector,) * 4 + (by_token,)
    return jax.shard_map(
        body,
        mesh=mesh,
        in_specs=placed,
        out_specs=(by_token, by_token) + (rows,) * 8 + (vector,) * 4,
        check_vma=False,
    )
```

```python
import functools

import jax
import jax.numpy as jnp
from jax import lax
from jax.experimental import pallas as pl
from jax.experimental.pallas import tpu as pltpu
from jax.sharding import PartitionSpec as P

H = 16
HD = 128
BLK = 128
SR = ("shard", "rep")
MESH = pl.DeviceIdType.MESH

norm_eps = 1e-05
head_eps = 1e-06

f32 = jnp.float32
bf16 = jnp.bfloat16


def dsilu(values_in):
    sig_vals = jax.nn.sigmoid(values_in)
    return sig_vals * (1.0 + values_in * (1.0 - sig_vals))


def matmul(left, right):
    return jnp.dot(left, right, preferred_element_type=f32)


def matmul_nt(left, right):
    return lax.dot_general(left, right, (((1,), (1,)), ((), ())), preferred_element_type=f32)


def matmul_tn(left, right):
    return lax.dot_general(left, right, (((0,), (0,)), ((), ())), preferred_element_type=f32)


def block_sums(lower, values):
    high, low = split(values)
    return matmul(lower, high) + matmul(lower, low)


def split(values):
    high = values.astype(bf16)
    return high, (values - high.astype(f32)).astype(bf16)


def head_forward(proj, gap, group_width):
    proj_query = proj[:, :group_width]
    proj_forget = proj[:, group_width : 2 * group_width]
    proj_input = proj[:, 2 * group_width : 3 * group_width]
    proj_gate = proj[:, 3 * group_width :]
    sig_query = jax.nn.sigmoid(proj_query)
    queries = (proj_query * sig_query).astype(bf16).astype(f32)
    forget_sig = jax.nn.sigmoid(-proj_forget)
    key_full = gap * forget_sig
    keys = key_full.astype(bf16).astype(f32)
    log_decay = jnp.log1p(-key_full)
    values = proj_input.astype(bf16)
    return proj_query, proj_gate, sig_query, queries, forget_sig, key_full, keys, log_decay, values


def triangle(kind, dtype):
    rows = lax.broadcasted_iota(jnp.int32, (BLK, BLK), 0)
    cols = lax.broadcasted_iota(jnp.int32, (BLK, BLK), 1)
    return (rows >= cols if kind == "lower" else rows <= cols).astype(dtype)


def forward_kernel(heads, proj_ref, gap_ref, gain_ref, branch_ref, states_ref, mixed_ref, state):
    width = heads * HD

    @pl.when(pl.program_id(1) == 0)
    def _():
        state[...] = jnp.zeros_like(state)

    proj = proj_ref[...]
    _, proj_gate, _, queries, _, _, keys, log_decay, values = head_forward(proj, gap_ref[...], width)
    lower = triangle("lower", f32)
    cumul = block_sums(lower.astype(bf16), log_decay)
    grown = jnp.exp(cumul)
    query_dec, query_low = split(queries * grown)
    key_dec, key_low = split(keys * jnp.exp(-cumul))
    last = cumul[BLK - 1 : BLK, :]
    key_tail = (keys * jnp.exp(last - cumul)).astype(bf16)
    last_decay = jnp.exp(last)
    gate_act = proj_gate * jax.nn.sigmoid(proj_gate)
    gain = gain_ref[...]
    for head in range(heads):
        span = slice(head * HD, (head + 1) * HD)
        before = state[head]
        states_ref[0, head] = before
        scores = matmul_nt(query_low[:, span], key_dec[:, span]) + matmul_nt(query_dec[:, span], key_low[:, span])
        scores = (scores + matmul_nt(query_dec[:, span], key_dec[:, span])) * lower
        scores, scores_low = split(scores)
        mixed = matmul(scores_low, values[:, span]) + matmul(scores, values[:, span])
        mixed = mixed + matmul(query_dec[:, span], before.astype(bf16))
        mixed_ref[:, span] = mixed
        decay_col = jnp.transpose(jnp.broadcast_to(last_decay[:, span], (HD, HD)))
        state[head] = decay_col * before + matmul_tn(key_tail[:, span], values[:, span])
        scale = lax.rsqrt(jnp.mean(mixed * mixed, axis=-1, keepdims=True) + head_eps)
        branch_ref[:, span] = (mixed * scale * gain * gate_act[:, span]).astype(bf16)


def backward_block(heads, proj, gap, gain, states, mixed_all, grad_in, dstate, after):
    width = heads * HD
    proj_query, proj_gate, sig_query, queries, forget_sig, key_full, keys, log_decay, values = head_forward(
        proj, gap, width
    )
    lower = triangle("lower", f32)
    upper = triangle("upper", bf16)
    cumul = block_sums(lower.astype(bf16), log_decay)
    grown = jnp.exp(cumul)
    shrunk = jnp.exp(-cumul)
    last = cumul[BLK - 1 : BLK, :]
    tail = jnp.exp(last - cumul)
    last_decay = jnp.exp(last)
    query_dec = (queries * grown).astype(bf16)
    key_dec = (keys * shrunk).astype(bf16)
    key_tail = (keys * tail).astype(bf16)
    sig_gate = jax.nn.sigmoid(proj_gate)
    gate_act = proj_gate * sig_gate
    gate_slope = sig_gate * (1.0 + proj_gate * (1.0 - sig_gate))
    gain_sum = jnp.zeros((1, HD), f32)
    query_grads, key_grads, value_grads, gate_grads, ends = [], [], [], [], []
    for head in range(heads):
        span = slice(head * HD, (head + 1) * HD)
        before = states[head]
        before_low = before.astype(bf16)
        q_dec, k_dec, vals = query_dec[:, span], key_dec[:, span], values[:, span]
        scores = (matmul_nt(q_dec, k_dec) * lower).astype(bf16)
        mixed = mixed_all[:, span]
        scale = lax.rsqrt(jnp.mean(mixed * mixed, axis=-1, keepdims=True) + head_eps)
        unit = mixed * scale
        grad_b = grad_in[:, span]
        gate_grads.append(grad_b * unit * gain * gate_slope[:, span])
        grad_normed = grad_b * gate_act[:, span]
        gain_sum = gain_sum + jnp.sum(grad_normed * unit, axis=0, keepdims=True)
        grad_unit = grad_normed * gain
        grad_mixed = scale * (grad_unit - unit * jnp.mean(grad_unit * unit, axis=-1, keepdims=True))
        grad_low = grad_mixed.astype(bf16)
        down = dstate[head]
        down_low = down.astype(bf16)
        grad_scores = (matmul_nt(grad_low, vals) * lower).astype(bf16)
        value_grads.append(matmul_tn(scores, grad_low) + matmul(key_tail[:, span], down_low))
        grad_q = matmul(grad_scores, k_dec) + matmul_nt(grad_low, before_low)
        grad_k = matmul_tn(grad_scores, q_dec)
        grad_t = matmul_nt(vals, down_low)
        query_grads.append(grad_q * grown[:, span])
        key_grads.append(grad_k * shrunk[:, span] + grad_t * tail[:, span])
        ends.append(jnp.transpose(jnp.sum(down * after[head], axis=1, keepdims=True)))
        after[head] = before
        decay_col = jnp.transpose(jnp.broadcast_to(last_decay[:, span], (HD, HD)))
        dstate[head] = decay_col * down + matmul_tn(q_dec, grad_low)
    grad_queries = jnp.concatenate(query_grads, axis=1)
    grad_keys = jnp.concatenate(key_grads, axis=1)
    grad_values = jnp.concatenate(value_grads, axis=1)
    end = jnp.concatenate(ends, axis=1)
    grad_decay = block_sums(upper, queries * grad_queries - keys * grad_keys) + end
    grad_key_full = grad_keys - grad_decay / (1.0 - key_full)
    gap_sum = jnp.sum(grad_key_full * forget_sig, axis=0, keepdims=True)
    query_slope = sig_query * (1.0 + proj_query * (1.0 - sig_query))
    grads = (
        grad_queries * query_slope,
        -grad_key_full * gap * forget_sig * (1.0 - forget_sig),
        grad_values,
        jnp.concatenate(gate_grads, axis=1),
    )
    return [grad.astype(bf16) for grad in grads], gap_sum, gain_sum


def backward_kernel(
    heads, proj_ref, gap_ref, gain_ref, states_ref, mixed_ref, grad_ref, out_ref, gap_out, gain_out, dstate, after
):
    width = heads * HD

    @pl.when(pl.program_id(1) == 0)
    def _():
        dstate[...] = jnp.zeros_like(dstate)
        after[...] = jnp.zeros_like(after)
        gap_out[...] = jnp.zeros_like(gap_out)
        gain_out[...] = jnp.zeros_like(gain_out)

    states = [states_ref[0, head] for head in range(heads)]
    grads, gap_sum, gain_sum = backward_block(
        heads, proj_ref[...], gap_ref[...], gain_ref[...], states, mixed_ref[...], grad_ref[...].astype(f32), dstate, after
    )
    for kind, grad in enumerate(grads):
        out_ref[:, kind * width : (kind + 1) * width] = grad
    gap_out[...] += gap_sum
    gain_out[...] += gain_sum


def mixer_forward(proj, gap, gain, heads):
    tokens, total = proj.shape
    groups, blocks = total // (4 * heads * HD), tokens // BLK
    width = heads * HD
    return pl.pallas_call(
        functools.partial(forward_kernel, heads),
        grid=(groups, blocks),
        in_specs=[
            pl.BlockSpec((BLK, 4 * width), lambda g, b: (b, g)),
            pl.BlockSpec((1, width), lambda g, b: (0, g)),
            pl.BlockSpec((1, HD), lambda g, b: (0, 0)),
        ],
        out_specs=[
            pl.BlockSpec((BLK, width), lambda g, b: (b, g)),
            pl.BlockSpec((1, heads, HD, HD), lambda g, b: (b, g, 0, 0)),
            pl.BlockSpec((BLK, width), lambda g, b: (b, g)),
        ],
        out_shape=[
            jax.ShapeDtypeStruct((tokens, groups * width), bf16),
            jax.ShapeDtypeStruct((blocks, groups * heads, HD, HD), f32),
            jax.ShapeDtypeStruct((tokens, groups * width), f32),
        ],
        scratch_shapes=[pltpu.VMEM((heads, HD, HD), f32)],
        compiler_params=pltpu.CompilerParams(vmem_limit_bytes=48 << 20),
        name="mixer_forward",
    )(proj, gap, gain)


def mixer_backward(proj, gap, gain, states, mixed, grad, heads):
    tokens, total = proj.shape
    groups, blocks = total // (4 * heads * HD), tokens // BLK
    width = heads * HD
    return pl.pallas_call(
        functools.partial(backward_kernel, heads),
        grid=(groups, blocks),
        in_specs=[
            pl.BlockSpec((BLK, 4 * width), lambda g, b: (blocks - 1 - b, g)),
            pl.BlockSpec((1, width), lambda g, b: (0, g)),
            pl.BlockSpec((1, HD), lambda g, b: (0, 0)),
            pl.BlockSpec((1, heads, HD, HD), lambda g, b: (blocks - 1 - b, g, 0, 0)),
            pl.BlockSpec((BLK, width), lambda g, b: (blocks - 1 - b, g)),
            pl.BlockSpec((BLK, width), lambda g, b: (blocks - 1 - b, g)),
        ],
        out_specs=[
            pl.BlockSpec((BLK, 4 * width), lambda g, b: (blocks - 1 - b, g)),
            pl.BlockSpec((1, width), lambda g, b: (0, g)),
            pl.BlockSpec((1, 1, HD), lambda g, b: (g, 0, 0)),
        ],
        out_shape=[
            jax.ShapeDtypeStruct((tokens, total), bf16),
            jax.ShapeDtypeStruct((1, groups * width), f32),
            jax.ShapeDtypeStruct((groups, 1, HD), f32),
        ],
        scratch_shapes=[pltpu.VMEM((heads, HD, HD), f32), pltpu.VMEM((heads, HD, HD), f32)],
        compiler_params=pltpu.CompilerParams(vmem_limit_bytes=48 << 20),
        name="mixer_backward",
    )(proj, gap, gain, states, mixed, grad)


def swap(value):
    return lax.ppermute(value, "seq", [(0, 1), (1, 0)])


def in_order(own, other, axis):
    first = lax.axis_index("seq") == 0
    return jnp.concatenate([jnp.where(first, own, other), jnp.where(first, other, own)], axis=axis)


def gather_tokens(value):
    if lax.axis_size("seq") != 2:
        return lax.all_gather(value, "seq", axis=0, tiled=True)
    return in_order(value, swap(value), 0)


def scatter_tokens(partial):
    if lax.axis_size("seq") != 2:
        return lax.psum_scatter(partial.astype(bf16), "seq", scatter_dimension=0, tiled=True).astype(f32)
    rows = partial.shape[0] // 2
    me = lax.axis_index("seq")
    theirs = lax.dynamic_slice_in_dim(partial, (1 - me) * rows, rows, 0).astype(bf16)
    return lax.dynamic_slice_in_dim(partial, me * rows, rows, 0) + swap(theirs).astype(f32)


def columns_to_tokens(value):
    if lax.axis_size("seq") != 2:
        return lax.all_to_all(value, "seq", 0, 1, tiled=True)
    rows = value.shape[0] // 2
    me = lax.axis_index("seq")
    theirs = swap(lax.dynamic_slice_in_dim(value, (1 - me) * rows, rows, 0))
    return in_order(lax.dynamic_slice_in_dim(value, me * rows, rows, 0), theirs, 1)


def tokens_to_columns(value):
    if lax.axis_size("seq") != 2:
        return lax.all_to_all(value, "seq", 1, 0, tiled=True)
    cols = value.shape[1] // 2
    me = lax.axis_index("seq")
    theirs = swap(lax.dynamic_slice_in_dim(value, (1 - me) * cols, cols, 1))
    return in_order(lax.dynamic_slice_in_dim(value, me * cols, cols, 1), theirs, 0)


RING = 8
CORE_RING = 4
CHUNK = 256


def reduce_kernel(counts, heads, *refs):
    kinds = len(counts)
    lefts = refs[:kinds]
    (
        units_ref,
        own_mid,
        other_mid,
        hidden_ref,
        cotangent_ref,
        valid_ref,
        gain_mid_ref,
        wout_ref,
        proj_ref,
        gap_ref,
        gain_ref,
        states_ref,
        mixed_ref,
        mix_ref,
        tokens_ref,
        gain_in_ref,
        inner_ref,
        down_ref,
        out_ref,
        small_out,
        input_out,
        layer_out,
        core_out,
        core_in,
        pair_out,
        pair_in,
        sums,
        line_in,
        done,
        core_sems,
        pair_sems,
        line_send,
        line_recv,
        done_sems,
        got_sems,
        small_in,
        small_all,
        small_sems,
        columns,
        column_sems,
        grad_proj,
        proj_in,
        proj_sems,
        dstate,
        after,
        gap_acc,
        gain_acc,
        weights_in,
        weight_sems,
        kept_normed,
        sent_normed,
        got_normed,
        normed_sems,
        got_mid,
        mid_sems,
        grad_hidden,
        branch_ref,
        grad_ref,
        sent_heads,
        head_sems,
        mid_sum,
        inner_in,
        inner_sems,
        output_sems,
        load_sems,
    ) = refs[kinds:]
    rights = (units_ref, columns, grad_proj)
    total = sum(counts)
    planes, rows = sums.shape[1:3]
    seq = lax.axis_index("seq")
    shard = lax.axis_index("shard")
    plane = lax.axis_index("rep")
    core, pair = shard % 2, shard // 2
    other_core = {"shard": shard + 1 - 2 * core}
    other_pair = {"shard": (shard + 2) % 4}
    other_seq = {"seq": 1 - seq}
    below, above = {"rep": plane - 1}, {"rep": plane + 1}
    me = shard * planes + plane
    owners = small_all.shape[0]
    devices = small_in.shape[0]
    number = seq * owners + me

    def others():
        for step in range(1, devices):
            there = (number + step) % devices
            owner = there % owners
            yield step, owner, {"seq": there // owners, "shard": owner // planes, "rep": owner % planes}

    barrier = pltpu.get_barrier_semaphore()
    for _, _, device in others():
        pl.semaphore_signal(barrier, inc=1, device_id=device, device_id_type=MESH)
    pl.semaphore_wait(barrier, devices - 1)

    def remote(source, target, send, recv, device):
        return pltpu.make_async_remote_copy(
            src_ref=source, dst_ref=target, send_sem=send, recv_sem=recv, device_id=device, device_id_type=MESH
        )

    own_tokens, width = tokens_ref.shape
    local_width = columns.shape[1]
    group_width = heads * HD
    groups, blocks = local_width // group_width, grad_proj.shape[0] // BLK

    piece = weights_in.shape[1]
    pieces = width // piece

    def aligned(start, size):
        return pl.ds(pl.multiple_of(start, size), size)

    def mid_copy():
        return remote(sent_normed, got_mid, mid_sems.at[0], mid_sems.at[1], other_seq)

    def mid_turn():
        mid_copy().wait()
        mid_loads[1].wait()
        gain = gain_mid_ref[...]
        size = 64

        def part(index, total_mid):
            rows_at = aligned(index * size, size)
            values = hidden_ref[rows_at]
            scale = lax.rsqrt(jnp.mean(values * values, axis=-1, keepdims=True) + norm_eps)
            unit = values * scale
            grad = kept_normed[rows_at] + got_mid[rows_at].astype(f32)
            grad_unit = grad * gain
            moved = scale * (grad_unit - unit * jnp.mean(grad_unit * unit, axis=-1, keepdims=True))
            both = cotangent_ref[rows_at].astype(f32) + moved
            grad_hidden[rows_at] = both
            branch_ref[rows_at] = (valid_ref[rows_at] * both).astype(bf16)
            return total_mid + jnp.sum(grad * unit, axis=0, keepdims=True)

        mid_sum[...] = lax.fori_loop(0, own_tokens // size, part, jnp.zeros((1, width), f32))

    def wout_load(index):
        return pltpu.make_async_copy(
            wout_ref.at[aligned(index * piece, piece)],
            weights_in.at[index % 2, :, pl.ds(0, width)],
            weight_sems.at[index % 2],
        )

    def head_copy():
        place = grad_ref.at[aligned(seq * own_tokens, own_tokens)]
        return remote(sent_heads, place, head_sems.at[0], head_sems.at[1], other_seq)

    def heads_turn():
        def part(index, _):
            @pl.when(index + 1 < pieces)
            def _():
                wout_load(index + 1).start()

            wout_load(index).wait()
            grad = matmul_nt(branch_ref[...], weights_in[index % 2, :, :width]).astype(bf16)
            span = aligned((index % per_seq) * piece, piece)

            @pl.when(index // per_seq == seq)
            def _():
                grad_ref[aligned(seq * own_tokens, own_tokens), span] = grad

            @pl.when(index // per_seq != seq)
            def _():
                sent_heads[:, span] = grad

            return 0

        per_seq = local_width // piece
        lax.fori_loop(0, pieces, part, 0)
        head_copy().start()
        weight_load(0).start()

    def heads_end():
        head_copy().wait()
        for copy in column_moves():
            copy.start()

    def column_moves():
        mine = branch_ref.at[:, aligned(seq * local_width, local_width)]
        theirs = branch_ref.at[:, aligned((1 - seq) * local_width, local_width)]
        place = columns.at[aligned(seq * own_tokens, own_tokens)]
        kept = pltpu.make_async_copy(mine, place, column_sems.at[0])
        return kept, remote(theirs, place, column_sems.at[1], column_sems.at[2], other_seq)

    def proj_load(index):
        group, block = index // blocks, blocks - 1 - index % blocks
        source = proj_ref.at[aligned(block * BLK, BLK), aligned(group * 4 * group_width, 4 * group_width)]
        return pltpu.make_async_copy(source, proj_in.at[index % 2], proj_sems.at[index % 2])

    def mixer_turn(index):
        group, block = index // blocks, blocks - 1 - index % blocks
        rows_at, span = aligned(block * BLK, BLK), aligned(group * group_width, group_width)

        @pl.when(index + 1 < groups * blocks)
        def _():
            proj_load(index + 1).start()

        @pl.when(index % blocks == 0)
        def _():
            dstate[...] = jnp.zeros_like(dstate)
            after[...] = jnp.zeros_like(after)
            gap_acc[:, span] = jnp.zeros((1, group_width), f32)

        proj_load(index).wait()
        states = [states_ref[block, group * heads + head] for head in range(heads)]
        grads, gap_sum, gain_sum = backward_block(
            heads,
            proj_in[index % 2],
            gap_ref[:, span],
            gain_ref[...],
            states,
            mixed_ref[rows_at, span],
            grad_ref[rows_at, span].astype(f32),
            dstate,
            after,
        )
        for kind, grad in enumerate(grads):
            grad_proj[rows_at, aligned((group * 4 + kind) * group_width, group_width)] = grad
        gap_acc[:, span] += gap_sum
        gain_acc[...] += gain_sum

    def weight_load(index):
        return pltpu.make_async_copy(
            mix_ref.at[aligned(index * piece, piece)], weights_in.at[index % 2], weight_sems.at[index % 2]
        )

    def normed_copy():
        return remote(sent_normed, got_normed, normed_sems.at[0], normed_sems.at[1], other_seq)

    def normed_turn(index):
        @pl.when(index + 1 < pieces)
        def _():
            weight_load(index + 1).start()

        weight_load(index).wait()
        weight = weights_in[index % 2]
        span = aligned(index * piece, piece)
        sent_normed[:, span] = matmul_nt(grad_proj[aligned((1 - seq) * own_tokens, own_tokens)], weight).astype(bf16)
        kept_normed[:, span] = matmul_nt(grad_proj[aligned(seq * own_tokens, own_tokens)], weight)

        @pl.when(index == pieces - 1)
        def _():
            normed_copy().start()

    unit_pieces = down_ref.shape[0] // piece

    def unit_loads(index):
        span = aligned(index * piece, piece)
        return (
            pltpu.make_async_copy(inner_ref.at[:, span], inner_in.at[index % 2], inner_sems.at[index % 2]),
            pltpu.make_async_copy(
                down_ref.at[span], weights_in.at[index % 2, :, pl.ds(0, width)], weight_sems.at[index % 2]
            ),
        )

    def output_copy():
        return remote(sent_normed, got_mid, output_sems.at[0], output_sems.at[1], other_seq)

    def output_turn(index):
        @pl.when(index == 0)
        def _():
            for copy in unit_loads(0):
                copy.start()
            kept_normed[...] = jnp.zeros_like(kept_normed)
            grad_hidden[...] = jnp.zeros_like(grad_hidden)

        @pl.when(index + 1 < unit_pieces)
        def _():
            for copy in unit_loads(index + 1):
                copy.start()

        for copy in unit_loads(index):
            copy.wait()
        weight = weights_in[index % 2, :, :width]
        for total_ref, which in ((grad_hidden, 1 - seq), (kept_normed, seq)):
            total_ref[...] += matmul(inner_in[index % 2, aligned(which * own_tokens, own_tokens)], weight)

        @pl.when(index == unit_pieces - 1)
        def _():
            sent_normed[...] = grad_hidden[...].astype(bf16)
            output_copy().start()

    def output_end():
        output_copy().wait()
        size = 64

        def part(index, _):
            rows_at = aligned(index * size, size)
            both = kept_normed[rows_at] + got_mid[rows_at].astype(f32)
            layer_out[rows_at] = (hidden_ref[rows_at] + valid_ref[rows_at] * both).astype(bf16)
            return 0

        lax.fori_loop(0, own_tokens // size, part, 0)

    def input_turn():
        normed_copy().wait()
        gain = gain_in_ref[...]
        size = 64

        def part(index, total_in):
            rows_at = aligned(index * size, size)
            values = tokens_ref[rows_at].astype(f32)
            scale = lax.rsqrt(jnp.mean(values * values, axis=-1, keepdims=True) + norm_eps)
            unit = values * scale
            grad = kept_normed[rows_at] + got_normed[rows_at].astype(f32)
            grad_unit = grad * gain
            moved = scale * (grad_unit - unit * jnp.mean(grad_unit * unit, axis=-1, keepdims=True))
            input_out[rows_at] = (grad_hidden[rows_at] + moved).astype(bf16)
            return total_in + jnp.sum(grad * unit, axis=0, keepdims=True)

        total_in = lax.fori_loop(0, own_tokens // size, part, jnp.zeros((1, width), f32))
        small_all[...] = jnp.zeros_like(small_all)
        for owner in range(owners):
            small_all[owner, 1:2, :] = mid_sum[:, owner * rows : (owner + 1) * rows]
            small_all[owner, 0:1, :] = total_in[:, owner * rows : (owner + 1) * rows]
            small_all[owner, 3:4, :] = gain_acc[...]
        first_owner = seq * (local_width // rows)
        for index in range(local_width // rows):
            small_all[first_owner + index, 2:3, :] = gap_acc[:, index * rows : (index + 1) * rows]
        for copy in small_copies:
            copy.start()

    small_copies = [
        remote(small_all.at[owner], small_in.at[number], small_sems.at[0, step], small_sems.at[1, step], device)
        for step, owner, device in others()
    ]
    gain_acc[...] = jnp.zeros_like(gain_acc)
    proj_load(0).start()
    wout_load(0).start()
    mid_loads = (
        pltpu.make_async_copy(other_mid, sent_normed, load_sems.at[0]),
        pltpu.make_async_copy(own_mid, kept_normed, load_sems.at[1]),
    )
    for copy in mid_loads:
        copy.start()
    mid_loads[0].wait()
    mid_copy().start()

    def core_copy(chunk):
        slot = chunk % CORE_RING
        return remote(
            core_out.at[slot], core_in.at[slot], core_sems.at[0, slot], core_sems.at[1, slot], other_core
        )

    def pair_copy(chunk):
        sent, got = chunk % CORE_RING, chunk % RING
        return remote(
            pair_out.at[sent], pair_in.at[got], pair_sems.at[0, sent], pair_sems.at[1, got], other_pair
        )

    def line_copy(way, step, slot, target):
        return remote(
            sums.at[slot, target],
            line_in.at[way, step - 1, slot],
            line_send.at[way, step - 1, slot],
            line_recv.at[way, step - 1, slot],
            above if way else below,
        )

    def done_copies(chunk):
        slot = chunk % RING
        place = out_ref.at[seq, :, pl.ds(pl.multiple_of(chunk * CHUNK, CHUNK), CHUNK)]
        kept = pltpu.make_async_copy(done.at[slot], place, done_sems.at[1, slot])
        sent = remote(done.at[slot], place, done_sems.at[0, slot], got_sems.at[chunk], other_seq)
        return kept, sent

    def product(kind, chunk, half, which):
        first = (half * 2 + which) * planes * rows
        left = lefts[kind][pl.ds(pl.multiple_of(first, planes * rows), planes * rows), :]
        start = (chunk - sum(counts[:kind])) * CHUNK
        return matmul(left, rights[kind][:, pl.ds(pl.multiple_of(start, CHUNK), CHUNK)])

    def line_target(way, step):
        return plane + planes - step if way else plane - planes + step

    def sends(way, step):
        return plane < step if way else plane >= planes - step

    def receives(way, step):
        return jnp.logical_and(plane > 0, plane <= step) if way else jnp.logical_and(plane < planes - 1, plane >= planes - step - 1)

    def front(kind, chunk):
        slot = chunk % CORE_RING

        @pl.when(chunk >= CORE_RING)
        def _():
            core_copy(chunk).wait_send()

        for half in range(2):
            core_out[slot, half] = product(kind, chunk, half, 1 - core).astype(bf16)
        core_copy(chunk).start()

    def middle(kind, chunk):
        slot, core_slot = chunk % RING, chunk % CORE_RING

        @pl.when(chunk >= CORE_RING)
        def _():
            pair_copy(chunk).wait_send()

        theirs = product(kind, chunk, 1 - pair, core)
        mine = product(kind, chunk, pair, core)
        core_copy(chunk).wait_recv()
        pair_out[core_slot] = (theirs + core_in[core_slot, 1 - pair].astype(f32)).astype(bf16)
        pair_copy(chunk).start()
        mine = mine + core_in[core_slot, pair].astype(f32)
        sums[slot] = mine.astype(bf16).reshape(planes, rows, CHUNK)

    def line_start(chunk, step):
        slot = chunk % RING
        for way in range(2):

            @pl.when(sends(way, step))
            def _(way=way):
                target = line_target(way, step)
                if step > 1:

                    @pl.when(receives(way, step - 1))
                    def _():
                        line_copy(way, step - 1, slot, 0).wait_recv()
                        got = line_in[way, step - 2, slot].astype(f32)
                        sums[slot, target] = (sums[slot, target].astype(f32) + got).astype(bf16)

                line_copy(way, step, slot, target).start()

    def pair_done(chunk):
        slot = chunk % RING
        pair_copy(chunk).wait_recv()
        got = pair_in[slot].reshape(planes, rows, CHUNK).astype(f32)
        sums[slot] = (sums[slot].astype(f32) + got).astype(bf16)
        line_start(chunk, 1)

    def finish(chunk):
        slot = chunk % RING
        kept, sent = done_copies(chunk)

        @pl.when(chunk >= RING)
        def _():
            kept.wait()
            sent.wait_send()

        last = planes - 1
        for way in range(2):

            @pl.when(receives(way, last))
            def _(way=way):
                line_copy(way, last, slot, 0).wait_recv()
                got = line_in[way, last - 1, slot].astype(f32)
                sums[slot, plane] = (sums[slot, plane].astype(f32) + got).astype(bf16)

        done[slot] = sums[slot, plane]
        kept.start()
        sent.start()
        for way in range(2):
            for step in range(1, planes):

                @pl.when(sends(way, step))
                def _(way=way, step=step):
                    line_copy(way, step, slot, 0).wait_send()

    def received(chunk, _):
        done_copies(chunk)[1].wait_recv()
        return 0

    later = [(pair_done, 3)] + [
        (functools.partial(line_start, step=step), 2 + step) for step in range(2, planes)
    ] + [(finish, 2 + planes)]
    mid_at, mixer_at = 6, 10
    normed_at = mixer_at + groups * blocks
    assert normed_at + pieces // 2 <= counts[0] and unit_pieces + 2 <= counts[-1]
    first = 0
    for kind, count in enumerate(counts):

        def step(turn, _, kind=kind, first=first):
            front(kind, turn)
            if kind == 0:
                pl.when(turn >= 1)(lambda: middle(0, turn - 1))
            else:
                pl.when(turn == first)(lambda: middle(kind - 1, turn - 1))
                pl.when(turn > first)(lambda: middle(kind, turn - 1))
            if kind == 0:
                pl.when(turn == mid_at)(mid_turn)
                pl.when(turn == mid_at + 1)(heads_turn)
                pl.when(turn == mixer_at)(heads_end)
                inside = jnp.logical_and(turn >= mixer_at, turn < normed_at)
                pl.when(inside)(lambda: mixer_turn(turn - mixer_at))

                @pl.when(jnp.logical_and(turn >= normed_at, turn < normed_at + pieces // 2))
                def _():
                    normed_turn(2 * (turn - normed_at))
                    normed_turn(2 * (turn - normed_at) + 1)

            elif kind == kinds - 1:
                pl.when(turn == first + 1)(input_turn)
                inside = jnp.logical_and(turn >= first + 2, turn < first + 2 + unit_pieces)
                pl.when(inside)(lambda: output_turn(turn - first - 2))
            for act, lag in later:
                pl.when(turn >= lag)(lambda act=act, lag=lag: act(turn - lag))
            return 0

        if kind == 1:
            for copy in column_moves():
                copy.wait()
        lax.fori_loop(first, first + count, step, 0)
        first += count

    def small_end():
        small_in[number] = small_all[me]
        for copy in small_copies:
            copy.wait()
        small_out[...] = jnp.sum(small_in[...], axis=0)

    def drain(turn, _):
        pl.when(turn == total)(lambda: middle(kinds - 1, turn - 1))
        for act, lag in later:
            pl.when(turn - lag < total)(lambda act=act, lag=lag: act(turn - lag))
        pl.when(turn == total + 1)(small_end)
        pl.when(turn == total + 3)(output_end)
        return 0

    lax.fori_loop(total, total + later[-1][1], drain, 0)
    for chunk in range(total - RING, total):
        slot = chunk % RING
        if chunk >= total - CORE_RING:
            core_copy(chunk).wait_send()
            pair_copy(chunk).wait_send()
        kept, sent = done_copies(chunk)
        kept.wait()
        sent.wait_send()
    lax.fori_loop(0, total, received, 0)


def reduced_gradients(lefts, grad_units, middle, mixer, w_out, w_mix, tokens, gain_in, inner, w_down, heads):
    proj, gap, gain, states, mixed = mixer
    own_tokens, width = tokens.shape
    local_width = mixed.shape[1]
    counts = [columns // CHUNK for columns in (grad_units.shape[1], local_width, proj.shape[1])]
    planes = lax.axis_size("rep")
    rows = lefts[0].shape[0] // lax.axis_size(SR)
    block = planes * rows
    owners = lax.axis_size(SR)
    devices = lax.axis_size(("seq",) + SR)
    vmem = pl.BlockSpec(memory_space=pltpu.VMEM)
    anywhere = pl.BlockSpec(memory_space=pl.ANY)
    return pl.pallas_call(
        functools.partial(reduce_kernel, counts, heads),
        in_specs=[vmem] * 4 + [anywhere] * 2 + [vmem] * 4 + [anywhere] * 2 + [vmem] * 4 + [anywhere] + [vmem] * 2 + [anywhere] * 2,
        out_specs=[anywhere, vmem, vmem, vmem],
        out_shape=[
            jax.ShapeDtypeStruct((2, rows, sum(counts) * CHUNK), bf16),
            jax.ShapeDtypeStruct((8, rows), f32),
            jax.ShapeDtypeStruct((own_tokens, width), bf16),
            jax.ShapeDtypeStruct((own_tokens, width), bf16),
        ],
        scratch_shapes=[
            pltpu.VMEM((CORE_RING, 2, block, CHUNK), bf16),
            pltpu.VMEM((CORE_RING, 2, block, CHUNK), bf16),
            pltpu.VMEM((CORE_RING, block, CHUNK), bf16),
            pltpu.VMEM((RING, block, CHUNK), bf16),
            pltpu.VMEM((RING, planes, rows, CHUNK), bf16),
            pltpu.VMEM((2, planes - 1, RING, rows, CHUNK), bf16),
            pltpu.VMEM((RING, rows, CHUNK), bf16),
            pltpu.SemaphoreType.DMA((2, CORE_RING)),
            pltpu.SemaphoreType.DMA((2, RING)),
            pltpu.SemaphoreType.DMA((2, planes - 1, RING)),
            pltpu.SemaphoreType.DMA((2, planes - 1, RING)),
            pltpu.SemaphoreType.DMA((2, RING)),
            pltpu.SemaphoreType.DMA((sum(counts),)),
            pltpu.VMEM((devices, 8, rows), f32),
            pltpu.VMEM((owners, 8, rows), f32),
            pltpu.SemaphoreType.DMA((2, devices)),
            pltpu.VMEM((2 * own_tokens, local_width), bf16),
            pltpu.SemaphoreType.DMA((3,)),
            pltpu.VMEM(proj.shape, bf16),
            pltpu.VMEM((2, BLK, 4 * heads * HD), f32),
            pltpu.SemaphoreType.DMA((2,)),
            pltpu.VMEM((heads, HD, HD), f32),
            pltpu.VMEM((heads, HD, HD), f32),
            pltpu.VMEM((1, local_width), f32),
            pltpu.VMEM((1, HD), f32),
            pltpu.VMEM((2, CHUNK, proj.shape[1]), bf16),
            pltpu.SemaphoreType.DMA((2,)),
            pltpu.VMEM((own_tokens, width), f32),
            pltpu.VMEM((own_tokens, width), bf16),
            pltpu.VMEM((own_tokens, width), bf16),
            pltpu.SemaphoreType.DMA((2,)),
            pltpu.VMEM((own_tokens, width), bf16),
            pltpu.SemaphoreType.DMA((2,)),
            pltpu.VMEM((own_tokens, width), f32),
            pltpu.VMEM((own_tokens, width), bf16),
            pltpu.VMEM((2 * own_tokens, local_width), bf16),
            pltpu.VMEM((own_tokens, local_width), bf16),
            pltpu.SemaphoreType.DMA((2,)),
            pltpu.VMEM((1, width), f32),
            pltpu.VMEM((2, 2 * own_tokens, CHUNK), bf16),
            pltpu.SemaphoreType.DMA((2,)),
            pltpu.SemaphoreType.DMA((2,)),
            pltpu.SemaphoreType.DMA((2,)),
        ],
        compiler_params=pltpu.CompilerParams(
            collective_id=0, has_side_effects=True, vmem_limit_bytes=62 << 20
        ),
        name="reduced_gradients",
    )(*lefts, grad_units, *middle, w_out, proj, gap, gain, states, mixed, w_mix, tokens, gain_in, inner, w_down)


def gather_kernel(
    tokens_ref,
    gains_ref,
    w_query,
    w_forget,
    w_input,
    w_gate_out,
    w_output,
    proj_ref,
    normed_ref,
    mix_ref,
    out_ref,
    all_gains_ref,
    pieces,
    all_tokens,
    normed,
    all_gains,
    products,
    load_sems,
    token_sems,
    gain_sems,
    line_send,
    line_recv,
    pair_sems,
    core_sems,
    write_sems,
    half_sems,
    last_sems,
):
    total, owners, rows = pieces.shape[:3]
    seqs, own_tokens, width = all_tokens.shape
    local_width = width // seqs
    out_count = local_width // CHUNK
    group_width = mix_ref.shape[2] // 4 // (local_width // (4 * HD))
    planes = lax.axis_size("rep")
    seq = lax.axis_index("seq")
    shard = lax.axis_index("shard")
    plane = lax.axis_index("rep")
    core, pair = shard % 2, shard // 2
    me = shard * planes + plane
    other_core = {"shard": shard + 1 - 2 * core}
    other_pair = {"shard": (shard + 2) % 4}
    other_seq = {"seq": 1 - seq}
    below, above = {"rep": plane - 1}, {"rep": plane + 1}

    loads = []
    per_group = group_width // CHUNK
    for chunk in range(total):
        if chunk < out_count:
            source, start = w_output, chunk * CHUNK
        else:
            group, rest = divmod(chunk - out_count, 4 * per_group)
            kind, part = divmod(rest, per_group)
            source = (w_query, w_forget, w_input, w_gate_out)[kind]
            start = group * group_width + part * CHUNK
        start = pl.multiple_of(seq * local_width + start, CHUNK)
        loads.append(
            pltpu.make_async_copy(source.at[:, pl.ds(start, CHUNK)], pieces.at[chunk, me], load_sems.at[chunk])
        )
    for load in loads:
        load.start()

    def others():
        for step in range(1, owners):
            number = (me + step) % owners
            yield step, {"shard": number // planes, "rep": number % planes}

    barrier = pltpu.get_barrier_semaphore()
    for _, device in others():
        pl.semaphore_signal(barrier, inc=1, device_id=device, device_id_type=MESH)
    pl.semaphore_signal(barrier, inc=1, device_id=other_seq, device_id_type=MESH)
    pl.semaphore_wait(barrier, owners)

    def remote(source, target, send, recv, device):
        return pltpu.make_async_remote_copy(
            src_ref=source, dst_ref=target, send_sem=send, recv_sem=recv, device_id=device, device_id_type=MESH
        )

    token_copy = remote(tokens_ref, all_tokens.at[seq], token_sems.at[0], token_sems.at[1], other_seq)
    token_copy.start()
    gain_copies = [
        remote(gains_ref, all_gains.at[me], gain_sems.at[0, step], gain_sems.at[1, step], device)
        for step, device in others()
    ]
    for copy in gain_copies:
        copy.start()

    def line_copy(way, step, chunk, owner):
        slot = chunk % RING
        return remote(
            pieces.at[chunk, owner],
            pieces.at[chunk, owner],
            line_send.at[way, step - 1, slot],
            line_recv.at[way, step - 1, slot],
            above if way else below,
        )

    def block(which_pair):
        return pl.ds((which_pair * 2 + core) * planes, planes)

    def pair_copy(chunk):
        slot = chunk % RING
        place = pieces.at[chunk, block(pair)]
        return remote(place, place, pair_sems.at[0, slot], pair_sems.at[1, slot], other_pair)

    def core_copy(chunk, which):
        slot = chunk % RING
        place = pieces.at[chunk, block(pair if which == 0 else 1 - pair)]
        return remote(place, place, core_sems.at[0, which, slot], core_sems.at[1, which, slot], other_core)

    def sends(way, step):
        if way:
            return jnp.logical_and(plane < planes - 1, plane - (step - 1) >= 0)
        return jnp.logical_and(plane > 0, plane + (step - 1) <= planes - 1)

    def receives(way, step):
        return plane - step >= 0 if way else plane + step <= planes - 1

    def line(chunk, step):
        for way in range(2):
            if step > 1:

                @pl.when(receives(way, step - 1))
                def _(way=way):
                    line_copy(way, step - 1, chunk, me).wait_recv()

            if step < planes:

                @pl.when(sends(way, step))
                def _(way=way):
                    line_copy(way, step, chunk, me - (step - 1) if way else me + (step - 1)).start()

    def first(chunk):
        slot = chunk
        pltpu.make_async_copy(pieces.at[chunk, me], pieces.at[chunk, me], load_sems.at[slot]).wait()
        line(chunk, 1)

    def across(chunk):
        line(chunk, planes)
        pair_copy(chunk).start()
        core_copy(chunk, 0).start()

    def to_core(chunk):
        pair_copy(chunk).wait_recv()
        core_copy(chunk, 1).start()

    def writes(chunk):
        slot = chunk % RING

        def mix_writes():
            span = pl.ds(pl.multiple_of((chunk - out_count) * CHUNK, CHUNK), CHUNK)
            return (
                pltpu.make_async_copy(pieces.at[chunk], mix_ref.at[:, :, span], write_sems.at[0, slot]),
                pltpu.make_async_copy(products.at[slot], proj_ref.at[:, span], write_sems.at[1, slot]),
            )

        def out_writes():
            place = out_ref.at[:, :, pl.ds(pl.multiple_of(seq * local_width + chunk * CHUNK, CHUNK), CHUNK)]
            return (
                pltpu.make_async_copy(pieces.at[chunk], place, half_sems.at[2, slot]),
                remote(pieces.at[chunk], place, half_sems.at[0, slot], half_sems.at[1, slot], other_seq),
            )

        return mix_writes, out_writes

    def finish(chunk):
        slot = chunk % RING
        core_copy(chunk, 0).wait_recv()
        core_copy(chunk, 1).wait_recv()
        mix_writes, out_writes = writes(chunk)

        @pl.when(chunk >= out_count + RING)
        def _():
            written(chunk - RING)

        @pl.when(chunk >= out_count)
        def _():
            weight = pieces[chunk].reshape(owners * rows, CHUNK)
            for half in range(seqs):
                products[slot, half * own_tokens : (half + 1) * own_tokens] = matmul(normed[half], weight)
            for copy in mix_writes():
                copy.start()

        @pl.when(chunk < out_count)
        def _():
            for copy in out_writes():
                copy.start()

        pair_copy(chunk).wait_send()
        core_copy(chunk, 0).wait_send()
        core_copy(chunk, 1).wait_send()
        for way in range(2):
            for step in range(1, planes):

                @pl.when(sends(way, step))
                def _(way=way, step=step):
                    line_copy(way, step, chunk, me).wait_send()

    def written(chunk):
        for copy in writes(chunk)[0]():
            copy.wait()

    def normalize():
        all_tokens[seq] = tokens_ref[...]
        all_gains[me] = gains_ref[...]
        token_copy.wait_recv()
        for copy in gain_copies:
            copy.wait_recv()
        gain = jnp.concatenate([all_gains[owner, 0:1, :] for owner in range(owners)], axis=1)
        size = 64
        per = own_tokens // size

        def part(index, _):
            span = pl.ds((index % per) * size, size)
            values = all_tokens[index // per, span].astype(f32)
            scale = lax.rsqrt(jnp.mean(values * values, axis=-1, keepdims=True) + norm_eps)
            normed[index // per, span] = (values * scale * gain).astype(bf16)
            return 0

        lax.fori_loop(0, seqs * per, part, 0)
        pltpu.make_async_copy(normed, normed_ref, last_sems.at[0]).start()
        pltpu.make_async_copy(all_gains, all_gains_ref, last_sems.at[1]).start()

    acts = [(first, 0)] + [(functools.partial(line, step=step), step - 1) for step in range(2, planes)]
    acts += [(across, planes - 1), (to_core, planes + 1), (finish, planes + 2)]
    last_lag = acts[-1][1]

    def turn_over(turn, _):
        pl.when(turn == last_lag - 1)(normalize)
        for act, lag in acts:
            inside = jnp.logical_and(turn >= lag, turn - lag < total)
            pl.when(inside)(lambda act=act, lag=lag: act(turn - lag))
        return 0

    lax.fori_loop(0, total + last_lag, turn_over, 0)

    def end(chunk, _):
        written(chunk)
        return 0

    lax.fori_loop(total - RING, total, end, 0)
    for chunk in range(out_count):
        for copy in writes(chunk)[1]():
            copy.wait()
    token_copy.wait_send()
    for copy in gain_copies:
        copy.wait_send()
    pltpu.make_async_copy(normed, normed_ref, last_sems.at[0]).wait()
    pltpu.make_async_copy(all_gains, all_gains_ref, last_sems.at[1]).wait()


def gathered_mixer(tokens, gains, weights):
    own_tokens, width = tokens.shape
    rows = weights[0].shape[0]
    seqs, planes = lax.axis_size("seq"), lax.axis_size("rep")
    owners = lax.axis_size(SR)
    local_width = width // seqs
    total = 5 * local_width // CHUNK
    vmem = pl.BlockSpec(memory_space=pltpu.VMEM)
    anywhere = pl.BlockSpec(memory_space=pl.ANY)
    proj, normed, mix, out, all_gains = pl.pallas_call(
        gather_kernel,
        in_specs=[vmem, vmem] + [anywhere] * 5,
        out_specs=[anywhere] * 5,
        out_shape=[
            jax.ShapeDtypeStruct((seqs * own_tokens, 4 * local_width), f32),
            jax.ShapeDtypeStruct((seqs, own_tokens, width), bf16),
            jax.ShapeDtypeStruct((owners, rows, 4 * local_width), bf16),
            jax.ShapeDtypeStruct((owners, rows, width), bf16),
            jax.ShapeDtypeStruct((owners,) + gains.shape, f32),
        ],
        scratch_shapes=[
            pltpu.VMEM((total, owners, rows, CHUNK), bf16),
            pltpu.VMEM((seqs, own_tokens, width), bf16),
            pltpu.VMEM((seqs, own_tokens, width), bf16),
            pltpu.VMEM((owners,) + gains.shape, f32),
            pltpu.VMEM((RING, seqs * own_tokens, CHUNK), f32),
            pltpu.SemaphoreType.DMA((total,)),
            pltpu.SemaphoreType.DMA((2,)),
            pltpu.SemaphoreType.DMA((2, owners)),
            pltpu.SemaphoreType.DMA((2, planes - 1, RING)),
            pltpu.SemaphoreType.DMA((2, planes - 1, RING)),
            pltpu.SemaphoreType.DMA((2, RING)),
            pltpu.SemaphoreType.DMA((2, 2, RING)),
            pltpu.SemaphoreType.DMA((2, RING)),
            pltpu.SemaphoreType.DMA((3, RING)),
            pltpu.SemaphoreType.DMA((2,)),
        ],
        compiler_params=pltpu.CompilerParams(collective_id=1, has_side_effects=True, vmem_limit_bytes=56 << 20),
        name="gathered_mixer",
    )(tokens, gains, *weights)
    normed = normed.reshape(seqs * own_tokens, width)
    return proj, normed, mix.reshape(width, 4 * local_width), out.reshape(width, width), all_gains


def layout_kernel(owners, part, group_width, reduced_ref, *outs):
    seqs = reduced_ref.shape[0]
    gate_ref, up_ref, out_ref = outs[:3]
    mix_outs = outs[3:]
    local_ff = owners * part
    local_width = out_ref.shape[1] // seqs
    for seq in range(seqs):
        start = 0
        for unit_ref in (gate_ref, up_ref):
            for owner in range(owners):
                place = (owner * seqs + seq) * part
                unit_ref[:, place : place + part] = reduced_ref[seq, :, start : start + part].astype(f32)
                start += part
        out_ref[:, seq * local_width : (seq + 1) * local_width] = reduced_ref[
            seq, :, start : start + local_width
        ].astype(f32)
        start += local_width
        for group in range(local_width // group_width):
            for mix_ref in mix_outs:
                place = seq * local_width + group * group_width
                mix_ref[:, place : place + group_width] = reduced_ref[seq, :, start : start + group_width].astype(f32)
                start += group_width


def laid_out(reduced, down_rows, group_width):
    seqs, share, total = reduced.shape
    owners = lax.axis_size(SR)
    width = share * owners
    steps = 4
    block = share // steps

    def rows_of(columns):
        return pl.BlockSpec((block, columns), lambda i: (i, 0))

    columns = [owners * down_rows] * 2 + [width] * 5
    return pl.pallas_call(
        functools.partial(layout_kernel, owners, down_rows // seqs, group_width),
        grid=(steps,),
        in_specs=[pl.BlockSpec((seqs, block, total), lambda i: (0, i, 0))],
        out_specs=[rows_of(count) for count in columns],
        out_shape=[jax.ShapeDtypeStruct((share, count), f32) for count in columns],
        compiler_params=pltpu.CompilerParams(vmem_limit_bytes=48 << 20),
        name="laid_out",
    )(reduced)


def share_columns(share):
    if lax.axis_size("seq") != 2:
        return lax.all_gather(share, "seq", axis=0)
    return in_order(share[None], swap(share)[None], 0)


def body(
    tokens,
    lengths,
    w_query,
    w_forget,
    w_input,
    w_gate_out,
    w_output,
    w_ffn_gate,
    w_ffn_up,
    w_ffn_down,
    norm_in,
    norm_mid,
    head_gain,
    gate_gap,
    cotangent,
):
    row_count, width = tokens.shape[1:]
    seqs = lax.axis_size("seq")
    owners = lax.axis_size(SR)
    seq_index = lax.axis_index("seq")
    owner_index = lax.axis_index(SR)
    share = w_query.shape[0]
    local_width = width // seqs
    local_heads = H // seqs
    group = min(4, local_heads)
    groups = local_heads // group
    down_rows = w_ffn_down.shape[0]
    part = down_rows // seqs
    local_ff = owners * part

    inputs = tokens[0].astype(f32)
    positions = seq_index * row_count + jnp.arange(row_count)
    valid_col = (positions < lengths[0]).astype(f32)[:, None]

    def gathered(value):
        return lax.all_gather(value, SR, axis=0, tiled=True)

    def owned(value):
        return lax.psum_scatter(value, SR, scatter_dimension=0, tiled=True)

    def my_columns(weight):
        return lax.dynamic_slice_in_dim(weight, seq_index * local_width, local_width, 1)

    def my_units(weight):
        shaped = weight.reshape(share, owners, seqs, part)
        return lax.dynamic_index_in_dim(shaped, seq_index, 2, keepdims=False).reshape(share, local_ff)

    gains = jnp.stack([norm_in, norm_mid, gate_gap, jnp.pad(head_gain, (0, share - head_gain.shape[0]))])
    gains = jnp.pad(gains.astype(f32), ((0, 4), (0, 0)))
    mix_weights = (w_query, w_forget, w_input, w_gate_out)
    fast = seqs == 2 and lax.axis_size("shard") == 4
    if fast:
        proj, normed, w_mix, w_out, gains = gathered_mixer(tokens[0], gains, mix_weights + (w_output,))
    else:
        gains = gathered(gains).reshape(owners, 8, share)
    gain_in = gains[:, 0].reshape(1, width)
    gain_mid = gains[:, 1].reshape(1, width)
    gap_full = gains[:, 2].reshape(1, width)
    gain_head = gains[:, 3, : head_gain.shape[0]].reshape(1, HD)
    gap = lax.dynamic_slice_in_dim(gap_full, seq_index * local_width, local_width, 1)
    scale_in = lax.rsqrt(jnp.mean(inputs * inputs, axis=-1, keepdims=True) + norm_eps)
    unit_in = inputs * scale_in
    if not fast:
        mix_share = jnp.stack([my_columns(w) for w in mix_weights], axis=1)
        mix_share = mix_share.reshape(share, 4, groups, group * HD).transpose(0, 2, 1, 3)
        w_mix = gathered(mix_share.reshape(share, 4 * local_width))
        w_out = gathered(w_output)
        normed = gather_tokens((unit_in * gain_in).astype(bf16))
        proj = matmul(normed, w_mix)

    w_gate_up = gathered(jnp.concatenate([my_units(w_ffn_gate), my_units(w_ffn_up)], axis=1))
    w_down = gathered(lax.dynamic_slice_in_dim(w_ffn_down, seq_index * part, part, 0))

    grad_out = cotangent[0].astype(f32)
    grad_ffn = gather_tokens((valid_col * grad_out).astype(bf16))
    branch_heads, states, mixed = mixer_forward(proj, gap, gain_head, group)
    branch_in = columns_to_tokens(branch_heads)
    hidden = inputs + valid_col * matmul(branch_in, w_out)

    scale_mid = lax.rsqrt(jnp.mean(hidden * hidden, axis=-1, keepdims=True) + norm_eps)
    unit_mid = hidden * scale_mid
    normed_mid = gather_tokens((unit_mid * gain_mid).astype(bf16))
    branch_all = gather_tokens(branch_in)
    normed_mid, branch_all = lax.optimization_barrier((normed_mid, branch_all))
    early_lefts = [value.T for value in (normed_mid, branch_all, normed)]
    gate_up = matmul(normed_mid, w_gate_up)
    gate_up, early_lefts = lax.optimization_barrier((gate_up, early_lefts))
    gate_vals = gate_up[:, :local_ff]
    up_vals = gate_up[:, local_ff:]
    gate_act = jax.nn.silu(gate_vals)
    inner = (gate_act * up_vals).astype(bf16)

    grad_inner = matmul_nt(grad_ffn, w_down)
    down_share = owned(matmul_tn(inner, grad_ffn).astype(bf16))
    grad_gate_vals = (grad_inner * up_vals * dsilu(gate_vals)).astype(bf16)
    grad_up_vals = (grad_inner * gate_act).astype(bf16)
    grad_gate_up = jnp.concatenate([grad_gate_vals, grad_up_vals], axis=1)
    lefts = early_lefts
    if fast:
        mid = matmul_nt(grad_gate_up, w_gate_up)
        own_mid = lax.dynamic_slice_in_dim(mid, seq_index * row_count, row_count, 0)
        other_mid = lax.dynamic_slice_in_dim(mid, (1 - seq_index) * row_count, row_count, 0).astype(bf16)
        middle = (own_mid, other_mid, hidden, cotangent[0], valid_col, gain_mid)
        mixer = (proj, gap, gain_head, states, mixed)
        reduced, small, input_grad, layer_out = reduced_gradients(
            lefts, grad_gate_up, middle, mixer, w_out, w_mix, tokens[0], gain_in, inner, w_down, group
        )
        small, down_share = lax.optimization_barrier((small, down_share))
        head_share = lax.dynamic_slice_in_dim(small[3], owner_index * (HD // owners), HD // owners)
        grad_gate, grad_up, grad_output, *mix_all = laid_out(reduced, down_rows, group * HD)
    else:
        grad_normed_mid = scatter_tokens(matmul_nt(grad_gate_up, w_gate_up))
        grad_gain_mid = jnp.sum(grad_normed_mid * unit_mid, axis=0)
        grad_unit_mid = grad_normed_mid * gain_mid
        grad_hidden = grad_out + scale_mid * (
            grad_unit_mid - unit_mid * jnp.mean(grad_unit_mid * unit_mid, axis=-1, keepdims=True)
        )
        grad_branch = (valid_col * grad_hidden).astype(bf16)
        grad_branch_in = tokens_to_columns(matmul_nt(grad_branch, w_out).astype(bf16))
        small = jnp.zeros((owners, 8, share), f32).at[:, 1].set(grad_gain_mid.reshape(owners, share))
        grad_proj, grad_gap, grad_gain_head = mixer_backward(
            proj, gap, gain_head, states, mixed, grad_branch_in, group
        )
        grad_normed = scatter_tokens(matmul_nt(grad_proj, w_mix))
        grad_unit_in = grad_normed * gain_in
        grad_inputs = grad_hidden + scale_in * (
            grad_unit_in - unit_in * jnp.mean(grad_unit_in * unit_in, axis=-1, keepdims=True)
        )
        input_grad = grad_inputs.astype(bf16)
        layer_out = (hidden + valid_col * scatter_tokens(matmul(inner, w_down))).astype(bf16)
        rights = [grad_gate_up, tokens_to_columns(grad_branch), grad_proj]
        partial = jnp.concatenate([matmul(left, right).astype(bf16) for left, right in zip(lefts, rights)], axis=1)
        reduced = lax.all_gather(owned(partial), "seq", axis=0).astype(f32)
        small = small.at[:, 0].set(jnp.sum(grad_normed * unit_in, axis=0).reshape(owners, share))
        gap_placed = lax.dynamic_update_slice_in_dim(
            jnp.zeros((width,), f32), grad_gap.reshape(local_width), seq_index * local_width, 0
        )
        small = small.at[:, 2].set(gap_placed.reshape(owners, share))
        head_total = jnp.sum(grad_gain_head, axis=(0, 1))
        small = small.at[:, 3, : HD // owners].set(head_total.reshape(owners, -1))
        small = lax.dynamic_index_in_dim(lax.psum(small, ("seq",) + SR), owner_index, 0, keepdims=False)
        head_share = small[3, : HD // owners]
        ends = (2 * local_ff, 2 * local_ff + local_width)
        grad_units = reduced[:, :, : ends[0]].reshape(seqs, share, 2, owners, part).transpose(2, 1, 3, 0, 4)
        grad_gate, grad_up = grad_units.reshape(2, share, owners * down_rows)
        grad_output = reduced[:, :, ends[0] : ends[1]].transpose(1, 0, 2).reshape(share, width)
        mix_all = reduced[:, :, ends[1] :].reshape(seqs, share, groups, 4, group * HD)
        mix_all = mix_all.transpose(3, 1, 0, 2, 4).reshape(4, share, width)
    grad_down = share_columns(down_share).reshape(down_rows, width).astype(f32)

    return (
        layer_out[None],
        input_grad[None],
        mix_all[0],
        mix_all[1],
        mix_all[2],
        mix_all[3],
        grad_output,
        grad_gate,
        grad_up,
        grad_down,
        small[0],
        small[1],
        head_share,
        small[2],
    )


def solution(mesh):
    rows = P(SR, None)
    vector = P(SR)
    by_token = P(SR, "seq", None)
    placed = (by_token, vector) + (rows,) * 8 + (vector,) * 4 + (by_token,)
    return jax.shard_map(
        body,
        mesh=mesh,
        in_specs=placed,
        out_specs=(by_token, by_token) + (rows,) * 8 + (vector,) * 4,
        check_vma=False,
    )
```
